32 devices in a mesh: grp: 4 (over z), sp: 8 (over y, x, core).
Axes of the slice: x: 2, y: 2, z: 4, core: 2. Of those that a mesh axis runs over, the one named last changes fastest.
Arguments:
- query_input: bfloat16 [4096, 4096], P(('grp', 'sp')), may hold values from -6 to 6
- key_input: bfloat16 [4096, 4096], P(('grp', 'sp')), may hold values from -6 to 6
- value_heads_input: bfloat16 [4096, 4096], P(('grp', 'sp')), may hold values from -6 to 6
- conv_weight: float32 [3, 4, 4096], P(None, None, 'sp'), may hold values from -3 to 3
- feature_map: bfloat16 [128, 1024], replicated, may hold values from -0.5 to 0.5
- out_gain: float32 [4096], P('sp'), may hold values from 0.25 to 1.75
Outputs:
- attended: bfloat16 [4096, 4096], P(('grp', 'sp'))
The draws below stay inside these ranges and needn't reach their ends.
All inputs are finite; a program needn't handle non-finite values.
Results may differ from the reference program's by a relative error of at most 0.0052.
Values may be sent and summed in bfloat16 or wider, within the bound.
No kernel may reach another device: no remote copies, remote signals or barrier semaphores. Data moves between devices by JAX's collectives and lax.ppermute only.
A program may use at most 128 MiB of HBM per device.

```python
import jax
import jax.numpy as jnp
from jax import lax

H = 32
DH = 128
M = 1024
CONV = 4
BLOCK = 256
D = 4096
TOKEN_COUNT = 4096


def block_scale(stream_key, extent, shards, smallest, top_value):
    loudness = 1.0
    for position, shards_of in shards:
        steps = jax.random.uniform(jax.random.fold_in(jax.random.fold_in(stream_key, 6), position), (shards_of,), jnp.float32, smallest / len(shards), top_value / len(shards))
        loudness = loudness * jnp.repeat(jnp.exp(steps), extent[position] // shards_of).reshape((-1,) + (1,) * (len(extent) - 1 - position))
    return loudness


def noise(stream_key, extent, width, bound, split=(), held_as=jnp.bfloat16):
    array = width * jax.random.normal(stream_key, extent, jnp.float32)
    if split:
        array = array * block_scale(stream_key, extent, split, -0.22, 0.18)
    return jnp.clip(array, -bound, bound).astype(held_as)


def setup_inputs(seed: int = 0) -> dict:
    key_of = jax.random.split(jax.random.key(seed), 7)
    query_input = noise(key_of[0], (TOKEN_COUNT, D), 1.0, 6.0, ((0, 32),))
    key_input = noise(key_of[1], (TOKEN_COUNT, D), 1.0, 6.0, ((0, 32),))
    value_heads_input = noise(key_of[2], (TOKEN_COUNT, D), 1.0, 6.0, ((0, 32),))
    conv_weight = noise(key_of[3], (3, CONV, D), 0.5, 3.0, ((2, 8),), jnp.float32)
    feature_map = noise(key_of[4], (DH, M), DH ** -0.5, 0.5)
    out_gain = jnp.clip(1.0 + 0.15 * jax.random.normal(key_of[5], (D,), jnp.float32), 0.25, 1.75)
    return {"query_input": query_input, "key_input": key_input, "value_heads_input": value_heads_input, "conv_weight": conv_weight, "feature_map": feature_map, "out_gain": out_gain}


def causal_conv(source, earlier, weights):
    tap_count = weights.shape[0]
    length = source.shape[0]
    padded = jnp.concatenate([earlier.astype(jnp.float32), source.astype(jnp.float32)], 0)
    summed = jnp.zeros(source.shape, jnp.float32)
    for tap_index in range(tap_count):
        row_begin = tap_count - 1 - tap_index
        summed = summed + weights[tap_index] * padded[row_begin:row_begin + length]
    return summed.astype(jnp.bfloat16)

def reference(query_input, key_input, value_heads_input, conv_weight, feature_map, out_gain):

    def by_head(matrix):
        return matrix.reshape(TOKEN_COUNT, H, DH).transpose(1, 0, 2)
    weights_all = conv_weight.reshape(3, CONV, H, DH).transpose(2, 0, 1, 3)
    gain_table = out_gain.reshape(H, DH)
    causal_mask = lax.iota(jnp.int32, BLOCK)[None, :] <= lax.iota(jnp.int32, BLOCK)[:, None]
    block_count = TOKEN_COUNT // BLOCK

    def one_head(inputs):
        query_head, key_head, value_head, weights, gain_head = inputs
        zero_rim = jnp.zeros((CONV - 1, DH), jnp.bfloat16)
        sources = (query_head, key_head, value_head)
        blocked = tuple((causal_conv(sources[member], zero_rim, weights[member]).reshape(block_count, BLOCK, DH) for member in range(3)))

        def block_step(kv_state, block_in):
            query_block, key_block, value_tile_rows = block_in
            query_featurized = jnp.maximum(jnp.dot(query_block, feature_map, preferred_element_type=jnp.float32), 0.0).astype(jnp.bfloat16)
            key_featurized = jnp.maximum(jnp.dot(key_block, feature_map, preferred_element_type=jnp.float32), 0.0).astype(jnp.bfloat16)
            scores = jnp.dot(query_featurized, key_featurized.T, preferred_element_type=jnp.float32)
            scores = jnp.where(causal_mask, scores, 0.0).astype(jnp.bfloat16)
            local_part = jnp.dot(scores, value_tile_rows, preferred_element_type=jnp.float32)
            carried_part = jnp.dot(query_featurized.astype(jnp.float32), kv_state, precision=lax.Precision.HIGHEST)
            numerator = local_part + carried_part
            kv_state = kv_state + jnp.dot(key_featurized.T, value_tile_rows, preferred_element_type=jnp.float32)
            normed = numerator * lax.rsqrt(lax.optimization_barrier(jnp.mean(numerator * numerator, -1, keepdims=True)) + 1e-06) * gain_head
            return (kv_state, normed.astype(jnp.bfloat16))
        _, outputs = lax.scan(block_step, jnp.zeros((M, DH), jnp.float32), blocked)
        return outputs.reshape(TOKEN_COUNT, DH)
    heads_out = lax.map(one_head, (by_head(query_input), by_head(key_input), by_head(value_heads_input), weights_all, gain_table))
    return heads_out.transpose(1, 0, 2).reshape(TOKEN_COUNT, H * DH)
```

```python
import functools

import jax
import jax.numpy as jnp
from jax import lax
from jax.experimental import pallas as pl
from jax.experimental.pallas import tpu as pltpu
from jax.sharding import Mesh
from jax.sharding import PartitionSpec as P

H = 32
DH = 128
BLOCK = 256
TAIL = 8
RIM = 16
GROUP = ("part", "sp")


def dot(a, b):
    return jnp.dot(a, b, preferred_element_type=jnp.float32)


def dot_nt(a, b):
    return lax.dot_general(a, b, (((1,), (1,)), ((), ())), preferred_element_type=jnp.float32)


def stage(rows_ref, halo, first, pad_ref):
    width = rows_ref.shape[-1]
    count = pad_ref.shape[0] - TAIL

    @pl.when(first)
    def _():
        pad_ref[:TAIL] = halo[RIM - TAIL :].astype(jnp.float32)

    @pl.when(jnp.logical_not(first))
    def _():
        pad_ref[:TAIL] = pad_ref[count:]

    pad_ref[TAIL:] = rows_ref[...].reshape(count, width).astype(jnp.float32)


def conv(pad_ref, weights, begin):
    total = jnp.zeros((BLOCK, pad_ref.shape[1]), jnp.float32)
    for tap in range(weights.shape[0]):
        row = TAIL + begin - tap
        total = total + weights[tap][None, :] * pad_ref[row : row + BLOCK]
    return total.astype(jnp.bfloat16)


def relu16(x):
    return jnp.maximum(x, 0.0).astype(jnp.bfloat16)


def totals_kernel(k_ref, v_ref, halo_ref, w_ref, map_t_ref, out_ref, k_pad, v_pad, state):
    step = pl.program_id(0)
    first = step == 0
    heads = state.shape[0]
    stage(k_ref, halo_ref[0], first, k_pad)
    stage(v_ref, halo_ref[1], first, v_pad)

    @pl.when(first)
    def _():
        state[...] = jnp.zeros_like(state)

    for begin in range(0, k_pad.shape[0] - TAIL, BLOCK):
        keys = conv(k_pad, w_ref[1], begin)
        values = conv(v_pad, w_ref[2], begin)
        for h in range(heads):
            cols = slice(h * DH, (h + 1) * DH)
            feats_t = relu16(dot_nt(map_t_ref[...], keys[:, cols]))
            state[h] += dot(feats_t, values[:, cols])

    @pl.when(step == pl.num_programs(0) - 1)
    def _():
        out_ref[...] = state[...].astype(jnp.bfloat16)


def span_kernel(
    q_ref, k_ref, v_ref, qk_halo, kv_halo, w_ref, map_ref, map_t_ref,
    part_ref, feat_ref, q_pad, k_pad, v_pad, state,
):
    first = pl.program_id(0) == 0
    heads = state.shape[0]
    stage(q_ref, qk_halo[0], first, q_pad)
    stage(k_ref, kv_halo[0], first, k_pad)
    stage(v_ref, kv_halo[1], first, v_pad)

    @pl.when(first)
    def _():
        state[...] = jnp.zeros_like(state)

    row = lax.broadcasted_iota(jnp.int32, (BLOCK, BLOCK), 0)
    col = lax.broadcasted_iota(jnp.int32, (BLOCK, BLOCK), 1)
    causal = col <= row
    for begin in range(0, k_pad.shape[0] - TAIL, BLOCK):
        rows = slice(begin, begin + BLOCK)
        queries = conv(q_pad, w_ref[0], begin)
        keys = conv(k_pad, w_ref[1], begin)
        values = conv(v_pad, w_ref[2], begin)
        for h in range(heads):
            cols = slice(h * DH, (h + 1) * DH)
            feats_t = relu16(dot_nt(map_t_ref[...], keys[:, cols]))
            feats = relu16(dot(queries[:, cols], map_ref[...]))
            feat_ref[h, rows] = feats
            scores = jnp.where(causal, dot(feats, feats_t), 0.0).astype(jnp.bfloat16)
            high = state[h].astype(jnp.bfloat16)
            low = (state[h] - high.astype(jnp.float32)).astype(jnp.bfloat16)
            carried = dot(feats, jnp.concatenate([high, low], 1))
            part_ref[rows, cols] = (
                dot(scores, values[:, cols]) + carried[:, :DH] + carried[:, DH:]
            )
            state[h] += dot(feats_t, values[:, cols])


def finish_kernel(part_ref, feat_ref, state_ref, gain_ref, out_ref):
    heads = state_ref.shape[0]
    for h in range(heads):
        cols = slice(h * DH, (h + 1) * DH)
        numerator = part_ref[:, cols] + dot(feat_ref[h], state_ref[h])
        scale = lax.rsqrt(jnp.mean(numerator * numerator, -1, keepdims=True) + 1e-06)
        out_ref[:, cols] = (numerator * scale * gain_ref[:, cols]).astype(jnp.bfloat16)


PARAMS = pltpu.CompilerParams(
    dimension_semantics=("arbitrary",), vmem_limit_bytes=40 * 1024 * 1024
)


def whole(array):
    zeros = (0,) * array.ndim
    return pl.BlockSpec(array.shape, lambda i: zeros)


def step_chunks(count, rows):
    per_block = BLOCK // rows
    return per_block * (2 if count % (2 * per_block) == 0 else 1)


def span_totals(kv, halo, weights, map_t):
    count, _, rows, width = kv.shape
    heads, chunks = width // DH, step_chunks(count, rows)
    features = map_t.shape[0]
    pad = pltpu.VMEM((TAIL + chunks * rows, width), jnp.float32)
    block = (chunks, 1, rows, width)
    shape = (heads, features, DH)
    return pl.pallas_call(
        totals_kernel,
        grid=(count // chunks,),
        in_specs=[
            pl.BlockSpec(block, lambda i: (i, 0, 0, 0)),
            pl.BlockSpec(block, lambda i: (i, 1, 0, 0)),
            whole(halo), whole(weights), whole(map_t),
        ],
        out_specs=pl.BlockSpec(shape, lambda i: (0, 0, 0)),
        out_shape=jax.ShapeDtypeStruct(shape, jnp.bfloat16),
        scratch_shapes=[pad, pad, pltpu.VMEM(shape, jnp.float32)],
        compiler_params=PARAMS,
        cost_estimate=pl.CostEstimate(
            flops=8 * count * rows * width * features, bytes_accessed=8 * count * rows * width,
            transcendentals=0,
        ),
    )(kv, kv, halo, weights, map_t)


def span_parts(queries, kv, q_halo, kv_halo, weights, feature_map, map_t):
    count, rows, width = queries.shape
    heads, chunks = width // DH, step_chunks(count, rows)
    features = map_t.shape[0]
    pad = pltpu.VMEM((TAIL + chunks * rows, width), jnp.float32)
    block = (chunks, 1, rows, width)
    tokens, step = count * rows, chunks * rows
    return pl.pallas_call(
        span_kernel,
        grid=(count // chunks,),
        in_specs=[
            pl.BlockSpec((chunks, rows, width), lambda i: (i, 0, 0)),
            pl.BlockSpec(block, lambda i: (i, 0, 0, 0)),
            pl.BlockSpec(block, lambda i: (i, 1, 0, 0)),
            whole(q_halo), whole(kv_halo), whole(weights), whole(feature_map), whole(map_t),
        ],
        out_specs=[
            pl.BlockSpec((step, width), lambda i: (i, 0)),
            pl.BlockSpec((heads, step, features), lambda i: (0, i, 0)),
        ],
        out_shape=[
            jax.ShapeDtypeStruct((tokens, width), jnp.float32),
            jax.ShapeDtypeStruct((heads, tokens, features), jnp.bfloat16),
        ],
        scratch_shapes=[pad, pad, pad, pltpu.VMEM((heads, features, DH), jnp.float32)],
        compiler_params=PARAMS,
        cost_estimate=pl.CostEstimate(
            flops=20 * tokens * width * features, bytes_accessed=24 * tokens * width,
            transcendentals=0,
        ),
    )(queries, kv, kv, q_halo, kv_halo, weights, feature_map, map_t)


def finished(parts, feats, state, gains):
    tokens, width = parts.shape
    heads, _, features = feats.shape
    step = tokens // 4
    return pl.pallas_call(
        finish_kernel,
        grid=(4,),
        in_specs=[
            pl.BlockSpec((step, width), lambda i: (i, 0)),
            pl.BlockSpec((heads, step, features), lambda i: (0, i, 0)),
            whole(state), whole(gains),
        ],
        out_specs=pl.BlockSpec((step, width), lambda i: (i, 0)),
        out_shape=jax.ShapeDtypeStruct((tokens, width), jnp.bfloat16),
        compiler_params=PARAMS,
        cost_estimate=pl.CostEstimate(
            flops=2 * tokens * width * features, bytes_accessed=24 * tokens * width,
            transcendentals=tokens,
        ),
    )(parts, feats, state, gains)


def next_span(block, spans):
    return lax.ppermute(block, "span", [(i, i + 1) for i in range(spans - 1)])


def local(spans, query_input, key_input, value_heads_input, conv_weight, feature_map, out_gain):
    rows, model = query_input.shape
    parts, members = lax.axis_size("part"), lax.axis_size("sp")
    count = parts * members
    width = model // count

    def by_owner(x):
        x = x.reshape(rows, members, parts, width)
        return x.transpose(2, 1, 0, 3).reshape(count, rows, width)

    kv = jnp.stack([by_owner(key_input), by_owner(value_heads_input)], 1)
    kv = lax.all_to_all(kv, GROUP, split_axis=0, concat_axis=0, tiled=True)
    queries = lax.all_to_all(by_owner(query_input), GROUP, split_axis=0, concat_axis=0, tiled=True)

    column = lax.axis_index("part") * width
    weights = lax.dynamic_slice_in_dim(conv_weight, column, width, 2)
    gains = lax.dynamic_slice_in_dim(out_gain, column, width, 0)[None]
    map_t = feature_map.T

    kv_rim = kv[count - 1, :, rows - RIM :]
    q_rim = queries[count - 1, None, rows - RIM :]
    rims = next_span(jnp.concatenate([kv_rim, q_rim], 0), spans)
    kv_halo, q_halo = rims[:2], rims[2:]

    if spans == 2:
        state = span_totals(kv, jnp.zeros_like(kv_halo), weights, map_t)
        earlier = next_span(state, spans)
    else:
        state = span_totals(kv, kv_halo, weights, map_t)
        gathered = lax.all_gather(state, "span")
        before = jnp.arange(spans) < lax.axis_index("span")
        earlier = jnp.sum(
            jnp.where(before[:, None, None, None], gathered.astype(jnp.float32), 0.0), 0
        ).astype(jnp.bfloat16)

    partial, feats = span_parts(queries, kv, q_halo, kv_halo, weights, feature_map, map_t)
    attended = finished(partial, feats, earlier, gains).reshape(count, rows, width)
    attended = lax.all_to_all(attended, GROUP, split_axis=0, concat_axis=0, tiled=True)
    attended = attended.reshape(parts, members, rows, width)
    return attended.transpose(2, 1, 0, 3).reshape(rows, model)


def solution(mesh):
    groups, members = mesh.devices.shape
    parts = 1
    while groups % (4 * parts) == 0 and H % (2 * parts * members) == 0:
        parts *= 2
    spans = groups // parts
    split = Mesh(mesh.devices.reshape(spans, parts, members), ("span", "part", "sp"))
    tokens = P(("span", "part", "sp"), None)
    placed = (tokens, tokens, tokens, P(None, None, "sp"), P(), P("sp"))
    return jax.shard_map(
        functools.partial(local, spans),
        mesh=split, in_specs=placed, out_specs=tokens, check_vma=False,
    )
```

```python
import functools

import jax
import jax.numpy as jnp
from jax import lax
from jax.experimental import pallas as pl
from jax.experimental.pallas import tpu as pltpu
from jax.sharding import Mesh
from jax.sharding import PartitionSpec as P

H = 32
DH = 128
BLOCK = 256
TAIL = 8
RIM = 16
GROUP = ("part", "sp")


def dot(a, b):
    return jnp.dot(a, b, preferred_element_type=jnp.float32)


def dot_nt(a, b):
    return lax.dot_general(a, b, (((1,), (1,)), ((), ())), preferred_element_type=jnp.float32)


def stage(rows_ref, halo, first, pad_ref):
    width = rows_ref.shape[-1]
    count = pad_ref.shape[0] - TAIL

    @pl.when(first)
    def _():
        pad_ref[:TAIL] = halo[RIM - TAIL :].astype(jnp.float32)

    @pl.when(jnp.logical_not(first))
    def _():
        pad_ref[:TAIL] = pad_ref[count:]

    pad_ref[TAIL:] = rows_ref[...].reshape(count, width).astype(jnp.float32)


def conv(pad_ref, weights, begin):
    total = jnp.zeros((BLOCK, pad_ref.shape[1]), jnp.float32)
    for tap in range(weights.shape[0]):
        row = TAIL + begin - tap
        total = total + weights[tap][None, :] * pad_ref[row : row + BLOCK]
    return total.astype(jnp.bfloat16)


def relu16(x):
    return jnp.maximum(x, 0.0).astype(jnp.bfloat16)


def pack_kernel(starts, q_ref, k_ref, v_ref, out_ref, sems):
    copies = []
    for member, source in enumerate((q_ref, k_ref, v_ref)):
        for owner, start in enumerate(starts):
            copies.append(
                pltpu.make_async_copy(
                    source.at[:, pl.ds(start, DH)], out_ref.at[owner, member], sems.at[len(copies)]
                )
            )
    for copy in copies:
        copy.start()
    for copy in copies:
        copy.wait()


def unpack_kernel(starts, *refs):
    *sources, out_ref, sems = refs
    copies = []
    for head, source in enumerate(sources):
        for owner, start in enumerate(starts[head]):
            copies.append(
                pltpu.make_async_copy(
                    source.at[owner], out_ref.at[:, pl.ds(start, DH)], sems.at[len(copies)]
                )
            )
    for copy in copies:
        copy.start()
    for copy in copies:
        copy.wait()


def totals_kernel(x_ref, halo_ref, w_ref, map_t_ref, out_ref, k_pad, v_pad, state):
    step = pl.program_id(0)
    first = step == 0
    stage(x_ref.at[:, 1], halo_ref[1], first, k_pad)
    stage(x_ref.at[:, 2], halo_ref[2], first, v_pad)

    @pl.when(first)
    def _():
        state[...] = jnp.zeros_like(state)

    for begin in range(0, k_pad.shape[0] - TAIL, BLOCK):
        keys = conv(k_pad, w_ref[1], begin)
        values = conv(v_pad, w_ref[2], begin)
        feats_t = relu16(dot_nt(map_t_ref[...], keys))
        state[...] += dot(feats_t, values)

    @pl.when(step == pl.num_programs(0) - 1)
    def _():
        out_ref[...] = state[...].astype(jnp.bfloat16)


def span_kernel(
    x_ref, halo_ref, w_ref, map_ref, map_t_ref, part_ref, feat_ref, q_pad, k_pad, v_pad, state,
):
    first = pl.program_id(0) == 0
    stage(x_ref.at[:, 0], halo_ref[0], first, q_pad)
    stage(x_ref.at[:, 1], halo_ref[1], first, k_pad)
    stage(x_ref.at[:, 2], halo_ref[2], first, v_pad)

    @pl.when(first)
    def _():
        state[...] = jnp.zeros_like(state)

    row = lax.broadcasted_iota(jnp.int32, (BLOCK, BLOCK), 0)
    col = lax.broadcasted_iota(jnp.int32, (BLOCK, BLOCK), 1)
    causal = col <= row
    for begin in range(0, k_pad.shape[0] - TAIL, BLOCK):
        rows = slice(begin, begin + BLOCK)
        queries = conv(q_pad, w_ref[0], begin)
        keys = conv(k_pad, w_ref[1], begin)
        values = conv(v_pad, w_ref[2], begin)
        feats_t = relu16(dot_nt(map_t_ref[...], keys))
        feats = relu16(dot(queries, map_ref[...]))
        feat_ref[rows] = feats
        scores = jnp.where(causal, dot(feats, feats_t), 0.0).astype(jnp.bfloat16)
        high = state[...].astype(jnp.bfloat16)
        low = (state[...] - high.astype(jnp.float32)).astype(jnp.bfloat16)
        carried = dot(feats, jnp.concatenate([high, low], 1))
        part_ref[rows] = dot(scores, values) + carried[:, :DH] + carried[:, DH:]
        state[...] += dot(feats_t, values)


def finish_kernel(part_ref, feat_ref, state_ref, gain_ref, out_ref):
    numerator = part_ref[...] + dot(feat_ref[...], state_ref[...])
    scale = lax.rsqrt(jnp.mean(numerator * numerator, -1, keepdims=True) + 1e-06)
    out_ref[...] = (numerator * scale * gain_ref[...]).astype(jnp.bfloat16)


PARAMS = pltpu.CompilerParams(
    dimension_semantics=("arbitrary",), vmem_limit_bytes=40 * 1024 * 1024
)
ANY = pl.BlockSpec(memory_space=pl.ANY)


def whole(array):
    zeros = (0,) * array.ndim
    return pl.BlockSpec(array.shape, lambda i: zeros)


def step_chunks(count, rows):
    chunks = BLOCK // rows
    for _ in range(2):
        if count % (2 * chunks) == 0:
            chunks *= 2
    return chunks


def packed(starts, query_input, key_input, value_heads_input):
    rows = query_input.shape[0]
    return pl.pallas_call(
        functools.partial(pack_kernel, starts),
        in_specs=[ANY] * 3,
        out_specs=ANY,
        out_shape=jax.ShapeDtypeStruct((len(starts), 3, rows, DH), jnp.bfloat16),
        scratch_shapes=[pltpu.SemaphoreType.DMA((3 * len(starts),))],
        cost_estimate=pl.CostEstimate(
            flops=0, bytes_accessed=12 * rows * DH * len(starts), transcendentals=0
        ),
    )(query_input, key_input, value_heads_input)


def unpacked(starts, outputs):
    owners, rows, _ = outputs[0].shape
    pieces = owners * len(outputs)
    return pl.pallas_call(
        functools.partial(unpack_kernel, starts),
        in_specs=[ANY] * len(outputs),
        out_specs=ANY,
        out_shape=jax.ShapeDtypeStruct((rows, pieces * DH), jnp.bfloat16),
        scratch_shapes=[pltpu.SemaphoreType.DMA((pieces,))],
        cost_estimate=pl.CostEstimate(
            flops=0, bytes_accessed=4 * rows * DH * pieces, transcendentals=0
        ),
    )(*outputs)


def span_total(x, halo, weights, map_t):
    count, _, rows, _ = x.shape
    chunks = step_chunks(count, rows)
    features = map_t.shape[0]
    pad = pltpu.VMEM((TAIL + chunks * rows, DH), jnp.float32)
    shape = (features, DH)
    return pl.pallas_call(
        totals_kernel,
        grid=(count // chunks,),
        in_specs=[
            pl.BlockSpec((chunks, 3, rows, DH), lambda i: (i, 0, 0, 0)),
            whole(halo), whole(weights), whole(map_t),
        ],
        out_specs=pl.BlockSpec(shape, lambda i: (0, 0)),
        out_shape=jax.ShapeDtypeStruct(shape, jnp.bfloat16),
        scratch_shapes=[pad, pad, pltpu.VMEM(shape, jnp.float32)],
        compiler_params=PARAMS,
        cost_estimate=pl.CostEstimate(
            flops=8 * count * rows * DH * features, bytes_accessed=8 * count * rows * DH,
            transcendentals=0,
        ),
    )(x, halo, weights, map_t)


def span_part(x, halo, weights, feature_map, map_t):
    count, _, rows, _ = x.shape
    chunks = step_chunks(count, rows)
    features = map_t.shape[0]
    pad = pltpu.VMEM((TAIL + chunks * rows, DH), jnp.float32)
    tokens, step = count * rows, chunks * rows
    return pl.pallas_call(
        span_kernel,
        grid=(count // chunks,),
        in_specs=[
            pl.BlockSpec((chunks, 3, rows, DH), lambda i: (i, 0, 0, 0)),
            whole(halo), whole(weights), whole(feature_map), whole(map_t),
        ],
        out_specs=[
            pl.BlockSpec((step, DH), lambda i: (i, 0)),
            pl.BlockSpec((step, features), lambda i: (i, 0)),
        ],
        out_shape=[
            jax.ShapeDtypeStruct((tokens, DH), jnp.float32),
            jax.ShapeDtypeStruct((tokens, features), jnp.bfloat16),
        ],
        scratch_shapes=[pad, pad, pad, pltpu.VMEM((features, DH), jnp.float32)],
        compiler_params=PARAMS,
        cost_estimate=pl.CostEstimate(
            flops=20 * tokens * DH * features, bytes_accessed=24 * tokens * DH,
            transcendentals=0,
        ),
    )(x, halo, weights, feature_map, map_t)


def finished(parts, feats, state, gains):
    tokens, features = feats.shape
    step = tokens // 4
    return pl.pallas_call(
        finish_kernel,
        grid=(4,),
        in_specs=[
            pl.BlockSpec((step, DH), lambda i: (i, 0)),
            pl.BlockSpec((step, features), lambda i: (i, 0)),
            whole(state), whole(gains),
        ],
        out_specs=pl.BlockSpec((step, DH), lambda i: (i, 0)),
        out_shape=jax.ShapeDtypeStruct((tokens, DH), jnp.bfloat16),
        compiler_params=PARAMS,
        cost_estimate=pl.CostEstimate(
            flops=2 * tokens * DH * features, bytes_accessed=24 * tokens * DH,
            transcendentals=tokens,
        ),
    )(parts, feats, state, gains)


def next_span(block, spans):
    return lax.ppermute(block, "span", [(i, i + 1) for i in range(spans - 1)])


def exchange(block):
    return lax.all_to_all(block, GROUP, split_axis=0, concat_axis=0, tiled=True)


def local(spans, query_input, key_input, value_heads_input, conv_weight, feature_map, out_gain):
    rows, model = query_input.shape
    parts, members = lax.axis_size("part"), lax.axis_size("sp")
    count = parts * members
    width = model // count
    heads = width // DH
    starts = [
        [(member * parts + part) * width + head * DH for part in range(parts) for member in range(members)]
        for head in range(heads)
    ]
    column = lax.axis_index("part") * width
    weights = lax.dynamic_slice_in_dim(conv_weight, column, width, 2)
    gains = lax.dynamic_slice_in_dim(out_gain, column, width, 0)[None]
    map_t = feature_map.T

    outputs = []
    for head in range(heads):
        cols = slice(head * DH, (head + 1) * DH)
        taps = weights[:, :, cols]
        x = exchange(packed(starts[head], query_input, key_input, value_heads_input))
        halo = next_span(x[count - 1, :, rows - RIM :], spans)
        if spans == 2:
            state = next_span(span_total(x, jnp.zeros_like(halo), taps, map_t), spans)
        else:
            total = span_total(x, halo, taps, map_t)
            gathered = lax.all_gather(total, "span").astype(jnp.float32)
            before = jnp.arange(spans) < lax.axis_index("span")
            state = jnp.sum(jnp.where(before[:, None, None], gathered, 0.0), 0)
            state = state.astype(jnp.bfloat16)
        partial, feats = span_part(x, halo, taps, feature_map, map_t)
        attended = finished(partial, feats, state, gains[:, cols])
        outputs.append(exchange(attended.reshape(count, rows, DH)))
    return unpacked(starts, outputs)


def solution(mesh):
    groups, members = mesh.devices.shape
    parts = 1
    while groups % (4 * parts) == 0 and H % (2 * parts * members) == 0:
        parts *= 2
    spans = groups // parts
    split = Mesh(mesh.devices.reshape(spans, parts, members), ("span", "part", "sp"))
    tokens = P(("span", "part", "sp"), None)
    placed = (tokens, tokens, tokens, P(None, None, "sp"), P(), P("sp"))
    return jax.shard_map(
        functools.partial(local, spans),
        mesh=split, in_specs=placed, out_specs=tokens, check_vma=False,
    )
```

```python
import functools

import jax
import jax.numpy as jnp
from jax import lax
from jax.experimental import pallas as pl
from jax.experimental.pallas import tpu as pltpu
from jax.sharding import Mesh
from jax.sharding import PartitionSpec as P

H = 32
DH = 128
BLOCK = 256
TAIL = 8
RIM = 16
GROUP = ("part", "sp")


def dot(a, b):
    return jnp.dot(a, b, preferred_element_type=jnp.float32)


def dot_nt(a, b):
    return lax.dot_general(a, b, (((1,), (1,)), ((), ())), preferred_element_type=jnp.float32)


def stage(rows, halo_ref, first, pad_ref):
    count = pad_ref.shape[0] - TAIL

    @pl.when(first)
    def _():
        pad_ref[:TAIL] = halo_ref[RIM - TAIL :].astype(jnp.float32)

    @pl.when(jnp.logical_not(first))
    def _():
        pad_ref[:TAIL] = pad_ref[count:]

    pad_ref[TAIL:] = rows.reshape(count, rows.shape[-1]).astype(jnp.float32)


def conv(pad_ref, weights, begin):
    total = jnp.zeros((BLOCK, pad_ref.shape[1]), jnp.float32)
    for tap in range(weights.shape[0]):
        row = TAIL + begin - tap
        total = total + weights[tap][None, :] * pad_ref[row : row + BLOCK]
    return total.astype(jnp.bfloat16)


def relu16(x):
    return jnp.maximum(x, 0.0).astype(jnp.bfloat16)


def channel_start(owner, parts, width):
    members = lax.axis_size("sp")
    return ((owner % members) * parts + owner // members) * width


def group_index():
    return lax.axis_index("part") * lax.axis_size("sp") + lax.axis_index("sp")


def split_kernel(parts, q_ref, k_ref, v_ref, *out_refs):
    me = group_index()
    rows, width = q_ref.shape[0], out_refs[0].shape[-1]
    for step, out_ref in enumerate(out_refs):
        start = pl.multiple_of(channel_start(me ^ step, parts, width), DH)
        cols = pl.ds(start, width)
        out_ref[:rows] = k_ref[:, cols]
        out_ref[rows : 2 * rows] = v_ref[:, cols]
        out_ref[2 * rows :] = q_ref[rows - RIM :, cols]


def pack_kernel(starts, x_ref, out_ref):
    width = out_ref.shape[-1]
    for owner, start in enumerate(starts):
        out_ref[owner] = x_ref[:, start : start + width]


def unpack_kernel(starts, x_ref, out_ref):
    width = x_ref.shape[-1]
    for owner, start in enumerate(starts):
        out_ref[:, start : start + width] = x_ref[owner]


def totals_kernel(*refs):
    *chunk_refs, halo_ref, w_ref, map_t_ref, total_ref, kv_ref, rim_ref, k_pad, v_pad, state = refs
    me = group_index()
    count, _, rows, _ = kv_ref.shape
    heads = state.shape[0]
    for step, chunk_ref in enumerate(chunk_refs):
        source = me ^ step
        kv_ref[source, 0] = chunk_ref[:rows]
        kv_ref[source, 1] = chunk_ref[rows : 2 * rows]

        @pl.when(source == count - 1)
        def _(chunk_ref=chunk_ref):
            rim_ref[0] = chunk_ref[2 * rows :]
            rim_ref[1] = chunk_ref[rows - RIM : rows]
            rim_ref[2] = chunk_ref[2 * rows - RIM : 2 * rows]

    state[...] = jnp.zeros_like(state)
    size = k_pad.shape[0] - TAIL
    chunks = size // rows

    def one(i, carry):
        held = pl.ds(i * chunks, chunks)
        stage(kv_ref[held, 0], halo_ref.at[1], i == 0, k_pad)
        stage(kv_ref[held, 1], halo_ref.at[2], i == 0, v_pad)
        for begin in range(0, size, BLOCK):
            keys = conv(k_pad, w_ref[1], begin)
            values = conv(v_pad, w_ref[2], begin)
            for h in range(heads):
                cols = slice(h * DH, (h + 1) * DH)
                feats_t = relu16(dot_nt(map_t_ref[...], keys[:, cols]))
                state[h] += dot(feats_t, values[:, cols])
        return carry

    lax.fori_loop(0, count // chunks, one, 0)
    total_ref[...] = state[...].astype(jnp.bfloat16)


def span_kernel(
    q_ref, k_ref, v_ref, halo_ref, w_ref, map_ref, map_t_ref,
    part_ref, feat_ref, q_pad, k_pad, v_pad, state,
):
    first = pl.program_id(0) == 0
    heads = state.shape[0]
    stage(q_ref[...], halo_ref.at[0], first, q_pad)
    stage(k_ref[...], halo_ref.at[1], first, k_pad)
    stage(v_ref[...], halo_ref.at[2], first, v_pad)

    @pl.when(first)
    def _():
        state[...] = jnp.zeros_like(state)

    row = lax.broadcasted_iota(jnp.int32, (BLOCK, BLOCK), 0)
    col = lax.broadcasted_iota(jnp.int32, (BLOCK, BLOCK), 1)
    causal = col <= row
    for begin in range(0, k_pad.shape[0] - TAIL, BLOCK):
        rows = slice(begin, begin + BLOCK)
        queries = conv(q_pad, w_ref[0], begin)
        keys = conv(k_pad, w_ref[1], begin)
        values = conv(v_pad, w_ref[2], begin)
        for h in range(heads):
            cols = slice(h * DH, (h + 1) * DH)
            feats_t = relu16(dot_nt(map_t_ref[...], keys[:, cols]))
            feats = relu16(dot(queries[:, cols], map_ref[...]))
            feat_ref[h, rows] = feats
            scores = jnp.where(causal, dot(feats, feats_t), 0.0).astype(jnp.bfloat16)
            high = state[h].astype(jnp.bfloat16)
            low = (state[h] - high.astype(jnp.float32)).astype(jnp.bfloat16)
            carried = dot(feats, jnp.concatenate([high, low], 1))
            part_ref[rows, cols] = (
                dot(scores, values[:, cols]) + carried[:, :DH] + carried[:, DH:]
            )
            state[h] += dot(feats_t, values[:, cols])


def finish_kernel(part_ref, feat_ref, state_ref, gain_ref, out_ref):
    heads = state_ref.shape[0]
    for h in range(heads):
        cols = slice(h * DH, (h + 1) * DH)
        numerator = part_ref[:, cols] + dot(feat_ref[h], state_ref[h])
        scale = lax.rsqrt(jnp.mean(numerator * numerator, -1, keepdims=True) + 1e-06)
        out_ref[:, cols] = (numerator * scale * gain_ref[:, cols]).astype(jnp.bfloat16)


LIMIT = 40 * 1024 * 1024
PARAMS = pltpu.CompilerParams(dimension_semantics=("arbitrary",), vmem_limit_bytes=LIMIT)
VMEM = pl.BlockSpec(memory_space=pltpu.VMEM)


def whole(array):
    zeros = (0,) * array.ndim
    return pl.BlockSpec(array.shape, lambda i: zeros)


def step_chunks(count, rows):
    per_block = BLOCK // rows
    return per_block * (2 if count % (2 * per_block) == 0 else 1)


def whole_call(kernel, inputs, outputs, scratch=(), flops=0):
    moved = sum(x.size * x.dtype.itemsize for x in [*inputs, *outputs])
    return pl.pallas_call(
        kernel,
        in_specs=[VMEM] * len(inputs),
        out_specs=[VMEM] * len(outputs),
        out_shape=outputs,
        scratch_shapes=scratch,
        compiler_params=pltpu.CompilerParams(vmem_limit_bytes=LIMIT),
        cost_estimate=pl.CostEstimate(flops=flops, bytes_accessed=moved, transcendentals=0),
    )(*inputs)


def shaped(shape, dtype=jnp.bfloat16):
    return jax.ShapeDtypeStruct(shape, dtype)


def span_totals(chunks, halo, weights, map_t, rows):
    count, width = len(chunks), chunks[0].shape[-1]
    heads, size = width // DH, step_chunks(count, rows) * rows
    features = map_t.shape[0]
    pad = pltpu.VMEM((TAIL + size, width), jnp.float32)
    shape = (heads, features, DH)
    return whole_call(
        totals_kernel,
        [*chunks, halo, weights, map_t],
        [shaped(shape), shaped((count, 2, rows, width)), shaped((3, RIM, width))],
        [pad, pad, pltpu.VMEM(shape, jnp.float32)],
        8 * count * rows * width * features,
    )


def span_parts(queries, kv, halo, weights, feature_map, map_t):
    count, rows, width = queries.shape
    heads, chunks = width // DH, step_chunks(count, rows)
    features = map_t.shape[0]
    pad = pltpu.VMEM((TAIL + chunks * rows, width), jnp.float32)
    block = (chunks, 1, rows, width)
    tokens, step = count * rows, chunks * rows
    return pl.pallas_call(
        span_kernel,
        grid=(count // chunks,),
        in_specs=[
            pl.BlockSpec((chunks, rows, width), lambda i: (i, 0, 0)),
            pl.BlockSpec(block, lambda i: (i, 0, 0, 0)),
            pl.BlockSpec(block, lambda i: (i, 1, 0, 0)),
            whole(halo), whole(weights), whole(feature_map), whole(map_t),
        ],
        out_specs=[
            pl.BlockSpec((step, width), lambda i: (i, 0)),
            pl.BlockSpec((heads, step, features), lambda i: (0, i, 0)),
        ],
        out_shape=[
            jax.ShapeDtypeStruct((tokens, width), jnp.float32),
            jax.ShapeDtypeStruct((heads, tokens, features), jnp.bfloat16),
        ],
        scratch_shapes=[pad, pad, pad, pltpu.VMEM((heads, features, DH), jnp.float32)],
        compiler_params=PARAMS,
        cost_estimate=pl.CostEstimate(
            flops=20 * tokens * width * features, bytes_accessed=24 * tokens * width,
            transcendentals=0,
        ),
    )(queries, kv, kv, halo, weights, feature_map, map_t)


def finished(parts, feats, state, gains):
    tokens, width = parts.shape
    heads, _, features = feats.shape
    step = tokens // 4
    return pl.pallas_call(
        finish_kernel,
        grid=(4,),
        in_specs=[
            pl.BlockSpec((step, width), lambda i: (i, 0)),
            pl.BlockSpec((heads, step, features), lambda i: (0, i, 0)),
            whole(state), whole(gains),
        ],
        out_specs=pl.BlockSpec((step, width), lambda i: (i, 0)),
        out_shape=jax.ShapeDtypeStruct((tokens, width), jnp.bfloat16),
        compiler_params=PARAMS,
        cost_estimate=pl.CostEstimate(
            flops=2 * tokens * width * features, bytes_accessed=24 * tokens * width,
            transcendentals=tokens,
        ),
    )(parts, feats, state, gains)


def next_span(block, spans):
    return lax.ppermute(block, "span", [(i, i + 1) for i in range(spans - 1)])


def local(spans, query_input, key_input, value_heads_input, conv_weight, feature_map, out_gain):
    rows, model = query_input.shape
    parts, members = lax.axis_size("part"), lax.axis_size("sp")
    count = parts * members
    width = model // count
    starts = [((d % members) * parts + d // members) * width for d in range(count)]

    chunks = whole_call(
        functools.partial(split_kernel, parts),
        [query_input, key_input, value_heads_input],
        [shaped((2 * rows + RIM, width))] * count,
    )
    chunks = [
        lax.ppermute(chunk, GROUP, [(d, d ^ step) for d in range(count)]) if step else chunk
        for step, chunk in enumerate(chunks)
    ]
    (queries,) = whole_call(
        functools.partial(pack_kernel, starts), [query_input], [shaped((count, rows, width))]
    )
    queries, *chunks = lax.optimization_barrier((queries, *chunks))
    queries = lax.all_to_all(queries, GROUP, split_axis=0, concat_axis=0, tiled=True)

    column = lax.axis_index("part") * width
    weights = lax.dynamic_slice_in_dim(conv_weight, column, width, 2)
    gains = lax.dynamic_slice_in_dim(out_gain, column, width, 0)[None]
    map_t = feature_map.T

    if spans == 2:
        nothing = jnp.zeros((3, RIM, width), jnp.bfloat16)
        state, kv, rim = span_totals(chunks, nothing, weights, map_t, rows)
        halo = next_span(rim, spans)
        earlier = next_span(state, spans)
    else:
        last = [jnp.where(group_index() ^ step == count - 1, c, 0) for step, c in enumerate(chunks)]
        last = functools.reduce(jnp.add, last)
        rim = jnp.stack([last[2 * rows :], last[rows - RIM : rows], last[2 * rows - RIM : 2 * rows]])
        halo = next_span(rim, spans)
        state, kv, _ = span_totals(chunks, halo, weights, map_t, rows)
        gathered = lax.all_gather(state, "span").astype(jnp.float32)
        before = jnp.arange(spans) < lax.axis_index("span")
        earlier = jnp.sum(jnp.where(before[:, None, None, None], gathered, 0.0), 0)
        earlier = earlier.astype(jnp.bfloat16)

    partial, feats = span_parts(queries, kv, halo, weights, feature_map, map_t)
    attended = finished(partial, feats, earlier, gains).reshape(count, rows, width)
    attended = lax.all_to_all(attended, GROUP, split_axis=0, concat_axis=0, tiled=True)
    (attended,) = whole_call(
        functools.partial(unpack_kernel, starts), [attended], [shaped((rows, model))]
    )
    return attended


def solution(mesh):
    groups, members = mesh.devices.shape
    parts = 1
    while groups % (4 * parts) == 0 and H % (2 * parts * members) == 0:
        parts *= 2
    spans = groups // parts
    split = Mesh(mesh.devices.reshape(spans, parts, members), ("span", "part", "sp"))
    tokens = P(("span", "part", "sp"), None)
    placed = (tokens, tokens, tokens, P(None, None, "sp"), P(), P("sp"))
    return jax.shard_map(
        functools.partial(local, spans),
        mesh=split, in_specs=placed, out_specs=tokens, check_vma=False,
    )
```

```python
import functools

import jax
import jax.numpy as jnp
from jax import lax
from jax.experimental import pallas as pl
from jax.experimental.pallas import tpu as pltpu
from jax.sharding import Mesh
from jax.sharding import PartitionSpec as P

H = 32
DH = 128
BLOCK = 256
TAIL = 8
RIM = 16
GROUP = ("part", "sp")


def dot(a, b):
    return jnp.dot(a, b, preferred_element_type=jnp.float32)


def dot_nt(a, b):
    return lax.dot_general(a, b, (((1,), (1,)), ((), ())), preferred_element_type=jnp.float32)


def conv(pad_ref, weights, begin):
    total = jnp.zeros((BLOCK, pad_ref.shape[1]), jnp.float32)
    for tap in range(weights.shape[0]):
        row = TAIL + begin - tap
        total = total + weights[tap][None, :] * pad_ref[row : row + BLOCK]
    return total.astype(jnp.bfloat16)


def relu16(x):
    return jnp.maximum(x, 0.0).astype(jnp.bfloat16)


def pack_kernel(width, q_ref, k_ref, v_ref, out_ref):
    parts, members, _, _ = out_ref.shape
    rows = k_ref.shape[0]
    for member in range(members):
        for part in range(parts):
            start = (member * parts + part) * width
            cols = slice(start, start + width)
            out_ref[part, member, :rows] = k_ref[:, cols]
            out_ref[part, member, rows : 2 * rows] = v_ref[:, cols]
            out_ref[part, member, 2 * rows :] = q_ref[:, cols]


def pack_one_kernel(width, x_ref, out_ref):
    parts, members, _, _ = out_ref.shape
    for member in range(members):
        for part in range(parts):
            start = (member * parts + part) * width
            out_ref[part, member] = x_ref[:, start : start + width]


def unpack_kernel(starts, *refs):
    *sources, out_ref = refs
    for head, source in enumerate(sources):
        for owner, start in enumerate(starts):
            begin = start + head * DH
            out_ref[:, begin : begin + DH] = source[owner]


def high_low(x):
    high = x.astype(jnp.bfloat16)
    return jnp.concatenate([high, (x - high.astype(jnp.float32)).astype(jnp.bfloat16)], 1)


def folded(x):
    return x[:, :DH] + x[:, DH:]


def over_pairs(blocks, one):
    size = 2 if blocks % 2 == 0 else 1
    one(0, range(size))

    def later(i, carry):
        one(i, [i * size + j for j in range(size)])
        return carry

    lax.fori_loop(1, blocks // size, later, 0)


def totals_kernel(
    cols, kv_ref, halo_ref, w_ref, map_t_ref,
    total_ref, feats_t_ref, prefix_ref, value_ref, k_pad, v_pad,
):
    blocks = feats_t_ref.shape[0]
    size = k_pad.shape[0] - TAIL
    rows = (kv_ref.shape[1] - RIM) // 2
    chunks = size // rows

    def one(i, members):
        held = pl.ds(i * chunks, chunks)
        if isinstance(i, int):
            k_pad[:TAIL] = halo_ref[1, RIM - TAIL :, cols].astype(jnp.float32)
            v_pad[:TAIL] = halo_ref[2, RIM - TAIL :, cols].astype(jnp.float32)
        else:
            k_pad[:TAIL] = k_pad[size:]
            v_pad[:TAIL] = v_pad[size:]
        k_pad[TAIL:] = kv_ref[held, :rows, cols].reshape(size, DH).astype(jnp.float32)
        v_pad[TAIL:] = kv_ref[held, rows : 2 * rows, cols].reshape(size, DH).astype(jnp.float32)
        for j, block in enumerate(members):
            keys = conv(k_pad, w_ref[1, :, cols], j * BLOCK)
            values = conv(v_pad, w_ref[2, :, cols], j * BLOCK)
            value_ref[block] = values
            feats_t = relu16(dot_nt(map_t_ref[...], keys))
            feats_t_ref[block] = feats_t
            update = dot(feats_t, values)
            if isinstance(block, int) and block == 0:
                prefix_ref[0] = update
                prefix_ref[1] = jnp.zeros_like(update)
            else:
                prefix_ref[block + 1] = prefix_ref[block] + update

    over_pairs(blocks, one)
    total_ref[...] = (prefix_ref[blocks] + prefix_ref[0]).astype(jnp.bfloat16)


def queries_kernel(
    cols, q_ref, kv_ref, halo_ref, w_ref, map_ref, map_t_ref, feats_t_ref, prefix_ref, value_ref,
    part_ref, feat_ref, update_ref, q_pad, k_pad, v_pad,
):
    blocks = feats_t_ref.shape[0]
    size = q_pad.shape[0] - TAIL
    rows = q_ref.shape[1]
    chunks = size // rows
    row = lax.broadcasted_iota(jnp.int32, (BLOCK, BLOCK), 0)
    col = lax.broadcasted_iota(jnp.int32, (BLOCK, BLOCK), 1)
    causal = col <= row

    def one(i, members):
        if isinstance(i, int):
            q_pad[:TAIL] = halo_ref[0, RIM - TAIL :, cols].astype(jnp.float32)
        else:
            q_pad[:TAIL] = q_pad[size:]
        held = q_ref[pl.ds(i * chunks, chunks), :, cols]
        q_pad[TAIL:] = held.reshape(size, DH).astype(jnp.float32)
        for j, block in enumerate(members):
            feats = relu16(dot(conv(q_pad, w_ref[0, :, cols], j * BLOCK), map_ref[...]))
            feat_ref[block] = feats
            if isinstance(block, int) and block == 0:
                k_pad[:TAIL] = halo_ref[1, RIM - TAIL :, cols].astype(jnp.float32)
                v_pad[:TAIL] = halo_ref[2, RIM - TAIL :, cols].astype(jnp.float32)
                first = kv_ref[: BLOCK // rows]
                k_pad[TAIL:] = first[:, :rows, cols].reshape(BLOCK, DH).astype(jnp.float32)
                v_pad[TAIL:] = first[:, rows : 2 * rows, cols].reshape(BLOCK, DH).astype(jnp.float32)
                keys = conv(k_pad, w_ref[1, :, cols], 0)
                values = conv(v_pad, w_ref[2, :, cols], 0)
                feats_t = relu16(dot_nt(map_t_ref[...], keys))
                update_ref[...] = dot(feats_t, values)
            else:
                feats_t, values = feats_t_ref[block], value_ref[block]
            scores = jnp.where(causal, dot(feats, feats_t), 0.0).astype(jnp.bfloat16)
            part = dot(scores, values)
            if not isinstance(block, int) or block > 1:
                part = part + folded(dot(feats, high_low(prefix_ref[block])))
            part_ref[block] = part

    over_pairs(blocks, one)


def finish_kernel(cols, part_ref, feat_ref, state_ref, update_ref, gain_ref, out_ref):
    blocks, _, features = feat_ref.shape
    per_block = BLOCK // out_ref.shape[1]
    state = state_ref[...]
    later = high_low(state.astype(jnp.float32) + update_ref[...])
    gain = gain_ref[:, cols]

    def put(begin, end, carried):
        numerator = part_ref[begin:end].reshape((end - begin) * BLOCK, DH) + carried
        scale = lax.rsqrt(jnp.mean(numerator * numerator, -1, keepdims=True) + 1e-06)
        done = (numerator * scale * gain).astype(jnp.bfloat16)
        held = slice(begin * per_block, end * per_block)
        out_ref[held] = done.reshape((end - begin) * per_block, BLOCK // per_block, DH)

    put(0, 1, dot(feat_ref[0], state))
    for begin in range(1, blocks, 2):
        end = min(begin + 2, blocks)
        feats = feat_ref[begin:end].reshape((end - begin) * BLOCK, features)
        put(begin, end, folded(dot(feats, later)))


LIMIT = 24 * 1024 * 1024
VMEM = pl.BlockSpec(memory_space=pltpu.VMEM)


def whole_call(kernel, inputs, outputs, scratch=(), flops=0):
    moved = sum(x.size * x.dtype.itemsize for x in [*inputs, *outputs])
    return pl.pallas_call(
        kernel,
        in_specs=[VMEM] * len(inputs),
        out_specs=[VMEM] * len(outputs),
        out_shape=outputs,
        scratch_shapes=scratch,
        compiler_params=pltpu.CompilerParams(vmem_limit_bytes=LIMIT),
        cost_estimate=pl.CostEstimate(flops=flops, bytes_accessed=moved, transcendentals=0),
    )(*inputs)


def shaped(shape, dtype=jnp.bfloat16):
    return jax.ShapeDtypeStruct(shape, dtype)


def packed(kernel, inputs, input_rows, parts, members, width, rows):
    held = max(1, members // 4)

    def spec(count, last):
        return pl.BlockSpec((count, held * parts * width), lambda i: (last, i))

    specs = [spec(count, inputs[0].shape[0] // count - 1) for count in input_rows]
    shape = (parts, members, rows, width)
    return pl.pallas_call(
        functools.partial(kernel, width),
        grid=(members // held,),
        in_specs=specs,
        out_specs=pl.BlockSpec((parts, held, rows, width), lambda i: (0, i, 0, 0)),
        out_shape=shaped(shape),
        compiler_params=pltpu.CompilerParams(
            dimension_semantics=("arbitrary",), vmem_limit_bytes=LIMIT
        ),
    )(*inputs).reshape(parts * members, rows, width)


def next_span(block, spans):
    return lax.ppermute(block, "span", [(i, i + 1) for i in range(spans - 1)])


def exchange(block):
    return lax.all_to_all(block, GROUP, split_axis=0, concat_axis=0, tiled=True)


def after(value, other):
    return lax.optimization_barrier((value, other))[0]


def local(spans, query_input, key_input, value_heads_input, conv_weight, feature_map, out_gain):
    rows, model = query_input.shape
    parts, members = lax.axis_size("part"), lax.axis_size("sp")
    count = parts * members
    width = model // count
    heads, tokens, features = width // DH, count * rows, feature_map.shape[1]
    blocks = tokens // BLOCK
    starts = [((d % members) * parts + d // members) * width for d in range(count)]
    sizes = (parts, members, width)

    column = lax.axis_index("part") * width
    weights = lax.dynamic_slice_in_dim(conv_weight, column, width, 2)
    gains = lax.dynamic_slice_in_dim(out_gain, column, width, 0)[None]
    map_t = feature_map.T

    inputs = [query_input, key_input, value_heads_input]
    kv = exchange(packed(pack_kernel, inputs, [RIM, rows, rows], *sizes, 2 * rows + RIM))
    queries = packed(pack_one_kernel, [query_input], [rows], *sizes, rows)
    queries = exchange(after(queries, kv))
    last = kv[count - 1]
    rim = jnp.stack([last[2 * rows :], last[rows - RIM : rows], last[2 * rows - RIM : 2 * rows]])
    halo = next_span(rim, spans)
    before = jnp.zeros_like(halo) if spans == 2 else halo

    pair = BLOCK * (2 if blocks % 2 == 0 else 1)
    wide = pltpu.VMEM((TAIL + pair, DH), jnp.float32)
    narrow = pltpu.VMEM((TAIL + BLOCK, DH), jnp.float32)
    keyed, states = [], []
    for head in range(heads):
        cols = slice(head * DH, (head + 1) * DH)
        total, *kept = whole_call(
            functools.partial(totals_kernel, cols),
            [kv, before, weights, map_t],
            [
                shaped((features, DH)),
                shaped((blocks, features, BLOCK)),
                shaped((blocks + 1, features, DH), jnp.float32),
                shaped((blocks, BLOCK, DH)),
            ],
            [wide, wide],
            8 * tokens * DH * features,
        )
        keyed.append(kept)
        if spans == 2:
            states.append(next_span(total, spans))
        else:
            gathered = lax.all_gather(total, "span").astype(jnp.float32)
            mine = lax.axis_index("span")
            earlier = jnp.where((jnp.arange(spans) < mine)[:, None, None], gathered, 0.0)
            states.append(jnp.sum(earlier, 0).astype(jnp.bfloat16))

    outputs, previous = [], total
    for head in range(heads):
        cols = slice(head * DH, (head + 1) * DH)
        partial, feats, update = whole_call(
            functools.partial(queries_kernel, cols),
            [after(queries, previous), kv, halo, weights, feature_map, map_t, *keyed[head]],
            [
                shaped((blocks, BLOCK, DH), jnp.float32),
                shaped((blocks, BLOCK, features)),
                shaped((features, DH), jnp.float32),
            ],
            [wide, narrow, narrow],
            12 * tokens * DH * features,
        )
        (attended,) = whole_call(
            functools.partial(finish_kernel, cols),
            [partial, feats, states[head], update, gains],
            [shaped((count, rows, DH))],
            (),
            4 * tokens * DH * features,
        )
        previous = attended
        outputs.append(exchange(attended))
    (attended,) = whole_call(
        functools.partial(unpack_kernel, starts), outputs, [shaped((rows, model))]
    )
    return attended


def solution(mesh):
    groups, members = mesh.devices.shape
    parts = 1
    while groups % (4 * parts) == 0 and H % (2 * parts * members) == 0:
        parts *= 2
    spans = groups // parts
    split = Mesh(mesh.devices.reshape(spans, parts, members), ("span", "part", "sp"))
    tokens = P(("span", "part", "sp"), None)
    placed = (tokens, tokens, tokens, P(None, None, "sp"), P(), P("sp"))
    return jax.shard_map(
        functools.partial(local, spans),
        mesh=split, in_specs=placed, out_specs=tokens, check_vma=False,
    )
```

```python
import functools

import jax
import jax.numpy as jnp
from jax import lax
from jax.experimental import pallas as pl
from jax.experimental.pallas import tpu as pltpu
from jax.sharding import Mesh
from jax.sharding import PartitionSpec as P

H = 32
DH = 128
BLOCK = 256
TAIL = 8
RIM = 16
GROUP = ("part", "sp")


def dot(a, b):
    return jnp.dot(a, b, preferred_element_type=jnp.float32)


def dot_nt(a, b):
    return lax.dot_general(a, b, (((1,), (1,)), ((), ())), preferred_element_type=jnp.float32)


def conv(pad_ref, weights, begin):
    total = jnp.zeros((BLOCK, pad_ref.shape[1]), jnp.float32)
    for tap in range(weights.shape[0]):
        row = TAIL + begin - tap
        total = total + weights[tap][None, :] * pad_ref[row : row + BLOCK]
    return total.astype(jnp.bfloat16)


def relu16(x):
    return jnp.maximum(x, 0.0).astype(jnp.bfloat16)


def pack_kernel(starts, *refs):
    *sources, out_ref, held, sems = refs
    width = held.shape[-1] // sems.shape[1]
    copies = {}
    for piece in range(sems.shape[1]):
        for member, source in enumerate(sources):
            cols = pl.ds(piece * width, width)
            copies[piece, member] = pltpu.make_async_copy(
                source.at[:, cols], held.at[member, :, cols], sems.at[member, piece]
            )
            copies[piece, member].start()
    for piece in range(sems.shape[1]):
        for member in range(len(sources)):
            copies[piece, member].wait()
            for owner, start in enumerate(starts):
                if start // width == piece:
                    out_ref[owner, member] = held[member, :, start : start + DH]


def unpack_kernel(starts, *refs):
    *sources, out_ref = refs
    for head, source in enumerate(sources):
        for owner, start in enumerate(starts[head]):
            out_ref[:, start : start + DH] = source[owner]


def high_low(x):
    high = x.astype(jnp.bfloat16)
    return jnp.concatenate([high, (x - high.astype(jnp.float32)).astype(jnp.bfloat16)], 1)


def folded(x):
    return x[:, :DH] + x[:, DH:]


def fill(pad_ref, x_ref, member, begin, count):
    rows = x_ref.shape[2]
    chunks = count // rows
    held = x_ref[pl.ds(begin, chunks), member]
    pad_ref[TAIL : TAIL + count] = held.reshape(count, DH).astype(jnp.float32)


def totals_kernel(x_ref, halo_ref, w_ref, map_t_ref, sent_ref, k_pad, v_pad, state):
    count, _, rows, _ = x_ref.shape
    features = map_t_ref.shape[0]
    blocks, size = count * rows // BLOCK, k_pad.shape[0] - TAIL
    for member in range(3):
        held = slice(features + member * RIM, features + (member + 1) * RIM)
        sent_ref[held] = x_ref[count - 1, member, rows - RIM :]
    k_pad[:TAIL] = halo_ref[1, RIM - TAIL :].astype(jnp.float32)
    v_pad[:TAIL] = halo_ref[2, RIM - TAIL :].astype(jnp.float32)

    def step(i):
        fill(k_pad, x_ref, 1, i * (size // rows), size)
        fill(v_pad, x_ref, 2, i * (size // rows), size)
        update = None
        for begin in range(0, size, BLOCK):
            keys = conv(k_pad, w_ref[1], begin)
            values = conv(v_pad, w_ref[2], begin)
            part = dot(relu16(dot_nt(map_t_ref[...], keys)), values)
            update = part if update is None else update + part
        return update

    state[...] = step(0)

    def later(i, carry):
        k_pad[:TAIL] = k_pad[size:]
        v_pad[:TAIL] = v_pad[size:]
        state[...] += step(i)
        return carry

    lax.fori_loop(1, blocks * BLOCK // size, later, 0)
    sent_ref[:features] = state[...].astype(jnp.bfloat16)


def causal_scores(feats, feats_t):
    row = lax.broadcasted_iota(jnp.int32, (BLOCK, BLOCK), 0)
    col = lax.broadcasted_iota(jnp.int32, (BLOCK, BLOCK), 1)
    return jnp.where(col <= row, dot(feats, feats_t), 0.0).astype(jnp.bfloat16)


def span_kernel(x_ref, w_ref, map_ref, map_t_ref, part_ref, feat_ref, q_pad, k_pad, v_pad, state):
    count, _, rows, _ = x_ref.shape
    blocks, size = count * rows // BLOCK, q_pad.shape[0] - TAIL
    pads = (q_pad, k_pad, v_pad)

    def step(i, members):
        for member, pad in enumerate(pads):
            fill(pad, x_ref, member, i * (size // rows), size)
        for j in members:
            block = i * (size // BLOCK) + j
            queries, keys, values = (conv(pad, w_ref[m], j * BLOCK) for m, pad in enumerate(pads))
            feats_t = relu16(dot_nt(map_t_ref[...], keys))
            feats = relu16(dot(queries, map_ref[...]))
            feat_ref[block] = feats
            carried = folded(dot(feats, high_low(state[...])))
            part_ref[block] = dot(causal_scores(feats, feats_t), values) + carried
            state[...] += dot(feats_t, values)

    state[...] = jnp.zeros_like(state)
    for pad in pads:
        pad[:TAIL] = jnp.zeros((TAIL, DH), jnp.float32)
    step(0, range(1, size // BLOCK))

    def later(i, carry):
        for pad in pads:
            pad[:TAIL] = pad[size:]
        step(i, range(size // BLOCK))
        return carry

    lax.fori_loop(1, blocks * BLOCK // size, later, 0)


def finish_kernel(
    x_ref, came_ref, w_ref, map_ref, map_t_ref, part_ref, feat_ref, gain_ref,
    out_ref, q_pad, k_pad, v_pad,
):
    blocks, _, features = feat_ref.shape
    per_block = BLOCK // out_ref.shape[1]
    gain = gain_ref[...]
    state = came_ref[:features]

    def put(begin, end, numerator):
        scale = lax.rsqrt(jnp.mean(numerator * numerator, -1, keepdims=True) + 1e-06)
        done = (numerator * scale * gain).astype(jnp.bfloat16)
        held = slice(begin * per_block, end * per_block)
        out_ref[held] = done.reshape((end - begin) * per_block, BLOCK // per_block, DH)

    pads = (q_pad, k_pad, v_pad)
    for member, pad in enumerate(pads):
        end = features + (member + 1) * RIM
        pad[:TAIL] = came_ref[end - TAIL : end].astype(jnp.float32)
        fill(pad, x_ref, member, 0, BLOCK)
    queries, keys, values = (conv(pad, w_ref[member], 0) for member, pad in enumerate(pads))
    feats_t = relu16(dot_nt(map_t_ref[...], keys))
    feats = relu16(dot(queries, map_ref[...]))
    later = high_low(state.astype(jnp.float32) + dot(feats_t, values))
    put(0, 1, dot(causal_scores(feats, feats_t), values) + dot(feats, state))
    for begin in range(1, blocks, 2):
        end = min(begin + 2, blocks)
        feats = feat_ref[begin:end].reshape((end - begin) * BLOCK, features)
        part = part_ref[begin:end].reshape((end - begin) * BLOCK, DH)
        put(begin, end, part + folded(dot(feats, later)))


LIMIT = 24 * 1024 * 1024
MOST = 60 * 1024 * 1024
VMEM = pl.BlockSpec(memory_space=pltpu.VMEM)
HBM = pl.BlockSpec(memory_space=pltpu.HBM)


def whole_call(kernel, inputs, outputs, scratch=(), flops=0, place=VMEM, limit=LIMIT):
    moved = sum(x.size * x.dtype.itemsize for x in [*inputs, *outputs])
    return pl.pallas_call(
        kernel,
        in_specs=[place] * len(inputs),
        out_specs=[VMEM] * len(outputs),
        out_shape=outputs,
        scratch_shapes=scratch,
        compiler_params=pltpu.CompilerParams(vmem_limit_bytes=limit),
        cost_estimate=pl.CostEstimate(flops=flops, bytes_accessed=moved, transcendentals=0),
    )(*inputs)


def shaped(shape, dtype=jnp.bfloat16):
    return jax.ShapeDtypeStruct(shape, dtype)


def next_span(block, spans):
    return lax.ppermute(block, "span", [(i, i + 1) for i in range(spans - 1)])


def exchange(block):
    return lax.all_to_all(block, GROUP, split_axis=0, concat_axis=0, tiled=True)


def after(value, other):
    return lax.optimization_barrier((value, other))[0]


def local(spans, query_input, key_input, value_heads_input, conv_weight, feature_map, out_gain):
    rows, model = query_input.shape
    parts, members = lax.axis_size("part"), lax.axis_size("sp")
    count = parts * members
    width = model // count
    heads, tokens, features = width // DH, count * rows, feature_map.shape[1]
    blocks = tokens // BLOCK
    starts = [
        [((d % members) * parts + d // members) * width + head * DH for d in range(count)]
        for head in range(heads)
    ]
    column = lax.axis_index("part") * width
    weights = lax.dynamic_slice_in_dim(conv_weight, column, width, 2)
    gains = lax.dynamic_slice_in_dim(out_gain, column, width, 0)[None]
    map_t = feature_map.T

    inputs = [query_input, key_input, value_heads_input]
    work = tokens * DH * features
    size = BLOCK * (2 if blocks % 2 == 0 else 1)
    wide = pltpu.VMEM((TAIL + size, DH), jnp.float32)
    narrow = pltpu.VMEM((TAIL + BLOCK, DH), jnp.float32)
    whole_state = pltpu.VMEM((features, DH), jnp.float32)
    outputs, attended = [], None
    for head in range(heads):
        cols = slice(head * DH, (head + 1) * DH)
        taps = weights[:, :, cols]
        (x,) = whole_call(
            functools.partial(pack_kernel, starts[head]),
            inputs,
            [shaped((count, 3, rows, DH))],
            [pltpu.VMEM((3, rows, model), jnp.bfloat16), pltpu.SemaphoreType.DMA((3, 4))],
            place=HBM,
            limit=MOST,
        )
        x = exchange(x)
        halo = jnp.zeros((3, RIM, DH), jnp.bfloat16)
        if spans > 2:
            halo = next_span(x[count - 1, :, rows - RIM :], spans)
        (sent,) = whole_call(
            totals_kernel,
            [x, halo, taps, map_t],
            [shaped((features + 3 * RIM, DH))],
            [wide, wide, whole_state],
            4 * work,
        )
        if spans == 2:
            came = next_span(sent, spans)
        else:
            gathered = lax.all_gather(sent[:features], "span").astype(jnp.float32)
            mine = lax.axis_index("span")
            earlier = jnp.where((jnp.arange(spans) < mine)[:, None, None], gathered, 0.0)
            state = jnp.sum(earlier, 0).astype(jnp.bfloat16)
            came = jnp.concatenate([state, halo.reshape(3 * RIM, DH)])
        if attended is not None:
            outputs.append(exchange(after(attended, sent)))
        partial, feats = whole_call(
            span_kernel,
            [x, taps, feature_map, map_t],
            [
                shaped((blocks, BLOCK, DH), jnp.float32),
                shaped((blocks, BLOCK, features)),
            ],
            [wide, wide, wide, whole_state],
            10 * work,
        )
        (attended,) = whole_call(
            finish_kernel,
            [x, came, taps, feature_map, map_t, partial, feats, gains[:, cols]],
            [shaped((count, rows, DH))],
            [narrow, narrow, narrow],
            4 * work,
        )
    outputs.append(exchange(attended))
    (result,) = whole_call(
        functools.partial(unpack_kernel, starts), outputs, [shaped((rows, model))]
    )
    return result


def solution(mesh):
    groups, members = mesh.devices.shape
    parts = 1
    while groups % (4 * parts) == 0 and H % (2 * parts * members) == 0:
        parts *= 2
    spans = groups // parts
    split = Mesh(mesh.devices.reshape(spans, parts, members), ("span", "part", "sp"))
    tokens = P(("span", "part", "sp"), None)
    placed = (tokens, tokens, tokens, P(None, None, "sp"), P(), P("sp"))
    return jax.shard_map(
        functools.partial(local, spans),
        mesh=split, in_specs=placed, out_specs=tokens, check_vma=False,
    )
```

```python
import functools

import jax
import jax.numpy as jnp
from jax import lax
from jax.experimental import pallas as pl
from jax.experimental.pallas import tpu as pltpu
from jax.sharding import Mesh
from jax.sharding import PartitionSpec as P

H = 32
DH = 128
BLOCK = 256
TAIL = 8
RIM = 16
GROUP = ("part", "sp")


def dot(a, b):
    return jnp.dot(a, b, preferred_element_type=jnp.float32)


def dot_nt(a, b):
    return lax.dot_general(a, b, (((1,), (1,)), ((), ())), preferred_element_type=jnp.float32)


def conv(pad_ref, weights, begin):
    total = jnp.zeros((BLOCK, pad_ref.shape[1]), jnp.float32)
    for tap in range(weights.shape[0]):
        row = TAIL + begin - tap
        total = total + weights[tap][None, :] * pad_ref[row : row + BLOCK]
    return total.astype(jnp.bfloat16)


def relu16(x):
    return jnp.maximum(x.astype(jnp.bfloat16), 0)


def pack_kernel(starts, *refs):
    *sources, out_ref, held, packed, load_sems, store_sems = refs
    pieces = load_sems.shape[1]
    width = held.shape[-1] // pieces
    loads = {}
    for piece in range(pieces):
        for member, source in enumerate(sources):
            cols = pl.ds(piece * width, width)
            loads[piece, member] = pltpu.make_async_copy(
                source.at[:, cols], held.at[member, :, cols], load_sems.at[member, piece]
            )
            loads[piece, member].start()
    stores = []
    for piece in range(pieces):
        owners = [owner for owner, start in enumerate(starts) if start // width == piece]
        for member in range(len(sources)):
            loads[piece, member].wait()
            for owner in owners:
                start = starts[owner]
                packed[owner, member] = held[member, :, start : start + DH]
        for owner in owners:
            stores.append(
                pltpu.make_async_copy(packed.at[owner], out_ref.at[owner], store_sems.at[owner])
            )
            stores[-1].start()
    for store in stores:
        store.wait()


def pack_whole_kernel(starts, *refs):
    *sources, out_ref = refs
    for member, source in enumerate(sources):
        for owner, start in enumerate(starts):
            out_ref[owner, member] = source[:, start : start + DH]


def unpack_kernel(starts, *refs):
    *sources, out_ref, held, sems = refs
    width = out_ref.shape[1] // sems.shape[0]
    stores = []
    for piece in range(sems.shape[0]):
        for head, source in enumerate(sources):
            for owner, start in enumerate(starts[head]):
                if start // width == piece:
                    held[:, start : start + DH] = source[owner]
        cols = pl.ds(piece * width, width)
        stores.append(pltpu.make_async_copy(held.at[:, cols], out_ref.at[:, cols], sems.at[piece]))
        stores[-1].start()
    for store in stores:
        store.wait()


def high_low(x):
    high = x.astype(jnp.bfloat16)
    return jnp.concatenate([high, (x - high.astype(jnp.float32)).astype(jnp.bfloat16)], 1)


def folded(x):
    return x[:, :DH] + x[:, DH:]


def fill(pad_ref, x_ref, member, begin, count):
    rows = x_ref.shape[2]
    chunks = count // rows
    held = x_ref[pl.ds(begin, chunks), member]
    pad_ref[TAIL : TAIL + count] = held.reshape(count, DH).astype(jnp.float32)


def totals_kernel(x_ref, halo_ref, w_ref, map_t_ref, sent_ref, k_pad, v_pad, state):
    count, _, rows, _ = x_ref.shape
    features = map_t_ref.shape[0]
    blocks, size = count * rows // BLOCK, k_pad.shape[0] - TAIL
    for member in range(3):
        held = slice(features + member * RIM, features + (member + 1) * RIM)
        sent_ref[held] = x_ref[count - 1, member, rows - RIM :]
    k_pad[:TAIL] = halo_ref[1, RIM - TAIL :].astype(jnp.float32)
    v_pad[:TAIL] = halo_ref[2, RIM - TAIL :].astype(jnp.float32)

    def step(i):
        fill(k_pad, x_ref, 1, i * (size // rows), size)
        fill(v_pad, x_ref, 2, i * (size // rows), size)
        update = None
        for begin in range(0, size, BLOCK):
            keys = conv(k_pad, w_ref[1], begin)
            values = conv(v_pad, w_ref[2], begin)
            part = dot(relu16(dot_nt(map_t_ref[...], keys)), values)
            update = part if update is None else update + part
        return update

    state[...] = step(0)

    def later(i, carry):
        k_pad[:TAIL] = k_pad[size:]
        v_pad[:TAIL] = v_pad[size:]
        state[...] += step(i)
        return carry

    lax.fori_loop(1, blocks * BLOCK // size, later, 0)
    sent_ref[:features] = state[...].astype(jnp.bfloat16)


def causal_scores(feats, feats_t):
    row = lax.broadcasted_iota(jnp.int32, (BLOCK, BLOCK), 0)
    col = lax.broadcasted_iota(jnp.int32, (BLOCK, BLOCK), 1)
    return jnp.where(col <= row, dot(feats, feats_t), 0.0).astype(jnp.bfloat16)


def span_kernel(x_ref, w_ref, map_ref, map_t_ref, part_ref, feat_ref, q_pad, k_pad, v_pad, state):
    count, _, rows, _ = x_ref.shape
    blocks, size = count * rows // BLOCK, q_pad.shape[0] - TAIL
    pads = (q_pad, k_pad, v_pad)

    def step(i, members):
        for member, pad in enumerate(pads):
            fill(pad, x_ref, member, i * (size // rows), size)
        for j in members:
            block = i * (size // BLOCK) + j
            queries, keys, values = (conv(pad, w_ref[m], j * BLOCK) for m, pad in enumerate(pads))
            feats_t = relu16(dot_nt(map_t_ref[...], keys))
            feats = relu16(dot(queries, map_ref[...]))
            feat_ref[block] = feats
            carried = folded(dot(feats, high_low(state[...])))
            part_ref[block] = dot(causal_scores(feats, feats_t), values) + carried
            state[...] += dot(feats_t, values)

    state[...] = jnp.zeros_like(state)
    for pad in pads:
        pad[:TAIL] = jnp.zeros((TAIL, DH), jnp.float32)
    step(0, range(1, size // BLOCK))

    def later(i, carry):
        for pad in pads:
            pad[:TAIL] = pad[size:]
        step(i, range(size // BLOCK))
        return carry

    lax.fori_loop(1, blocks * BLOCK // size, later, 0)


def finish_kernel(
    x_ref, came_ref, w_ref, map_ref, map_t_ref, part_ref, feat_ref, gain_ref,
    out_ref, q_pad, k_pad, v_pad, done, sems,
):
    blocks, _, features = feat_ref.shape
    per_block = BLOCK // out_ref.shape[1]
    gain = gain_ref[...]
    state = came_ref[:features]

    stores = []

    def put(begin, end, numerator):
        scale = lax.rsqrt(jnp.mean(numerator * numerator, -1, keepdims=True) + 1e-06)
        normed = (numerator * scale * gain).astype(jnp.bfloat16)
        first, extent = begin * per_block, (end - begin) * per_block
        done[first : first + extent] = normed.reshape(extent, BLOCK // per_block, DH)
        held = pl.ds(first, extent)
        stores.append(pltpu.make_async_copy(done.at[held], out_ref.at[held], sems.at[len(stores)]))
        stores[-1].start()

    pads = (q_pad, k_pad, v_pad)
    for member, pad in enumerate(pads):
        end = features + (member + 1) * RIM
        pad[:TAIL] = came_ref[end - TAIL : end].astype(jnp.float32)
        fill(pad, x_ref, member, 0, BLOCK)
    queries, keys, values = (conv(pad, w_ref[member], 0) for member, pad in enumerate(pads))
    feats_t = relu16(dot_nt(map_t_ref[...], keys))
    feats = relu16(dot(queries, map_ref[...]))
    later = high_low(state.astype(jnp.float32) + dot(feats_t, values))
    put(0, 1, dot(causal_scores(feats, feats_t), values) + dot(feats, state))
    for begin in range(1, blocks, 2):
        end = min(begin + 2, blocks)
        feats = feat_ref[begin:end].reshape((end - begin) * BLOCK, features)
        part = part_ref[begin:end].reshape((end - begin) * BLOCK, DH)
        put(begin, end, part + folded(dot(feats, later)))
    for store in stores:
        store.wait()


LIMIT = 24 * 1024 * 1024
MOST = 60 * 1024 * 1024
VMEM = pl.BlockSpec(memory_space=pltpu.VMEM)
HBM = pl.BlockSpec(memory_space=pltpu.HBM)


def whole_call(kernel, inputs, outputs, scratch=(), read=VMEM, written=VMEM, limit=LIMIT):
    return pl.pallas_call(
        kernel,
        in_specs=[read] * len(inputs),
        out_specs=[written] * len(outputs),
        out_shape=outputs,
        scratch_shapes=scratch,
        compiler_params=pltpu.CompilerParams(vmem_limit_bytes=limit),
    )(*inputs)


def shaped(shape, dtype=jnp.bfloat16):
    return jax.ShapeDtypeStruct(shape, dtype)


def next_span(block, spans):
    return lax.ppermute(block, "span", [(i, i + 1) for i in range(spans - 1)])


def exchange(block):
    return lax.all_to_all(block, GROUP, split_axis=0, concat_axis=0, tiled=True)


def after(value, other):
    return lax.optimization_barrier((value, other))[0]


def local(spans, query_input, key_input, value_heads_input, conv_weight, feature_map, out_gain):
    rows, model = query_input.shape
    parts, members = lax.axis_size("part"), lax.axis_size("sp")
    count = parts * members
    width = model // count
    heads, tokens, features = width // DH, count * rows, feature_map.shape[1]
    blocks = tokens // BLOCK
    starts = [
        [((d % members) * parts + d // members) * width + head * DH for d in range(count)]
        for head in range(heads)
    ]
    column = lax.axis_index("part") * width
    weights = lax.dynamic_slice_in_dim(conv_weight, column, width, 2)
    gains = lax.dynamic_slice_in_dim(out_gain, column, width, 0)[None]
    map_t = feature_map.T

    inputs = [query_input, key_input, value_heads_input]
    size = BLOCK * (2 if blocks % 2 == 0 else 1)
    wide = pltpu.VMEM((TAIL + size, DH), jnp.float32)
    narrow = pltpu.VMEM((TAIL + BLOCK, DH), jnp.float32)
    whole_state = pltpu.VMEM((features, DH), jnp.float32)
    outputs, attended = [], None
    for head in range(heads):
        cols = slice(head * DH, (head + 1) * DH)
        taps = weights[:, :, cols]
        packed = shaped((count, 3, rows, DH))
        if head == 0:
            (x,) = whole_call(
                functools.partial(pack_kernel, starts[head]),
                inputs,
                [packed],
                [
                    pltpu.VMEM((3, rows, model), jnp.bfloat16),
                    pltpu.VMEM(packed.shape, packed.dtype),
                    pltpu.SemaphoreType.DMA((3, 4)),
                    pltpu.SemaphoreType.DMA((count,)),
                ],
                read=HBM, written=HBM, limit=MOST,
            )
        else:
            (x,) = whole_call(functools.partial(pack_whole_kernel, starts[head]), inputs, [packed])
        x = exchange(x)
        if attended is not None:
            x = after(x, attended)
        halo = jnp.zeros((3, RIM, DH), jnp.bfloat16)
        if spans > 2:
            halo = next_span(x[count - 1, :, rows - RIM :], spans)
        (sent,) = whole_call(
            totals_kernel,
            [x, halo, taps, map_t],
            [shaped((features + 3 * RIM, DH))],
            [wide, wide, whole_state],
        )
        if spans == 2:
            came = next_span(sent, spans)
        else:
            gathered = lax.all_gather(sent[:features], "span").astype(jnp.float32)
            mine = lax.axis_index("span")
            earlier = jnp.where((jnp.arange(spans) < mine)[:, None, None], gathered, 0.0)
            state = jnp.sum(earlier, 0).astype(jnp.bfloat16)
            came = jnp.concatenate([state, halo.reshape(3 * RIM, DH)])
        if attended is not None:
            outputs.append(exchange(after(attended, sent)))
        partial, feats = whole_call(
            span_kernel,
            [x, taps, feature_map, map_t],
            [
                shaped((blocks, BLOCK, DH), jnp.float32),
                shaped((blocks, BLOCK, features)),
            ],
            [wide, wide, wide, whole_state],
        )
        (attended,) = whole_call(
            finish_kernel,
            [x, came, taps, feature_map, map_t, partial, feats, gains[:, cols]],
            [shaped((count, rows, DH))],
            [
                narrow, narrow, narrow,
                pltpu.VMEM((count, rows, DH), jnp.bfloat16),
                pltpu.SemaphoreType.DMA((blocks // 2 + 1,)),
            ],
            written=HBM,
        )
    outputs.append(exchange(attended))
    (result,) = whole_call(
        functools.partial(unpack_kernel, starts),
        outputs,
        [shaped((rows, model))],
        [pltpu.VMEM((rows, model), jnp.bfloat16), pltpu.SemaphoreType.DMA((4,))],
        written=HBM,
    )
    return result


def solution(mesh):
    groups, members = mesh.devices.shape
    parts = 1
    while groups % (4 * parts) == 0 and H % (2 * parts * members) == 0:
        parts *= 2
    spans = groups // parts
    split = Mesh(mesh.devices.reshape(spans, parts, members), ("span", "part", "sp"))
    tokens = P(("span", "part", "sp"), None)
    placed = (tokens, tokens, tokens, P(None, None, "sp"), P(), P("sp"))
    return jax.shard_map(
        functools.partial(local, spans),
        mesh=split, in_specs=placed, out_specs=tokens, check_vma=False,
    )
```

```python
import functools

import jax
import jax.numpy as jnp
from jax import lax
from jax.experimental import pallas as pl
from jax.experimental.pallas import tpu as pltpu
from jax.sharding import Mesh
from jax.sharding import PartitionSpec as P

H = 32
DH = 128
BLOCK = 256
TAIL = 8
RIM = 16
GROUP = ("part", "sp")


def dot(a, b):
    return jnp.dot(a, b, preferred_element_type=jnp.float32)


def dot_nt(a, b):
    return lax.dot_general(a, b, (((1,), (1,)), ((), ())), preferred_element_type=jnp.float32)


def conv(pad_ref, weights, begin):
    total = jnp.zeros((BLOCK, pad_ref.shape[1]), jnp.float32)
    for tap in range(weights.shape[0]):
        row = TAIL + begin - tap
        total = total + weights[tap][None, :] * pad_ref[row : row + BLOCK]
    return total.astype(jnp.bfloat16)


def relu16(x):
    return jnp.maximum(x.astype(jnp.bfloat16), 0)


def pack_kernel(starts, *refs):
    *sources, out_ref, held, packed, load_sems, store_sems = refs
    pieces = load_sems.shape[1]
    width = held.shape[-1] // pieces
    loads = {}
    for piece in range(pieces):
        for member, source in enumerate(sources):
            cols = pl.ds(piece * width, width)
            loads[piece, member] = pltpu.make_async_copy(
                source.at[:, cols], held.at[member, :, cols], load_sems.at[member, piece]
            )
            loads[piece, member].start()
    stores = []
    for piece in range(pieces):
        owners = [owner for owner, start in enumerate(starts) if start // width == piece]
        for member in range(len(sources)):
            loads[piece, member].wait()
            for owner in owners:
                start = starts[owner]
                packed[owner, member] = held[member, :, start : start + DH]
        for owner in owners:
            stores.append(
                pltpu.make_async_copy(packed.at[owner], out_ref.at[owner], store_sems.at[owner])
            )
            stores[-1].start()
    for store in stores:
        store.wait()


def pack_whole_kernel(starts, *refs):
    *sources, out_ref = refs
    for member, source in enumerate(sources):
        for owner, start in enumerate(starts):
            out_ref[owner, member] = source[:, start : start + DH]


def unpack_kernel(x_ref, out_ref):
    parts, members, heads, _, _ = x_ref.shape
    for member in range(members):
        for part in range(parts):
            for head in range(heads):
                start = ((member * parts + part) * heads + head) * DH
                out_ref[:, start : start + DH] = x_ref[part, member, head]


def high_low(x):
    high = x.astype(jnp.bfloat16)
    return jnp.concatenate([high, (x - high.astype(jnp.float32)).astype(jnp.bfloat16)], 1)


def folded(x):
    return x[:, :DH] + x[:, DH:]


def fill(pad_ref, held):
    count = pad_ref.shape[0] - TAIL
    pad_ref[TAIL:] = held.reshape(count, DH).astype(jnp.float32)


def carry_tail(pads, first, halo):
    for member, pad in enumerate(pads):
        count = pad.shape[0] - TAIL

        @pl.when(first)
        def _(pad=pad, member=member):
            pad[:TAIL] = halo(member)

        @pl.when(jnp.logical_not(first))
        def _(pad=pad, count=count):
            pad[:TAIL] = pad[count:]


def totals_kernel(k_ref, v_ref, rim_ref, halo_ref, w_ref, map_t_ref, sent_ref, k_pad, v_pad, state):
    rows, features = k_ref.shape[2], map_t_ref.shape[0]
    size = k_pad.shape[0] - TAIL
    first = pl.program_id(0) == 0
    carry_tail(
        (k_pad, v_pad), first,
        lambda member: halo_ref[member + 1, RIM - TAIL :].astype(jnp.float32),
    )
    fill(k_pad, k_ref[...])
    fill(v_pad, v_ref[...])

    @pl.when(first)
    def _():
        state[...] = jnp.zeros_like(state)

    for begin in range(0, size, BLOCK):
        keys = conv(k_pad, w_ref[1], begin)
        values = conv(v_pad, w_ref[2], begin)
        state[...] += dot(relu16(dot_nt(map_t_ref[...], keys)), values)

    @pl.when(pl.program_id(0) == pl.num_programs(0) - 1)
    def _():
        sent_ref[:features] = state[...].astype(jnp.bfloat16)
        for member in range(3):
            held = slice(features + member * RIM, features + (member + 1) * RIM)
            sent_ref[held] = rim_ref[0, member, rows - RIM :]


def causal_scores(feats, feats_t):
    row = lax.broadcasted_iota(jnp.int32, (BLOCK, BLOCK), 0)
    col = lax.broadcasted_iota(jnp.int32, (BLOCK, BLOCK), 1)
    return jnp.where(col <= row, dot(feats, feats_t), 0.0).astype(jnp.bfloat16)


def span_kernel(x_ref, w_ref, map_ref, map_t_ref, part_ref, feat_ref, q_pad, k_pad, v_pad, state):
    first = pl.program_id(0) == 0
    pads = (q_pad, k_pad, v_pad)
    carry_tail(pads, first, lambda member: jnp.zeros((TAIL, DH), jnp.float32))
    for member, pad in enumerate(pads):
        fill(pad, x_ref[:, member])

    def one(j):
        queries, keys, values = (conv(pad, w_ref[m], j * BLOCK) for m, pad in enumerate(pads))
        feats_t = relu16(dot_nt(map_t_ref[...], keys))
        feats = relu16(dot(queries, map_ref[...]))
        feat_ref[j] = feats
        carried = folded(dot(feats, high_low(state[...])))
        part_ref[j] = dot(causal_scores(feats, feats_t), values) + carried
        state[...] += dot(feats_t, values)

    @pl.when(first)
    def _():
        state[...] = jnp.zeros_like(state)

    @pl.when(jnp.logical_not(first))
    def _():
        one(0)

    for j in range(1, part_ref.shape[0]):
        one(j)


def finish_kernel(
    x_ref, came_ref, w_ref, map_ref, map_t_ref, part_ref, feat_ref, gain_ref, *refs
):
    *others, out_ref, q_pad, k_pad, v_pad, later = refs
    blocks, _, features = feat_ref.shape
    per_block = BLOCK // out_ref.shape[2]
    gain = gain_ref[...]
    first = pl.program_id(0) == 0
    for place, other in enumerate(others):
        out_ref[:, place] = other[:, 0]

    def put(begin, end, numerator):
        scale = lax.rsqrt(jnp.mean(numerator * numerator, -1, keepdims=True) + 1e-06)
        normed = (numerator * scale * gain).astype(jnp.bfloat16)
        held = slice(begin * per_block, end * per_block)
        extent = (end - begin) * per_block
        out_ref[held, len(others)] = normed.reshape(extent, BLOCK // per_block, DH)

    def rest(begin):
        extent = (blocks - begin) * BLOCK
        feats = feat_ref[begin:].reshape(extent, features)
        put(begin, blocks, part_ref[begin:].reshape(extent, DH) + folded(dot(feats, later[...])))

    @pl.when(first)
    def _():
        state = came_ref[:features]
        pads = (q_pad, k_pad, v_pad)
        for member, pad in enumerate(pads):
            end = features + (member + 1) * RIM
            pad[:TAIL] = came_ref[end - TAIL : end].astype(jnp.float32)
            fill(pad, x_ref[:, member])
        queries, keys, values = (conv(pad, w_ref[member], 0) for member, pad in enumerate(pads))
        feats_t = relu16(dot_nt(map_t_ref[...], keys))
        feats = relu16(dot(queries, map_ref[...]))
        later[...] = high_low(state.astype(jnp.float32) + dot(feats_t, values))
        put(0, 1, dot(causal_scores(feats, feats_t), values) + dot(feats, state))
        if blocks > 1:
            rest(1)

    @pl.when(jnp.logical_not(first))
    def _():
        rest(0)


LIMIT = 24 * 1024 * 1024
MOST = 60 * 1024 * 1024
VMEM = pl.BlockSpec(memory_space=pltpu.VMEM)
HBM = pl.BlockSpec(memory_space=pltpu.HBM)


COST = pl.CostEstimate(flops=1000, bytes_accessed=1000, transcendentals=0)
GRID = pltpu.CompilerParams(dimension_semantics=("arbitrary",), vmem_limit_bytes=LIMIT)


def whole_call(kernel, inputs, outputs, scratch=(), read=VMEM, written=VMEM, limit=LIMIT):
    return pl.pallas_call(
        kernel,
        in_specs=[read] * len(inputs),
        out_specs=[written] * len(outputs),
        out_shape=outputs,
        scratch_shapes=scratch,
        compiler_params=pltpu.CompilerParams(vmem_limit_bytes=limit),
        cost_estimate=COST,
    )(*inputs)


def stepped(kernel, steps, inputs, specs, out_specs, outputs, scratch):
    return pl.pallas_call(
        kernel,
        grid=(steps,),
        in_specs=specs,
        out_specs=out_specs,
        out_shape=outputs,
        scratch_shapes=scratch,
        compiler_params=GRID,
        cost_estimate=COST,
    )(*inputs)


def whole(array):
    zeros = (0,) * array.ndim
    return pl.BlockSpec(array.shape, lambda i: zeros)


def leading(*shape):
    zeros = (0,) * (len(shape) - 1)
    return pl.BlockSpec(shape, lambda i: (i, *zeros))


def shaped(shape, dtype=jnp.bfloat16):
    return jax.ShapeDtypeStruct(shape, dtype)


def next_span(block, spans):
    return lax.ppermute(block, "span", [(i, i + 1) for i in range(spans - 1)])


def exchange(block):
    return lax.all_to_all(block, GROUP, split_axis=0, concat_axis=0, tiled=True)


def after(value, other):
    return lax.optimization_barrier((value, other))[0]


def local(spans, query_input, key_input, value_heads_input, conv_weight, feature_map, out_gain):
    rows, model = query_input.shape
    parts, members = lax.axis_size("part"), lax.axis_size("sp")
    count = parts * members
    width = model // count
    heads, tokens, features = width // DH, count * rows, feature_map.shape[1]
    blocks = tokens // BLOCK
    starts = [
        [((d % members) * parts + d // members) * width + head * DH for d in range(count)]
        for head in range(heads)
    ]
    column = lax.axis_index("part") * width
    weights = lax.dynamic_slice_in_dim(conv_weight, column, width, 2)
    gains = lax.dynamic_slice_in_dim(out_gain, column, width, 0)[None]
    map_t = feature_map.T

    inputs = [query_input, key_input, value_heads_input]
    size = BLOCK * (2 if blocks % 2 == 0 else 1)
    wide = pltpu.VMEM((TAIL + size, DH), jnp.float32)
    narrow = pltpu.VMEM((TAIL + BLOCK, DH), jnp.float32)
    whole_state = pltpu.VMEM((features, DH), jnp.float32)
    chunks = size // rows
    xs, sents, spans_done = [], [], []
    for head in range(heads):
        taps = weights[:, :, head * DH : (head + 1) * DH]
        packed = shaped((count, 3, rows, DH))
        if head == 0:
            (x,) = whole_call(
                functools.partial(pack_kernel, starts[head]),
                inputs,
                [packed],
                [
                    pltpu.VMEM((3, rows, model), jnp.bfloat16),
                    pltpu.VMEM(packed.shape, packed.dtype),
                    pltpu.SemaphoreType.DMA((3, 4)),
                    pltpu.SemaphoreType.DMA((count,)),
                ],
                read=HBM, written=HBM, limit=MOST,
            )
        else:
            (x,) = whole_call(functools.partial(pack_whole_kernel, starts[head]), inputs, [packed])
        x = exchange(x)
        if spans_done:
            x = after(x, spans_done[-1][1])
        halo = jnp.zeros((3, RIM, DH), jnp.bfloat16)
        if spans > 2:
            halo = next_span(x[count - 1, :, rows - RIM :], spans)
        big = chunks * (2 if count % (2 * chunks) == 0 else 1)
        tall = pltpu.VMEM((TAIL + big * rows, DH), jnp.float32)
        sent = stepped(
            totals_kernel,
            count // big,
            [x, x, x, halo, taps, map_t],
            [
                pl.BlockSpec((big, 1, rows, DH), lambda i: (i, 1, 0, 0)),
                pl.BlockSpec((big, 1, rows, DH), lambda i: (i, 2, 0, 0)),
                pl.BlockSpec((1, 3, rows, DH), lambda i: (count - 1, 0, 0, 0)),
                whole(halo), whole(taps), whole(map_t),
            ],
            pl.BlockSpec((features + 3 * RIM, DH), lambda i: (0, 0)),
            shaped((features + 3 * RIM, DH)),
            [tall, tall, whole_state],
        )
        if spans == 2:
            came = next_span(sent, spans)
        else:
            gathered = lax.all_gather(sent[:features], "span").astype(jnp.float32)
            mine = lax.axis_index("span")
            earlier = jnp.where((jnp.arange(spans) < mine)[:, None, None], gathered, 0.0)
            state = jnp.sum(earlier, 0).astype(jnp.bfloat16)
            came = jnp.concatenate([state, halo.reshape(3 * RIM, DH)])
        done = stepped(
            span_kernel,
            count // chunks,
            [x, taps, feature_map, map_t],
            [leading(chunks, 3, rows, DH), whole(taps), whole(feature_map), whole(map_t)],
            [leading(size // BLOCK, BLOCK, DH), leading(size // BLOCK, BLOCK, features)],
            [
                shaped((blocks, BLOCK, DH), jnp.float32),
                shaped((blocks, BLOCK, features)),
            ],
            [wide, wide, wide, whole_state],
        )
        xs.append((x, came, taps))
        sents.append(sent)
        spans_done.append(done)

    attended = []
    for head in range(heads):
        x, came, taps = xs[head]
        partial, feats = spans_done[head]
        gain = gains[:, head * DH : (head + 1) * DH]
        if head < heads - 1:
            gain = after(gain, sents[-1])
        others = attended if head == heads - 1 else []
        piece = shaped((count, len(others) + 1, rows, DH))
        out = stepped(
            finish_kernel,
            count // chunks,
            [x, came, taps, feature_map, map_t, partial, feats, gain, *others],
            [
                pl.BlockSpec((BLOCK // rows, 3, rows, DH), lambda i: (0, 0, 0, 0)),
                whole(came), whole(taps), whole(feature_map), whole(map_t),
                leading(size // BLOCK, BLOCK, DH), leading(size // BLOCK, BLOCK, features),
                whole(gain), *[leading(chunks, 1, rows, DH)] * len(others),
            ],
            leading(chunks, *piece.shape[1:]),
            piece,
            [narrow, narrow, narrow, pltpu.VMEM((features, 2 * DH), jnp.bfloat16)],
        )
        attended.append(out)
    landed = exchange(attended[-1]).reshape(parts, members, heads, rows, DH)
    held = max(1, members // 4)
    return stepped(
        unpack_kernel,
        members // held,
        [landed],
        [pl.BlockSpec((parts, held, heads, rows, DH), lambda i: (0, i, 0, 0, 0))],
        pl.BlockSpec((rows, held * parts * width), lambda i: (0, i)),
        shaped((rows, model)),
        [],
    )


def solution(mesh):
    groups, members = mesh.devices.shape
    parts = 1
    while groups % (4 * parts) == 0 and H % (2 * parts * members) == 0:
        parts *= 2
    spans = groups // parts
    split = Mesh(mesh.devices.reshape(spans, parts, members), ("span", "part", "sp"))
    tokens = P(("span", "part", "sp"), None)
    placed = (tokens, tokens, tokens, P(None, None, "sp"), P(), P("sp"))
    return jax.shard_map(
        functools.partial(local, spans),
        mesh=split, in_specs=placed, out_specs=tokens, check_vma=False,
    )
```

```python
import functools

import jax
import jax.numpy as jnp
from jax import lax
from jax.experimental import pallas as pl
from jax.experimental.pallas import tpu as pltpu
from jax.sharding import Mesh
from jax.sharding import PartitionSpec as P

H = 32
DH = 128
BLOCK = 256
TAIL = 8
RIM = 16
GROUP = ("part", "sp")


def dot(a, b):
    return jnp.dot(a, b, preferred_element_type=jnp.float32)


def dot_nt(a, b):
    return lax.dot_general(a, b, (((1,), (1,)), ((), ())), preferred_element_type=jnp.float32)


def conv(pad_ref, weights, begin, count=BLOCK):
    total = jnp.zeros((count, pad_ref.shape[1]), jnp.float32)
    for tap in range(weights.shape[0]):
        row = TAIL + begin - tap
        total = total + weights[tap][None, :] * pad_ref[row : row + count]
    return total.astype(jnp.bfloat16)


def relu16(x):
    return jnp.maximum(x.astype(jnp.bfloat16), 0)


def pack_kernel(starts, *refs):
    *sources, out_ref, held, packed, load_sems, store_sems = refs
    pieces = load_sems.shape[1]
    width = held.shape[-1] // pieces
    loads = {}
    for piece in range(pieces):
        for member, source in enumerate(sources):
            cols = pl.ds(piece * width, width)
            loads[piece, member] = pltpu.make_async_copy(
                source.at[:, cols], held.at[member, :, cols], load_sems.at[member, piece]
            )
            loads[piece, member].start()
    stores = []
    for piece in range(pieces):
        owners = [owner for owner, start in enumerate(starts) if start // width == piece]
        for member in range(len(sources)):
            loads[piece, member].wait()
            for owner in owners:
                start = starts[owner]
                packed[owner, member] = held[member, :, start : start + DH]
        for owner in owners:
            stores.append(
                pltpu.make_async_copy(packed.at[owner], out_ref.at[owner], store_sems.at[owner])
            )
            stores[-1].start()
    for store in stores:
        store.wait()


def pack_whole_kernel(starts, *refs):
    *sources, out_ref = refs
    for member, source in enumerate(sources):
        for owner, start in enumerate(starts):
            out_ref[owner, member] = source[:, start : start + DH]


def unpack_kernel(x_ref, out_ref):
    parts, members, heads, _, _ = x_ref.shape
    for member in range(members):
        for part in range(parts):
            for head in range(heads):
                start = ((member * parts + part) * heads + head) * DH
                out_ref[:, start : start + DH] = x_ref[part, member, head]


def high_low(x):
    high = x.astype(jnp.bfloat16)
    return jnp.concatenate([high, (x - high.astype(jnp.float32)).astype(jnp.bfloat16)], 1)


def folded(x):
    return x[:, :DH] + x[:, DH:]


def fill(pad_ref, held):
    count = pad_ref.shape[0] - TAIL
    pad_ref[TAIL:] = held.reshape(count, DH).astype(jnp.float32)


def carry_tail(pads, first, halo):
    for member, pad in enumerate(pads):
        count = pad.shape[0] - TAIL

        @pl.when(first)
        def _(pad=pad, member=member):
            pad[:TAIL] = halo(member)

        @pl.when(jnp.logical_not(first))
        def _(pad=pad, count=count):
            pad[:TAIL] = pad[count:]


def totals_kernel(k_ref, v_ref, rim_ref, halo_ref, w_ref, map_t_ref, sent_ref, k_pad, v_pad, state):
    rows, features = k_ref.shape[2], map_t_ref.shape[0]
    size = k_pad.shape[0] - TAIL
    first = pl.program_id(0) == 0
    carry_tail(
        (k_pad, v_pad), first,
        lambda member: halo_ref[member + 1, RIM - TAIL :].astype(jnp.float32),
    )
    fill(k_pad, k_ref[...])
    fill(v_pad, v_ref[...])

    @pl.when(first)
    def _():
        state[...] = jnp.zeros_like(state)

    extent = 2 * BLOCK if size % (2 * BLOCK) == 0 else BLOCK
    for begin in range(0, size, extent):
        keys = conv(k_pad, w_ref[1], begin, extent)
        values = conv(v_pad, w_ref[2], begin, extent)
        state[...] += dot(relu16(dot_nt(map_t_ref[...], keys)), values)

    @pl.when(pl.program_id(0) == pl.num_programs(0) - 1)
    def _():
        sent_ref[:features] = state[...].astype(jnp.bfloat16)
        for member in range(3):
            held = slice(features + member * RIM, features + (member + 1) * RIM)
            sent_ref[held] = rim_ref[0, member, rows - RIM :]


def causal_scores(feats, feats_t):
    row = lax.broadcasted_iota(jnp.int32, (BLOCK, BLOCK), 0)
    col = lax.broadcasted_iota(jnp.int32, (BLOCK, BLOCK), 1)
    return jnp.where(col <= row, dot(feats, feats_t), 0.0).astype(jnp.bfloat16)


def span_kernel(x_ref, w_ref, map_ref, map_t_ref, part_ref, feat_ref, q_pad, k_pad, v_pad, state):
    first = pl.program_id(0) == 0
    pads = (q_pad, k_pad, v_pad)
    carry_tail(pads, first, lambda member: jnp.zeros((TAIL, DH), jnp.float32))
    for member, pad in enumerate(pads):
        fill(pad, x_ref[:, member])

    def one(j):
        queries, keys, values = (conv(pad, w_ref[m], j * BLOCK) for m, pad in enumerate(pads))
        feats_t = relu16(dot_nt(map_t_ref[...], keys))
        feats = relu16(dot(queries, map_ref[...]))
        feat_ref[j] = feats
        carried = folded(dot(feats, high_low(state[...])))
        part_ref[j] = dot(causal_scores(feats, feats_t), values) + carried
        state[...] += dot(feats_t, values)

    @pl.when(first)
    def _():
        state[...] = jnp.zeros_like(state)

    @pl.when(jnp.logical_not(first))
    def _():
        one(0)

    for j in range(1, part_ref.shape[0]):
        one(j)


def finish_kernel(
    x_ref, came_ref, w_ref, map_ref, map_t_ref, part_ref, feat_ref, gain_ref, *refs
):
    *others, out_ref, q_pad, k_pad, v_pad, later = refs
    blocks, _, features = feat_ref.shape
    per_block = BLOCK // out_ref.shape[2]
    gain = gain_ref[...]
    first = pl.program_id(0) == 0
    for place, other in enumerate(others):
        out_ref[:, place] = other[:, 0]

    def put(begin, end, numerator):
        scale = lax.rsqrt(jnp.mean(numerator * numerator, -1, keepdims=True) + 1e-06)
        normed = (numerator * scale * gain).astype(jnp.bfloat16)
        held = slice(begin * per_block, end * per_block)
        extent = (end - begin) * per_block
        out_ref[held, len(others)] = normed.reshape(extent, BLOCK // per_block, DH)

    def rest(begin):
        extent = (blocks - begin) * BLOCK
        feats = feat_ref[begin:].reshape(extent, features)
        put(begin, blocks, part_ref[begin:].reshape(extent, DH) + folded(dot(feats, later[...])))

    @pl.when(first)
    def _():
        follows = lax.axis_index("span") > 0
        state = jnp.where(follows, came_ref[:features], jnp.zeros((features, DH), jnp.bfloat16))
        pads = (q_pad, k_pad, v_pad)
        for member, pad in enumerate(pads):
            end = features + (member + 1) * RIM
            pad[:TAIL] = jnp.where(follows, came_ref[end - TAIL : end].astype(jnp.float32), 0.0)
            fill(pad, x_ref[:, member])
        queries, keys, values = (conv(pad, w_ref[member], 0) for member, pad in enumerate(pads))
        feats_t = relu16(dot_nt(map_t_ref[...], keys))
        feats = relu16(dot(queries, map_ref[...]))
        later[...] = high_low(state.astype(jnp.float32) + dot(feats_t, values))
        put(0, 1, dot(causal_scores(feats, feats_t), values) + dot(feats, state))
        if blocks > 1:
            rest(1)

    @pl.when(jnp.logical_not(first))
    def _():
        rest(0)


LIMIT = 24 * 1024 * 1024
MOST = 60 * 1024 * 1024
VMEM = pl.BlockSpec(memory_space=pltpu.VMEM)
HBM = pl.BlockSpec(memory_space=pltpu.HBM)


COST = pl.CostEstimate(flops=1000, bytes_accessed=1000, transcendentals=0)
GRID = pltpu.CompilerParams(dimension_semantics=("arbitrary",), vmem_limit_bytes=LIMIT)


def whole_call(kernel, inputs, outputs, scratch=(), read=VMEM, written=VMEM, limit=LIMIT):
    return pl.pallas_call(
        kernel,
        in_specs=[read] * len(inputs),
        out_specs=[written] * len(outputs),
        out_shape=outputs,
        scratch_shapes=scratch,
        compiler_params=pltpu.CompilerParams(vmem_limit_bytes=limit),
        cost_estimate=COST,
    )(*inputs)


def stepped(kernel, steps, inputs, specs, out_specs, outputs, scratch):
    return pl.pallas_call(
        kernel,
        grid=(steps,),
        in_specs=specs,
        out_specs=out_specs,
        out_shape=outputs,
        scratch_shapes=scratch,
        compiler_params=GRID,
        cost_estimate=COST,
    )(*inputs)


def whole(array):
    zeros = (0,) * array.ndim
    return pl.BlockSpec(array.shape, lambda i: zeros)


def leading(*shape):
    zeros = (0,) * (len(shape) - 1)
    return pl.BlockSpec(shape, lambda i: (i, *zeros))


def shaped(shape, dtype=jnp.bfloat16):
    return jax.ShapeDtypeStruct(shape, dtype)


def next_span(block, spans):
    return lax.ppermute(block, "span", [(i, i + 1) for i in range(spans - 1)])


def exchange(block):
    return lax.all_to_all(block, GROUP, split_axis=0, concat_axis=0, tiled=True)


def after(value, other):
    return lax.optimization_barrier((value, other))[0]


def local(spans, query_input, key_input, value_heads_input, conv_weight, feature_map, out_gain):
    rows, model = query_input.shape
    parts, members = lax.axis_size("part"), lax.axis_size("sp")
    count = parts * members
    width = model // count
    heads, tokens, features = width // DH, count * rows, feature_map.shape[1]
    blocks = tokens // BLOCK
    starts = [
        [((d % members) * parts + d // members) * width + head * DH for d in range(count)]
        for head in range(heads)
    ]
    column = lax.axis_index("part") * width
    weights = lax.dynamic_slice_in_dim(conv_weight, column, width, 2)
    gains = lax.dynamic_slice_in_dim(out_gain, column, width, 0)[None]
    map_t = feature_map.T

    inputs = [query_input, key_input, value_heads_input]
    size = BLOCK * (2 if blocks % 2 == 0 else 1)
    wide = pltpu.VMEM((TAIL + size, DH), jnp.float32)
    narrow = pltpu.VMEM((TAIL + BLOCK, DH), jnp.float32)
    whole_state = pltpu.VMEM((features, DH), jnp.float32)
    chunks = size // rows
    xs, sents, spans_done = [], [], []
    for head in range(heads):
        taps = weights[:, :, head * DH : (head + 1) * DH]
        packed = shaped((count, 3, rows, DH))
        if head == 0:
            (x,) = whole_call(
                functools.partial(pack_kernel, starts[head]),
                inputs,
                [packed],
                [
                    pltpu.VMEM((3, rows, model), jnp.bfloat16),
                    pltpu.VMEM(packed.shape, packed.dtype),
                    pltpu.SemaphoreType.DMA((3, 4)),
                    pltpu.SemaphoreType.DMA((count,)),
                ],
                read=HBM, written=HBM, limit=MOST,
            )
        else:
            (x,) = whole_call(functools.partial(pack_whole_kernel, starts[head]), inputs, [packed])
        x = exchange(x)
        if spans_done:
            x = after(x, spans_done[-1][1])
        halo = jnp.zeros((3, RIM, DH), jnp.bfloat16)
        if spans > 2:
            halo = next_span(x[count - 1, :, rows - RIM :], spans)
        big = chunks * (2 if count % (2 * chunks) == 0 else 1)
        tall = pltpu.VMEM((TAIL + big * rows, DH), jnp.float32)
        sent = stepped(
            totals_kernel,
            count // big,
            [x, x, x, halo, taps, map_t],
            [
                pl.BlockSpec((big, 1, rows, DH), lambda i: (i, 1, 0, 0)),
                pl.BlockSpec((big, 1, rows, DH), lambda i: (i, 2, 0, 0)),
                pl.BlockSpec((1, 3, rows, DH), lambda i: (count - 1, 0, 0, 0)),
                whole(halo), whole(taps), whole(map_t),
            ],
            pl.BlockSpec((features + 3 * RIM, DH), lambda i: (0, 0)),
            shaped((features + 3 * RIM, DH)),
            [tall, tall, whole_state],
        )
        if spans == 2:
            came = lax.ppermute(sent, "span", [(0, 1), (1, 0)])
        else:
            gathered = lax.all_gather(sent[:features], "span").astype(jnp.float32)
            mine = lax.axis_index("span")
            earlier = jnp.where((jnp.arange(spans) < mine)[:, None, None], gathered, 0.0)
            state = jnp.sum(earlier, 0).astype(jnp.bfloat16)
            came = jnp.concatenate([state, halo.reshape(3 * RIM, DH)])
        done = stepped(
            span_kernel,
            count // chunks,
            [x, taps, feature_map, map_t],
            [leading(chunks, 3, rows, DH), whole(taps), whole(feature_map), whole(map_t)],
            [leading(size // BLOCK, BLOCK, DH), leading(size // BLOCK, BLOCK, features)],
            [
                shaped((blocks, BLOCK, DH), jnp.float32),
                shaped((blocks, BLOCK, features)),
            ],
            [wide, wide, wide, whole_state],
        )
        xs.append((x, came, taps))
        sents.append(sent)
        spans_done.append(done)

    attended = []
    for head in range(heads):
        x, came, taps = xs[head]
        partial, feats = spans_done[head]
        gain = gains[:, head * DH : (head + 1) * DH]
        if head < heads - 1:
            gain = after(gain, sents[-1])
        others = attended if head == heads - 1 else []
        piece = shaped((count, len(others) + 1, rows, DH))
        out = stepped(
            finish_kernel,
            count // chunks,
            [x, came, taps, feature_map, map_t, partial, feats, gain, *others],
            [
                pl.BlockSpec((BLOCK // rows, 3, rows, DH), lambda i: (0, 0, 0, 0)),
                whole(came), whole(taps), whole(feature_map), whole(map_t),
                leading(size // BLOCK, BLOCK, DH), leading(size // BLOCK, BLOCK, features),
                whole(gain), *[leading(chunks, 1, rows, DH)] * len(others),
            ],
            leading(chunks, *piece.shape[1:]),
            piece,
            [narrow, narrow, narrow, pltpu.VMEM((features, 2 * DH), jnp.bfloat16)],
        )
        attended.append(out)
    landed = exchange(attended[-1]).reshape(parts, members, heads, rows, DH)
    held = max(1, members // 4)
    return stepped(
        unpack_kernel,
        members // held,
        [landed],
        [pl.BlockSpec((parts, held, heads, rows, DH), lambda i: (0, i, 0, 0, 0))],
        pl.BlockSpec((rows, held * parts * width), lambda i: (0, i)),
        shaped((rows, model)),
        [],
    )


def solution(mesh):
    groups, members = mesh.devices.shape
    parts = 1
    while groups % (4 * parts) == 0 and H % (2 * parts * members) == 0:
        parts *= 2
    spans = groups // parts
    split = Mesh(mesh.devices.reshape(spans, parts, members), ("span", "part", "sp"))
    tokens = P(("span", "part", "sp"), None)
    placed = (tokens, tokens, tokens, P(None, None, "sp"), P(), P("sp"))
    return jax.shard_map(
        functools.partial(local, spans),
        mesh=split, in_specs=placed, out_specs=tokens, check_vma=False,
    )
```

```python
import functools

import jax
import jax.numpy as jnp
from jax import lax
from jax.experimental import pallas as pl
from jax.experimental.pallas import tpu as pltpu
from jax.sharding import Mesh
from jax.sharding import PartitionSpec as P

H = 32
DH = 128
BLOCK = 256
TAIL = 8
RIM = 16
GROUP = ("part", "sp")


def dot(a, b):
    return jnp.dot(a, b, preferred_element_type=jnp.float32)


def dot_nt(a, b):
    return lax.dot_general(a, b, (((1,), (1,)), ((), ())), preferred_element_type=jnp.float32)


def conv(pad_ref, weights, begin, count=BLOCK):
    total = jnp.zeros((count, pad_ref.shape[1]), jnp.float32)
    for tap in range(weights.shape[0]):
        row = TAIL + begin - tap
        total = total + weights[tap][None, :] * pad_ref[row : row + count]
    return total.astype(jnp.bfloat16)


def relu16(x):
    return jnp.maximum(x.astype(jnp.bfloat16), 0)


def pack_kernel(starts, *refs):
    *sources, out_ref, held, packed, load_sems, store_sems = refs
    pieces = load_sems.shape[1]
    width = held.shape[-1] // pieces
    loads = {}
    for piece in range(pieces):
        for member, source in enumerate(sources):
            cols = pl.ds(piece * width, width)
            loads[piece, member] = pltpu.make_async_copy(
                source.at[:, cols], held.at[member, :, cols], load_sems.at[member, piece]
            )
            loads[piece, member].start()
    stores = []
    for piece in range(pieces):
        owners = [owner for owner, start in enumerate(starts) if start // width == piece]
        for member in range(len(sources)):
            loads[piece, member].wait()
            for owner in owners:
                start = starts[owner]
                packed[owner, member] = held[member, :, start : start + DH]
        for owner in owners:
            stores.append(
                pltpu.make_async_copy(packed.at[owner], out_ref.at[owner], store_sems.at[owner])
            )
            stores[-1].start()
    for store in stores:
        store.wait()


def pack_whole_kernel(starts, *refs):
    *sources, out_ref = refs
    for member, source in enumerate(sources):
        for owner, start in enumerate(starts):
            out_ref[owner, member] = source[:, start : start + DH]


def unpack_kernel(x_ref, out_ref):
    parts, members, heads, _, _ = x_ref.shape
    for member in range(members):
        for part in range(parts):
            for head in range(heads):
                start = ((member * parts + part) * heads + head) * DH
                out_ref[:, start : start + DH] = x_ref[part, member, head]


def high_low(x):
    high = x.astype(jnp.bfloat16)
    return jnp.concatenate([high, (x - high.astype(jnp.float32)).astype(jnp.bfloat16)], 1)


def folded(x):
    return x[:, :DH] + x[:, DH:]


def fill(pad_ref, held):
    count = pad_ref.shape[0] - TAIL
    pad_ref[TAIL:] = held.reshape(count, DH).astype(jnp.float32)


def carry_tail(pads, first, halo):
    for member, pad in enumerate(pads):
        count = pad.shape[0] - TAIL

        @pl.when(first)
        def _(pad=pad, member=member):
            pad[:TAIL] = halo(member)

        @pl.when(jnp.logical_not(first))
        def _(pad=pad, count=count):
            pad[:TAIL] = pad[count:]


def totals_kernel(k_ref, v_ref, rim_ref, halo_ref, w_ref, map_t_ref, sent_ref, k_pad, v_pad, state):
    rows, features = k_ref.shape[2], map_t_ref.shape[0]
    size = k_pad.shape[0] - TAIL
    first = pl.program_id(0) == 0
    carry_tail(
        (k_pad, v_pad), first,
        lambda member: halo_ref[member + 1, RIM - TAIL :].astype(jnp.float32),
    )
    fill(k_pad, k_ref[...])
    fill(v_pad, v_ref[...])

    @pl.when(first)
    def _():
        state[...] = jnp.zeros_like(state)

    extent = 2 * BLOCK if size % (2 * BLOCK) == 0 else BLOCK
    for begin in range(0, size, extent):
        keys = conv(k_pad, w_ref[1], begin, extent)
        values = conv(v_pad, w_ref[2], begin, extent)
        state[...] += dot(relu16(dot_nt(map_t_ref[...], keys)), values)

    @pl.when(pl.program_id(0) == pl.num_programs(0) - 1)
    def _():
        sent_ref[:features] = state[...].astype(jnp.bfloat16)
        for member in range(3):
            held = slice(features + member * RIM, features + (member + 1) * RIM)
            sent_ref[held] = rim_ref[0, member, rows - RIM :]


def causal_scores(feats, feats_t):
    row = lax.broadcasted_iota(jnp.int32, (BLOCK, BLOCK), 0)
    col = lax.broadcasted_iota(jnp.int32, (BLOCK, BLOCK), 1)
    return jnp.where(col <= row, dot(feats, feats_t), 0.0).astype(jnp.bfloat16)


def span_kernel(x_ref, w_ref, map_ref, map_t_ref, part_ref, feat_ref, q_pad, k_pad, v_pad, state):
    blocks, size = part_ref.shape[0], q_pad.shape[0] - TAIL
    chunks, group = size // x_ref.shape[2], size // BLOCK
    pads = (q_pad, k_pad, v_pad)

    def step(i, members):
        for member, pad in enumerate(pads):
            fill(pad, x_ref[pl.ds(i * chunks, chunks), member])
        for j in members:
            queries, keys, values = (conv(pad, w_ref[m], j * BLOCK) for m, pad in enumerate(pads))
            feats_t = relu16(dot_nt(map_t_ref[...], keys))
            feats = relu16(dot(queries, map_ref[...]))
            block = i * group + j
            feat_ref[block] = feats
            carried = folded(dot(feats, high_low(state[...])))
            part_ref[block] = dot(causal_scores(feats, feats_t), values) + carried
            state[...] += dot(feats_t, values)

    state[...] = jnp.zeros_like(state)
    for pad in pads:
        pad[:TAIL] = jnp.zeros((TAIL, DH), jnp.float32)
    step(0, range(1, group))

    def later(i, carry):
        for pad in pads:
            pad[:TAIL] = pad[size:]
        step(i, range(group))
        return carry

    lax.fori_loop(1, blocks // group, later, 0)


def finish_kernel(
    x_ref, came_ref, w_ref, map_ref, map_t_ref, part_ref, feat_ref, gain_ref, *refs
):
    *others, out_ref, q_pad, k_pad, v_pad = refs
    blocks, _, features = feat_ref.shape
    per_block = BLOCK // out_ref.shape[2]
    gain = gain_ref[...]
    for place, other in enumerate(others):
        out_ref[:, place] = other[:, 0]

    def put(begin, end, numerator):
        scale = lax.rsqrt(jnp.mean(numerator * numerator, -1, keepdims=True) + 1e-06)
        normed = (numerator * scale * gain).astype(jnp.bfloat16)
        held = slice(begin * per_block, end * per_block)
        extent = (end - begin) * per_block
        out_ref[held, len(others)] = normed.reshape(extent, BLOCK // per_block, DH)

    follows = lax.axis_index("span") > 0
    state = jnp.where(follows, came_ref[:features], jnp.zeros((features, DH), jnp.bfloat16))
    pads = (q_pad, k_pad, v_pad)
    for member, pad in enumerate(pads):
        end = features + (member + 1) * RIM
        pad[:TAIL] = jnp.where(follows, came_ref[end - TAIL : end].astype(jnp.float32), 0.0)
        fill(pad, x_ref[: (pad.shape[0] - TAIL) // x_ref.shape[2], member])
    queries, keys, values = (conv(pad, w_ref[member], 0) for member, pad in enumerate(pads))
    feats_t = relu16(dot_nt(map_t_ref[...], keys))
    feats = relu16(dot(queries, map_ref[...]))
    later = high_low(state.astype(jnp.float32) + dot(feats_t, values))
    put(0, 1, dot(causal_scores(feats, feats_t), values) + dot(feats, state))
    for begin in range(1, blocks, 2):
        end = min(begin + 2, blocks)
        extent = (end - begin) * BLOCK
        feats = feat_ref[begin:end].reshape(extent, features)
        put(begin, end, part_ref[begin:end].reshape(extent, DH) + folded(dot(feats, later)))


LIMIT = 24 * 1024 * 1024
MOST = 60 * 1024 * 1024
VMEM = pl.BlockSpec(memory_space=pltpu.VMEM)
HBM = pl.BlockSpec(memory_space=pltpu.HBM)


COST = pl.CostEstimate(flops=1000, bytes_accessed=1000, transcendentals=0)
GRID = pltpu.CompilerParams(dimension_semantics=("arbitrary",), vmem_limit_bytes=LIMIT)


def whole_call(kernel, inputs, outputs, scratch=(), read=VMEM, written=VMEM, limit=LIMIT):
    return pl.pallas_call(
        kernel,
        in_specs=[read] * len(inputs),
        out_specs=[written] * len(outputs),
        out_shape=outputs,
        scratch_shapes=scratch,
        compiler_params=pltpu.CompilerParams(vmem_limit_bytes=limit),
        cost_estimate=COST,
    )(*inputs)


def stepped(kernel, steps, inputs, specs, out_specs, outputs, scratch):
    return pl.pallas_call(
        kernel,
        grid=(steps,),
        in_specs=specs,
        out_specs=out_specs,
        out_shape=outputs,
        scratch_shapes=scratch,
        compiler_params=GRID,
        cost_estimate=COST,
    )(*inputs)


def whole(array):
    zeros = (0,) * array.ndim
    return pl.BlockSpec(array.shape, lambda i: zeros)


def shaped(shape, dtype=jnp.bfloat16):
    return jax.ShapeDtypeStruct(shape, dtype)


def next_span(block, spans):
    return lax.ppermute(block, "span", [(i, i + 1) for i in range(spans - 1)])


def exchange(block):
    return lax.all_to_all(block, GROUP, split_axis=0, concat_axis=0, tiled=True)


def after(value, other):
    return lax.optimization_barrier((value, other))[0]


def local(spans, query_input, key_input, value_heads_input, conv_weight, feature_map, out_gain):
    rows, model = query_input.shape
    parts, members = lax.axis_size("part"), lax.axis_size("sp")
    count = parts * members
    width = model // count
    heads, tokens, features = width // DH, count * rows, feature_map.shape[1]
    blocks = tokens // BLOCK
    starts = [
        [((d % members) * parts + d // members) * width + head * DH for d in range(count)]
        for head in range(heads)
    ]
    column = lax.axis_index("part") * width
    weights = lax.dynamic_slice_in_dim(conv_weight, column, width, 2)
    gains = lax.dynamic_slice_in_dim(out_gain, column, width, 0)[None]
    map_t = feature_map.T

    inputs = [query_input, key_input, value_heads_input]
    size = BLOCK * (2 if blocks % 2 == 0 else 1)
    narrow = pltpu.VMEM((TAIL + BLOCK, DH), jnp.float32)
    whole_state = pltpu.VMEM((features, DH), jnp.float32)
    chunks = size // rows
    xs, sents, spans_done = [], [], []
    for head in range(heads):
        taps = weights[:, :, head * DH : (head + 1) * DH]
        packed = shaped((count, 3, rows, DH))
        if head == 0:
            (x,) = whole_call(
                functools.partial(pack_kernel, starts[head]),
                inputs,
                [packed],
                [
                    pltpu.VMEM((3, rows, model), jnp.bfloat16),
                    pltpu.VMEM(packed.shape, packed.dtype),
                    pltpu.SemaphoreType.DMA((3, 4)),
                    pltpu.SemaphoreType.DMA((count,)),
                ],
                read=HBM, written=HBM, limit=MOST,
            )
        else:
            (x,) = whole_call(functools.partial(pack_whole_kernel, starts[head]), inputs, [packed])
        x = exchange(x)
        if spans_done:
            x = after(x, spans_done[-1][1])
        halo = jnp.zeros((3, RIM, DH), jnp.bfloat16)
        if spans > 2:
            halo = next_span(x[count - 1, :, rows - RIM :], spans)
        big = chunks * (2 if count % (2 * chunks) == 0 else 1)
        tall = pltpu.VMEM((TAIL + big * rows, DH), jnp.float32)
        sent = stepped(
            totals_kernel,
            count // big,
            [x, x, x, halo, taps, map_t],
            [
                pl.BlockSpec((big, 1, rows, DH), lambda i: (i, 1, 0, 0)),
                pl.BlockSpec((big, 1, rows, DH), lambda i: (i, 2, 0, 0)),
                pl.BlockSpec((1, 3, rows, DH), lambda i: (count - 1, 0, 0, 0)),
                whole(halo), whole(taps), whole(map_t),
            ],
            pl.BlockSpec((features + 3 * RIM, DH), lambda i: (0, 0)),
            shaped((features + 3 * RIM, DH)),
            [tall, tall, whole_state],
        )
        if spans == 2:
            both = head == heads - 1
            came = lax.ppermute(sent, "span", [(0, 1), (1, 0)] if both else [(0, 1)])
        else:
            gathered = lax.all_gather(sent[:features], "span").astype(jnp.float32)
            mine = lax.axis_index("span")
            earlier = jnp.where((jnp.arange(spans) < mine)[:, None, None], gathered, 0.0)
            state = jnp.sum(earlier, 0).astype(jnp.bfloat16)
            came = jnp.concatenate([state, halo.reshape(3 * RIM, DH)])
        done = whole_call(
            span_kernel,
            [x, taps, feature_map, map_t],
            [
                shaped((blocks, BLOCK, DH), jnp.float32),
                shaped((blocks, BLOCK, features)),
            ],
            [tall, tall, tall, whole_state],
        )
        xs.append((x, came, taps))
        sents.append(sent)
        spans_done.append(done)

    attended = []
    for head in range(heads):
        x, came, taps = xs[head]
        partial, feats = spans_done[head]
        gain = gains[:, head * DH : (head + 1) * DH]
        if head < heads - 1:
            gain = after(gain, sents[-1])
        others = attended if head == heads - 1 else []
        piece = shaped((count, len(others) + 1, rows, DH))
        (out,) = whole_call(
            finish_kernel,
            [x, came, taps, feature_map, map_t, partial, feats, gain, *others],
            [piece],
            [narrow, narrow, narrow],
        )
        attended.append(out)
    landed = exchange(attended[-1]).reshape(parts, members, heads, rows, DH)
    held = max(1, members // 4)
    return stepped(
        unpack_kernel,
        members // held,
        [landed],
        [pl.BlockSpec((parts, held, heads, rows, DH), lambda i: (0, i, 0, 0, 0))],
        pl.BlockSpec((rows, held * parts * width), lambda i: (0, i)),
        shaped((rows, model)),
        [],
    )


def solution(mesh):
    groups, members = mesh.devices.shape
    parts = 1
    while groups % (4 * parts) == 0 and H % (2 * parts * members) == 0:
        parts *= 2
    spans = groups // parts
    split = Mesh(mesh.devices.reshape(spans, parts, members), ("span", "part", "sp"))
    tokens = P(("span", "part", "sp"), None)
    placed = (tokens, tokens, tokens, P(None, None, "sp"), P(), P("sp"))
    return jax.shard_map(
        functools.partial(local, spans),
        mesh=split, in_specs=placed, out_specs=tokens, check_vma=False,
    )
```

```python
import functools

import jax
import jax.numpy as jnp
from jax import lax
from jax.experimental import pallas as pl
from jax.experimental.pallas import tpu as pltpu
from jax.sharding import Mesh
from jax.sharding import PartitionSpec as P

H = 32
DH = 128
BLOCK = 256
TAIL = 8
RIM = 16
GROUP = ("part", "sp")


def dot(a, b):
    return jnp.dot(a, b, preferred_element_type=jnp.float32)


def dot_nt(a, b):
    return lax.dot_general(a, b, (((1,), (1,)), ((), ())), preferred_element_type=jnp.float32)


def conv(pad_ref, weights, begin, count=BLOCK):
    total = jnp.zeros((count, pad_ref.shape[1]), jnp.float32)
    for tap in range(weights.shape[0]):
        row = TAIL + begin - tap
        total = total + weights[tap][None, :] * pad_ref[row : row + count]
    return total.astype(jnp.bfloat16)


def relu16(x):
    return jnp.maximum(x.astype(jnp.bfloat16), 0)


def pack_kernel(starts, *refs):
    *sources, out_ref, held, packed, load_sems, store_sems = refs
    pieces = load_sems.shape[1]
    width = held.shape[-1] // pieces
    loads = {}
    for piece in range(pieces):
        for member, source in enumerate(sources):
            cols = pl.ds(piece * width, width)
            loads[piece, member] = pltpu.make_async_copy(
                source.at[:, cols], held.at[member, :, cols], load_sems.at[member, piece]
            )
            loads[piece, member].start()
    stores = []
    for piece in range(pieces):
        owners = [owner for owner, start in enumerate(starts) if start // width == piece]
        for member in range(len(sources)):
            loads[piece, member].wait()
            for owner in owners:
                start = starts[owner]
                packed[owner, member] = held[member, :, start : start + DH]
        for owner in owners:
            stores.append(
                pltpu.make_async_copy(packed.at[owner], out_ref.at[owner], store_sems.at[owner])
            )
            stores[-1].start()
    for store in stores:
        store.wait()


def pack_whole_kernel(starts, *refs):
    *sources, out_ref = refs
    for member, source in enumerate(sources):
        for owner, start in enumerate(starts):
            out_ref[owner, member] = source[:, start : start + DH]


def unpack_kernel(x_ref, out_ref):
    parts, members, heads, _, _ = x_ref.shape
    for member in range(members):
        for part in range(parts):
            for head in range(heads):
                start = ((member * parts + part) * heads + head) * DH
                out_ref[:, start : start + DH] = x_ref[part, member, head]


def high_low(x):
    high = x.astype(jnp.bfloat16)
    return jnp.concatenate([high, (x - high.astype(jnp.float32)).astype(jnp.bfloat16)], 1)


def folded(x):
    return x[:, :DH] + x[:, DH:]


def fill(pad_ref, held):
    count = pad_ref.shape[0] - TAIL
    pad_ref[TAIL:] = held.reshape(count, DH).astype(jnp.float32)


def totals_kernel(x_ref, halo_ref, w_ref, map_t_ref, sent_ref, k_pad, v_pad, state):
    count, _, rows, _ = x_ref.shape
    features, size = map_t_ref.shape[0], k_pad.shape[0] - TAIL
    chunks = size // rows
    for member in range(3):
        held = slice(features + member * RIM, features + (member + 1) * RIM)
        sent_ref[held] = x_ref[count - 1, member, rows - RIM :]
    k_pad[:TAIL] = halo_ref[1, RIM - TAIL :].astype(jnp.float32)
    v_pad[:TAIL] = halo_ref[2, RIM - TAIL :].astype(jnp.float32)
    extent = 2 * BLOCK if size % (2 * BLOCK) == 0 else BLOCK

    def step(i):
        fill(k_pad, x_ref[pl.ds(i * chunks, chunks), 1])
        fill(v_pad, x_ref[pl.ds(i * chunks, chunks), 2])
        for begin in range(0, size, extent):
            keys = conv(k_pad, w_ref[1], begin, extent)
            values = conv(v_pad, w_ref[2], begin, extent)
            update = dot(relu16(dot_nt(map_t_ref[...], keys)), values)
            if isinstance(i, int) and begin == 0:
                state[...] = update
            else:
                state[...] += update

    step(0)

    def later(i, carry):
        for pad in (k_pad, v_pad):
            pad[:TAIL] = pad[size:]
        step(i)
        return carry

    lax.fori_loop(1, count // chunks, later, 0)
    sent_ref[:features] = state[...].astype(jnp.bfloat16)


def causal_scores(feats, feats_t):
    row = lax.broadcasted_iota(jnp.int32, (BLOCK, BLOCK), 0)
    col = lax.broadcasted_iota(jnp.int32, (BLOCK, BLOCK), 1)
    return jnp.where(col <= row, dot(feats, feats_t), 0.0).astype(jnp.bfloat16)


def span_kernel(x_ref, w_ref, map_ref, map_t_ref, part_ref, feat_ref, q_pad, k_pad, v_pad, state):
    blocks, size = part_ref.shape[0], q_pad.shape[0] - TAIL
    chunks, group = size // x_ref.shape[2], size // BLOCK
    pads = (q_pad, k_pad, v_pad)

    def step(i, members):
        for member, pad in enumerate(pads):
            fill(pad, x_ref[pl.ds(i * chunks, chunks), member])
        for j in members:
            queries, keys, values = (conv(pad, w_ref[m], j * BLOCK) for m, pad in enumerate(pads))
            feats_t = relu16(dot_nt(map_t_ref[...], keys))
            feats = relu16(dot(queries, map_ref[...]))
            block = i * group + j
            feat_ref[block] = feats
            carried = folded(dot(feats, high_low(state[...])))
            part_ref[block] = dot(causal_scores(feats, feats_t), values) + carried
            state[...] += dot(feats_t, values)

    state[...] = jnp.zeros_like(state)
    for pad in pads:
        pad[:TAIL] = jnp.zeros((TAIL, DH), jnp.float32)
    step(0, range(1, group))

    def later(i, carry):
        for pad in pads:
            pad[:TAIL] = pad[size:]
        step(i, range(group))
        return carry

    lax.fori_loop(1, blocks // group, later, 0)


def finish_kernel(
    x_ref, came_ref, w_ref, map_ref, map_t_ref, part_ref, feat_ref, gain_ref, *refs
):
    *others, out_ref, q_pad, k_pad, v_pad = refs
    blocks, _, features = feat_ref.shape
    per_block = BLOCK // out_ref.shape[2]
    gain = gain_ref[...]
    for place, other in enumerate(others):
        out_ref[:, place] = other[:, 0]

    def put(begin, end, numerator):
        scale = lax.rsqrt(jnp.mean(numerator * numerator, -1, keepdims=True) + 1e-06)
        normed = (numerator * scale * gain).astype(jnp.bfloat16)
        held = slice(begin * per_block, end * per_block)
        extent = (end - begin) * per_block
        out_ref[held, len(others)] = normed.reshape(extent, BLOCK // per_block, DH)

    follows = lax.axis_index("span") > 0
    state = jnp.where(follows, came_ref[:features], jnp.zeros((features, DH), jnp.bfloat16))
    pads = (q_pad, k_pad, v_pad)
    for member, pad in enumerate(pads):
        end = features + (member + 1) * RIM
        pad[:TAIL] = jnp.where(follows, came_ref[end - TAIL : end].astype(jnp.float32), 0.0)
        fill(pad, x_ref[: (pad.shape[0] - TAIL) // x_ref.shape[2], member])
    queries, keys, values = (conv(pad, w_ref[member], 0) for member, pad in enumerate(pads))
    feats_t = relu16(dot_nt(map_t_ref[...], keys))
    feats = relu16(dot(queries, map_ref[...]))
    later = high_low(state.astype(jnp.float32) + dot(feats_t, values))
    put(0, 1, dot(causal_scores(feats, feats_t), values) + dot(feats, state))
    for begin in range(1, blocks, 2):
        end = min(begin + 2, blocks)
        extent = (end - begin) * BLOCK
        feats = feat_ref[begin:end].reshape(extent, features)
        put(begin, end, part_ref[begin:end].reshape(extent, DH) + folded(dot(feats, later)))


LIMIT = 24 * 1024 * 1024
MOST = 60 * 1024 * 1024
VMEM = pl.BlockSpec(memory_space=pltpu.VMEM)
HBM = pl.BlockSpec(memory_space=pltpu.HBM)


COST = pl.CostEstimate(flops=1000, bytes_accessed=1000, transcendentals=0)


def whole_call(kernel, inputs, outputs, scratch=(), read=VMEM, written=VMEM, limit=LIMIT):
    return pl.pallas_call(
        kernel,
        in_specs=[read] * len(inputs),
        out_specs=[written] * len(outputs),
        out_shape=outputs,
        scratch_shapes=scratch,
        compiler_params=pltpu.CompilerParams(vmem_limit_bytes=limit),
        cost_estimate=COST,
    )(*inputs)


def shaped(shape, dtype=jnp.bfloat16):
    return jax.ShapeDtypeStruct(shape, dtype)


def next_span(block, spans):
    return lax.ppermute(block, "span", [(i, i + 1) for i in range(spans - 1)])


def exchange(block):
    return lax.all_to_all(block, GROUP, split_axis=0, concat_axis=0, tiled=True)


def after(value, other):
    return lax.optimization_barrier((value, other))[0]


def local(spans, query_input, key_input, value_heads_input, conv_weight, feature_map, out_gain):
    rows, model = query_input.shape
    parts, members = lax.axis_size("part"), lax.axis_size("sp")
    count = parts * members
    width = model // count
    heads, tokens, features = width // DH, count * rows, feature_map.shape[1]
    blocks = tokens // BLOCK
    starts = [
        [((d % members) * parts + d // members) * width + head * DH for d in range(count)]
        for head in range(heads)
    ]
    column = lax.axis_index("part") * width
    weights = lax.dynamic_slice_in_dim(conv_weight, column, width, 2)
    gains = lax.dynamic_slice_in_dim(out_gain, column, width, 0)[None]
    map_t = feature_map.T

    inputs = [query_input, key_input, value_heads_input]
    size = BLOCK * (2 if blocks % 2 == 0 else 1)
    narrow = pltpu.VMEM((TAIL + BLOCK, DH), jnp.float32)
    whole_state = pltpu.VMEM((features, DH), jnp.float32)
    chunks = size // rows
    xs, sents, spans_done = [], [], []
    for head in range(heads):
        taps = weights[:, :, head * DH : (head + 1) * DH]
        packed = shaped((count, 3, rows, DH))
        if head == 0:
            (x,) = whole_call(
                functools.partial(pack_kernel, starts[head]),
                inputs,
                [packed],
                [
                    pltpu.VMEM((3, rows, model), jnp.bfloat16),
                    pltpu.VMEM(packed.shape, packed.dtype),
                    pltpu.SemaphoreType.DMA((3, 4)),
                    pltpu.SemaphoreType.DMA((count,)),
                ],
                read=HBM, written=HBM, limit=MOST,
            )
        else:
            (x,) = whole_call(functools.partial(pack_whole_kernel, starts[head]), inputs, [packed])
        x = exchange(x)
        if spans_done:
            x = after(x, spans_done[-1][1])
        halo = jnp.zeros((3, RIM, DH), jnp.bfloat16)
        if spans > 2:
            halo = next_span(x[count - 1, :, rows - RIM :], spans)
        big = chunks * (2 if count % (2 * chunks) == 0 else 1)
        tall = pltpu.VMEM((TAIL + big * rows, DH), jnp.float32)
        (sent,) = whole_call(
            totals_kernel,
            [x, halo, taps, map_t],
            [shaped((features + 3 * RIM, DH))],
            [tall, tall, whole_state],
        )
        if spans == 2:
            both = head == heads - 1
            came = lax.ppermute(sent, "span", [(0, 1), (1, 0)] if both else [(0, 1)])
        else:
            gathered = lax.all_gather(sent[:features], "span").astype(jnp.float32)
            mine = lax.axis_index("span")
            earlier = jnp.where((jnp.arange(spans) < mine)[:, None, None], gathered, 0.0)
            state = jnp.sum(earlier, 0).astype(jnp.bfloat16)
            came = jnp.concatenate([state, halo.reshape(3 * RIM, DH)])
        done = whole_call(
            span_kernel,
            [x, taps, feature_map, map_t],
            [
                shaped((blocks, BLOCK, DH), jnp.float32),
                shaped((blocks, BLOCK, features)),
            ],
            [tall, tall, tall, whole_state],
        )
        xs.append((x, came, taps))
        sents.append(sent)
        spans_done.append(done)

    attended = []
    for head in range(heads):
        x, came, taps = xs[head]
        partial, feats = spans_done[head]
        gain = gains[:, head * DH : (head + 1) * DH]
        if head < heads - 1:
            gain = after(gain, sents[-1])
        others = attended if head == heads - 1 else []
        piece = shaped((count, len(others) + 1, rows, DH))
        (out,) = whole_call(
            finish_kernel,
            [x, came, taps, feature_map, map_t, partial, feats, gain, *others],
            [piece],
            [narrow, narrow, narrow],
        )
        attended.append(out)
    landed = exchange(attended[-1]).reshape(parts, members, heads, rows, DH)
    (result,) = whole_call(unpack_kernel, [landed], [shaped((rows, model))])
    return result


def solution(mesh):
    groups, members = mesh.devices.shape
    parts = 1
    while groups % (4 * parts) == 0 and H % (2 * parts * members) == 0:
        parts *= 2
    spans = groups // parts
    split = Mesh(mesh.devices.reshape(spans, parts, members), ("span", "part", "sp"))
    tokens = P(("span", "part", "sp"), None)
    placed = (tokens, tokens, tokens, P(None, None, "sp"), P(), P("sp"))
    return jax.shard_map(
        functools.partial(local, spans),
        mesh=split, in_specs=placed, out_specs=tokens, check_vma=False,
    )
```

```python
import functools

import jax
import jax.numpy as jnp
from jax import lax
from jax.experimental import pallas as pl
from jax.experimental.pallas import tpu as pltpu
from jax.sharding import Mesh
from jax.sharding import PartitionSpec as P

H = 32
DH = 128
BLOCK = 256
TAIL = 8
RIM = 16
GROUP = ("part", "sp")


def dot(a, b):
    return jnp.dot(a, b, preferred_element_type=jnp.float32)


def dot_nt(a, b):
    return lax.dot_general(a, b, (((1,), (1,)), ((), ())), preferred_element_type=jnp.float32)


def conv(pad_ref, weights, begin, count=BLOCK):
    total = jnp.zeros((count, pad_ref.shape[1]), jnp.float32)
    for tap in range(weights.shape[0]):
        row = TAIL + begin - tap
        total = total + weights[tap][None, :] * pad_ref[row : row + count]
    return total.astype(jnp.bfloat16)


def relu16(x):
    return jnp.maximum(x.astype(jnp.bfloat16), 0)


def pack_kernel(starts, *refs):
    *sources, out_ref, held, packed, load_sems, store_sems = refs
    pieces = load_sems.shape[1]
    width = held.shape[-1] // pieces
    loads = {}
    for piece in range(pieces):
        for member, source in enumerate(sources):
            cols = pl.ds(piece * width, width)
            loads[piece, member] = pltpu.make_async_copy(
                source.at[:, cols], held.at[member, :, cols], load_sems.at[member, piece]
            )
            loads[piece, member].start()
    stores = []
    for piece in range(pieces):
        owners = [owner for owner, start in enumerate(starts) if start // width == piece]
        for member in range(len(sources)):
            loads[piece, member].wait()
            for owner in owners:
                start = starts[owner]
                packed[owner, member] = held[member, :, start : start + DH]
        for owner in owners:
            stores.append(
                pltpu.make_async_copy(packed.at[owner], out_ref.at[owner], store_sems.at[owner])
            )
            stores[-1].start()
    for store in stores:
        store.wait()


def pack_whole_kernel(starts, *refs):
    *sources, out_ref = refs
    for member, source in enumerate(sources):
        for owner, start in enumerate(starts):
            out_ref[owner, member] = source[:, start : start + DH]


def unpack_kernel(starts, *refs):
    *sources, out_ref = refs
    for head, source in enumerate(sources):
        for owner, start in enumerate(starts[head]):
            out_ref[:, start : start + DH] = source[owner]


def high_low(x):
    high = x.astype(jnp.bfloat16)
    return jnp.concatenate([high, (x - high.astype(jnp.float32)).astype(jnp.bfloat16)], 1)


def folded(x):
    return x[:, :DH] + x[:, DH:]


def fill(pad_ref, held):
    count = pad_ref.shape[0] - TAIL
    pad_ref[TAIL:] = held.reshape(count, DH).astype(jnp.float32)


def totals_kernel(x_ref, halo_ref, w_ref, map_t_ref, sent_ref, k_pad, v_pad, state):
    count, _, rows, _ = x_ref.shape
    features, size = map_t_ref.shape[0], k_pad.shape[0] - TAIL
    chunks = size // rows
    for member in range(3):
        held = slice(features + member * RIM, features + (member + 1) * RIM)
        sent_ref[held] = x_ref[count - 1, member, rows - RIM :]
    k_pad[:TAIL] = halo_ref[1, RIM - TAIL :].astype(jnp.float32)
    v_pad[:TAIL] = halo_ref[2, RIM - TAIL :].astype(jnp.float32)
    extent = 2 * BLOCK if size % (2 * BLOCK) == 0 else BLOCK

    def step(i):
        fill(k_pad, x_ref[pl.ds(i * chunks, chunks), 1])
        fill(v_pad, x_ref[pl.ds(i * chunks, chunks), 2])
        for begin in range(0, size, extent):
            keys = conv(k_pad, w_ref[1], begin, extent)
            values = conv(v_pad, w_ref[2], begin, extent)
            update = dot(relu16(dot_nt(map_t_ref[...], keys)), values)
            if isinstance(i, int) and begin == 0:
                state[...] = update
            else:
                state[...] += update

    step(0)

    def later(i, carry):
        for pad in (k_pad, v_pad):
            pad[:TAIL] = pad[size:]
        step(i)
        return carry

    lax.fori_loop(1, count // chunks, later, 0)
    sent_ref[:features] = state[...].astype(jnp.bfloat16)


def causal_scores(feats, feats_t):
    row = lax.broadcasted_iota(jnp.int32, (BLOCK, BLOCK), 0)
    col = lax.broadcasted_iota(jnp.int32, (BLOCK, BLOCK), 1)
    return jnp.where(col <= row, dot(feats, feats_t), 0.0).astype(jnp.bfloat16)


def span_kernel(x_ref, w_ref, map_ref, map_t_ref, part_ref, feat_ref, q_pad, k_pad, v_pad, state):
    blocks, size = part_ref.shape[0], q_pad.shape[0] - TAIL
    chunks, group = size // x_ref.shape[2], size // BLOCK
    pads = (q_pad, k_pad, v_pad)

    def step(i, members):
        for member, pad in enumerate(pads):
            fill(pad, x_ref[pl.ds(i * chunks, chunks), member])
        for j in members:
            queries, keys, values = (conv(pad, w_ref[m], j * BLOCK) for m, pad in enumerate(pads))
            feats_t = relu16(dot_nt(map_t_ref[...], keys))
            feats = relu16(dot(queries, map_ref[...]))
            block = i * group + j
            feat_ref[block] = feats
            carried = folded(dot(feats, high_low(state[...])))
            part_ref[block] = dot(causal_scores(feats, feats_t), values) + carried
            state[...] += dot(feats_t, values)

    state[...] = jnp.zeros_like(state)
    for pad in pads:
        pad[:TAIL] = jnp.zeros((TAIL, DH), jnp.float32)
    step(0, range(1, group))

    def later(i, carry):
        for pad in pads:
            pad[:TAIL] = pad[size:]
        step(i, range(group))
        return carry

    lax.fori_loop(1, blocks // group, later, 0)


def finish_kernel(
    x_ref, came_ref, w_ref, map_ref, map_t_ref, part_ref, feat_ref, gain_ref,
    out_ref, q_pad, k_pad, v_pad,
):
    blocks, _, features = feat_ref.shape
    per_block = BLOCK // out_ref.shape[1]
    gain = gain_ref[...]

    def put(begin, end, numerator):
        scale = lax.rsqrt(jnp.mean(numerator * numerator, -1, keepdims=True) + 1e-06)
        normed = (numerator * scale * gain).astype(jnp.bfloat16)
        held = slice(begin * per_block, end * per_block)
        extent = (end - begin) * per_block
        out_ref[held] = normed.reshape(extent, BLOCK // per_block, DH)

    follows = lax.axis_index("span") > 0
    state = jnp.where(follows, came_ref[:features], jnp.zeros((features, DH), jnp.bfloat16))
    pads = (q_pad, k_pad, v_pad)
    for member, pad in enumerate(pads):
        end = features + (member + 1) * RIM
        pad[:TAIL] = jnp.where(follows, came_ref[end - TAIL : end].astype(jnp.float32), 0.0)
        fill(pad, x_ref[: (pad.shape[0] - TAIL) // x_ref.shape[2], member])
    queries, keys, values = (conv(pad, w_ref[member], 0) for member, pad in enumerate(pads))
    feats_t = relu16(dot_nt(map_t_ref[...], keys))
    feats = relu16(dot(queries, map_ref[...]))
    later = high_low(state.astype(jnp.float32) + dot(feats_t, values))
    put(0, 1, dot(causal_scores(feats, feats_t), values) + dot(feats, state))
    for begin in range(1, blocks, 2):
        end = min(begin + 2, blocks)
        extent = (end - begin) * BLOCK
        feats = feat_ref[begin:end].reshape(extent, features)
        put(begin, end, part_ref[begin:end].reshape(extent, DH) + folded(dot(feats, later)))


LIMIT = 24 * 1024 * 1024
MOST = 60 * 1024 * 1024
VMEM = pl.BlockSpec(memory_space=pltpu.VMEM)
HBM = pl.BlockSpec(memory_space=pltpu.HBM)


COST = pl.CostEstimate(flops=1000, bytes_accessed=1000, transcendentals=0)
LONG = pl.CostEstimate(flops=10**11, bytes_accessed=1000, transcendentals=0)


def whole_call(kernel, inputs, outputs, scratch=(), read=VMEM, written=VMEM, limit=LIMIT, cost=COST):
    return pl.pallas_call(
        kernel,
        in_specs=[read] * len(inputs),
        out_specs=[written] * len(outputs),
        out_shape=outputs,
        scratch_shapes=scratch,
        compiler_params=pltpu.CompilerParams(vmem_limit_bytes=limit),
        cost_estimate=cost,
    )(*inputs)


def shaped(shape, dtype=jnp.bfloat16):
    return jax.ShapeDtypeStruct(shape, dtype)


def next_span(block, spans):
    return lax.ppermute(block, "span", [(i, i + 1) for i in range(spans - 1)])


def exchange(block):
    return lax.all_to_all(block, GROUP, split_axis=0, concat_axis=0, tiled=True)


def after(value, other):
    return lax.optimization_barrier((value, other))[0]


def local(spans, query_input, key_input, value_heads_input, conv_weight, feature_map, out_gain):
    rows, model = query_input.shape
    parts, members = lax.axis_size("part"), lax.axis_size("sp")
    count = parts * members
    width = model // count
    heads, tokens, features = width // DH, count * rows, feature_map.shape[1]
    blocks = tokens // BLOCK
    starts = [
        [((d % members) * parts + d // members) * width + head * DH for d in range(count)]
        for head in range(heads)
    ]
    column = lax.axis_index("part") * width
    weights = lax.dynamic_slice_in_dim(conv_weight, column, width, 2)
    gains = lax.dynamic_slice_in_dim(out_gain, column, width, 0)[None]
    map_t = feature_map.T

    inputs = [query_input, key_input, value_heads_input]
    size = BLOCK * (2 if blocks % 2 == 0 else 1)
    narrow = pltpu.VMEM((TAIL + BLOCK, DH), jnp.float32)
    whole_state = pltpu.VMEM((features, DH), jnp.float32)
    chunks = size // rows
    outputs, attended = [], None
    for head in range(heads):
        taps = weights[:, :, head * DH : (head + 1) * DH]
        packed = shaped((count, 3, rows, DH))
        if head == 0:
            (x,) = whole_call(
                functools.partial(pack_kernel, starts[head]),
                inputs,
                [packed],
                [
                    pltpu.VMEM((3, rows, model), jnp.bfloat16),
                    pltpu.VMEM(packed.shape, packed.dtype),
                    pltpu.SemaphoreType.DMA((3, 4)),
                    pltpu.SemaphoreType.DMA((count,)),
                ],
                read=HBM, written=HBM, limit=MOST,
            )
        else:
            (x,) = whole_call(functools.partial(pack_whole_kernel, starts[head]), inputs, [packed])
        x = exchange(x)
        if attended is not None:
            x = after(x, attended)
        halo = jnp.zeros((3, RIM, DH), jnp.bfloat16)
        if spans > 2:
            halo = next_span(x[count - 1, :, rows - RIM :], spans)
        big = chunks * (2 if count % (2 * chunks) == 0 else 1)
        tall = pltpu.VMEM((TAIL + big * rows, DH), jnp.float32)
        (sent,) = whole_call(
            totals_kernel,
            [x, halo, taps, map_t],
            [shaped((features + 3 * RIM, DH))],
            [tall, tall, whole_state],
        )
        if spans == 2:
            both = head == heads - 1
            came = lax.ppermute(sent, "span", [(0, 1), (1, 0)] if both else [(0, 1)])
        else:
            gathered = lax.all_gather(sent[:features], "span").astype(jnp.float32)
            mine = lax.axis_index("span")
            earlier = jnp.where((jnp.arange(spans) < mine)[:, None, None], gathered, 0.0)
            state = jnp.sum(earlier, 0).astype(jnp.bfloat16)
            came = jnp.concatenate([state, halo.reshape(3 * RIM, DH)])
        if attended is not None:
            outputs.append(exchange(after(attended, sent)))
        partial, feats = whole_call(
            span_kernel,
            [x, taps, feature_map, map_t],
            [
                shaped((blocks, BLOCK, DH), jnp.float32),
                shaped((blocks, BLOCK, features)),
            ],
            [tall, tall, tall, whole_state],
        )
        gain = gains[:, head * DH : (head + 1) * DH]
        (attended,) = whole_call(
            finish_kernel,
            [x, came, taps, feature_map, map_t, partial, feats, gain],
            [shaped((count, rows, DH))],
            [narrow, narrow, narrow],
            cost=LONG if head == heads - 1 else COST,
        )
    outputs.append(exchange(attended))
    (result,) = whole_call(
        functools.partial(unpack_kernel, starts), outputs, [shaped((rows, model))]
    )
    return result


def solution(mesh):
    groups, members = mesh.devices.shape
    parts = 1
    while groups % (4 * parts) == 0 and H % (2 * parts * members) == 0:
        parts *= 2
    spans = groups // parts
    split = Mesh(mesh.devices.reshape(spans, parts, members), ("span", "part", "sp"))
    tokens = P(("span", "part", "sp"), None)
    placed = (tokens, tokens, tokens, P(None, None, "sp"), P(), P("sp"))
    return jax.shard_map(
        functools.partial(local, spans),
        mesh=split, in_specs=placed, out_specs=tokens, check_vma=False,
    )
```

```python
import functools

import jax
import jax.numpy as jnp
from jax import lax
from jax.experimental import pallas as pl
from jax.experimental.pallas import tpu as pltpu
from jax.sharding import Mesh
from jax.sharding import PartitionSpec as P

H = 32
DH = 128
BLOCK = 256
TAIL = 8
RIM = 16
GROUP = ("part", "sp")


def dot(a, b):
    return jnp.dot(a, b, preferred_element_type=jnp.float32)


def dot_nt(a, b):
    return lax.dot_general(a, b, (((1,), (1,)), ((), ())), preferred_element_type=jnp.float32)


def conv(pad_ref, weights, begin, count=BLOCK):
    total = jnp.zeros((count, pad_ref.shape[1]), jnp.float32)
    for tap in range(weights.shape[0]):
        row = TAIL + begin - tap
        total = total + weights[tap][None, :] * pad_ref[row : row + count]
    return total.astype(jnp.bfloat16)


def relu16(x):
    return jnp.maximum(x.astype(jnp.bfloat16), 0)


def pack_kernel(starts, *refs):
    *sources, out_ref, held, packed, load_sems, store_sems = refs
    pieces = load_sems.shape[1]
    width = held.shape[-1] // pieces
    loads = {}
    for piece in range(pieces):
        for member, source in enumerate(sources):
            cols = pl.ds(piece * width, width)
            loads[piece, member] = pltpu.make_async_copy(
                source.at[:, cols], held.at[member, :, cols], load_sems.at[member, piece]
            )
            loads[piece, member].start()
    stores = []
    for piece in range(pieces):
        owners = [owner for owner, start in enumerate(starts) if start // width == piece]
        for member in range(len(sources)):
            loads[piece, member].wait()
            for owner in owners:
                start = starts[owner]
                packed[owner, member] = held[member, :, start : start + DH]
        for owner in owners:
            stores.append(
                pltpu.make_async_copy(packed.at[owner], out_ref.at[owner], store_sems.at[owner])
            )
            stores[-1].start()
    for store in stores:
        store.wait()


def pack_whole_kernel(starts, *refs):
    *sources, out_ref = refs
    for member, source in enumerate(sources):
        for owner, start in enumerate(starts):
            out_ref[owner, member] = source[:, start : start + DH]


def unpack_kernel(starts, x_ref, out_ref):
    for head, owners in enumerate(starts):
        for owner, start in enumerate(owners):
            out_ref[:, start : start + DH] = x_ref[owner, head]


def high_low(x):
    high = x.astype(jnp.bfloat16)
    return jnp.concatenate([high, (x - high.astype(jnp.float32)).astype(jnp.bfloat16)], 1)


def folded(x):
    return x[:, :DH] + x[:, DH:]


def fill(pad_ref, held):
    count = pad_ref.shape[0] - TAIL
    pad_ref[TAIL:] = held.reshape(count, DH).astype(jnp.float32)


def totals_kernel(x_ref, halo_ref, w_ref, map_t_ref, sent_ref, k_pad, v_pad, state):
    count, _, rows, _ = x_ref.shape
    features, size = map_t_ref.shape[0], k_pad.shape[0] - TAIL
    chunks = size // rows
    for member in range(3):
        held = slice(features + member * RIM, features + (member + 1) * RIM)
        sent_ref[held] = x_ref[count - 1, member, rows - RIM :]
    k_pad[:TAIL] = halo_ref[1, RIM - TAIL :].astype(jnp.float32)
    v_pad[:TAIL] = halo_ref[2, RIM - TAIL :].astype(jnp.float32)
    extent = 2 * BLOCK if size % (2 * BLOCK) == 0 else BLOCK

    def step(i):
        fill(k_pad, x_ref[pl.ds(i * chunks, chunks), 1])
        fill(v_pad, x_ref[pl.ds(i * chunks, chunks), 2])
        for begin in range(0, size, extent):
            keys = conv(k_pad, w_ref[1], begin, extent)
            values = conv(v_pad, w_ref[2], begin, extent)
            update = dot(relu16(dot_nt(map_t_ref[...], keys)), values)
            if isinstance(i, int) and begin == 0:
                state[...] = update
            else:
                state[...] += update

    step(0)

    def later(i, carry):
        for pad in (k_pad, v_pad):
            pad[:TAIL] = pad[size:]
        step(i)
        return carry

    lax.fori_loop(1, count // chunks, later, 0)
    sent_ref[:features] = state[...].astype(jnp.bfloat16)


def causal_scores(feats, feats_t):
    row = lax.broadcasted_iota(jnp.int32, (BLOCK, BLOCK), 0)
    col = lax.broadcasted_iota(jnp.int32, (BLOCK, BLOCK), 1)
    return jnp.where(col <= row, dot(feats, feats_t), 0.0).astype(jnp.bfloat16)


def span_kernel(x_ref, w_ref, map_ref, map_t_ref, part_ref, feat_ref, q_pad, k_pad, v_pad, state):
    blocks, size = part_ref.shape[0], q_pad.shape[0] - TAIL
    chunks, group = size // x_ref.shape[2], size // BLOCK
    pads = (q_pad, k_pad, v_pad)

    def step(i, members):
        for member, pad in enumerate(pads):
            fill(pad, x_ref[pl.ds(i * chunks, chunks), member])
        for j in members:
            queries, keys, values = (conv(pad, w_ref[m], j * BLOCK) for m, pad in enumerate(pads))
            feats_t = relu16(dot_nt(map_t_ref[...], keys))
            feats = relu16(dot(queries, map_ref[...]))
            block = i * group + j
            feat_ref[block] = feats
            carried = folded(dot(feats, high_low(state[...])))
            part_ref[block] = dot(causal_scores(feats, feats_t), values) + carried
            state[...] += dot(feats_t, values)

    state[...] = jnp.zeros_like(state)
    for pad in pads:
        pad[:TAIL] = jnp.zeros((TAIL, DH), jnp.float32)
    step(0, range(1, group))

    def later(i, carry):
        for pad in pads:
            pad[:TAIL] = pad[size:]
        step(i, range(group))
        return carry

    lax.fori_loop(1, blocks // group, later, 0)


def finish_kernel(
    x_ref, came_ref, w_ref, map_ref, map_t_ref, part_ref, feat_ref, gain_ref, *refs
):
    *others, out_ref, q_pad, k_pad, v_pad = refs
    blocks, _, features = feat_ref.shape
    per_block = BLOCK // out_ref.shape[2]
    gain = gain_ref[...]
    for place, other in enumerate(others):
        out_ref[:, place] = other[:, 0]

    def put(begin, end, numerator):
        scale = lax.rsqrt(jnp.mean(numerator * numerator, -1, keepdims=True) + 1e-06)
        normed = (numerator * scale * gain).astype(jnp.bfloat16)
        held = slice(begin * per_block, end * per_block)
        extent = (end - begin) * per_block
        out_ref[held, len(others)] = normed.reshape(extent, BLOCK // per_block, DH)

    follows = lax.axis_index("span") > 0
    state = jnp.where(follows, came_ref[:features], jnp.zeros((features, DH), jnp.bfloat16))
    pads = (q_pad, k_pad, v_pad)
    for member, pad in enumerate(pads):
        end = features + (member + 1) * RIM
        pad[:TAIL] = jnp.where(follows, came_ref[end - TAIL : end].astype(jnp.float32), 0.0)
        fill(pad, x_ref[: (pad.shape[0] - TAIL) // x_ref.shape[2], member])
    queries, keys, values = (conv(pad, w_ref[member], 0) for member, pad in enumerate(pads))
    feats_t = relu16(dot_nt(map_t_ref[...], keys))
    feats = relu16(dot(queries, map_ref[...]))
    later = high_low(state.astype(jnp.float32) + dot(feats_t, values))
    put(0, 1, dot(causal_scores(feats, feats_t), values) + dot(feats, state))
    for begin in range(1, blocks, 2):
        end = min(begin + 2, blocks)
        extent = (end - begin) * BLOCK
        feats = feat_ref[begin:end].reshape(extent, features)
        put(begin, end, part_ref[begin:end].reshape(extent, DH) + folded(dot(feats, later)))


LIMIT = 24 * 1024 * 1024
MOST = 60 * 1024 * 1024
VMEM = pl.BlockSpec(memory_space=pltpu.VMEM)
HBM = pl.BlockSpec(memory_space=pltpu.HBM)


COST = pl.CostEstimate(flops=1000, bytes_accessed=1000, transcendentals=0)


def whole_call(kernel, inputs, outputs, scratch=(), read=VMEM, written=VMEM, limit=LIMIT):
    return pl.pallas_call(
        kernel,
        in_specs=[read] * len(inputs),
        out_specs=[written] * len(outputs),
        out_shape=outputs,
        scratch_shapes=scratch,
        compiler_params=pltpu.CompilerParams(vmem_limit_bytes=limit),
        cost_estimate=COST,
    )(*inputs)


def shaped(shape, dtype=jnp.bfloat16):
    return jax.ShapeDtypeStruct(shape, dtype)


def next_span(block, spans):
    return lax.ppermute(block, "span", [(i, i + 1) for i in range(spans - 1)])


def exchange(block):
    return lax.all_to_all(block, GROUP, split_axis=0, concat_axis=0, tiled=True)


def after(value, other):
    return lax.optimization_barrier((value, other))[0]


def local(spans, query_input, key_input, value_heads_input, conv_weight, feature_map, out_gain):
    rows, model = query_input.shape
    parts, members = lax.axis_size("part"), lax.axis_size("sp")
    count = parts * members
    width = model // count
    heads, tokens, features = width // DH, count * rows, feature_map.shape[1]
    blocks = tokens // BLOCK
    starts = [
        [((d % members) * parts + d // members) * width + head * DH for d in range(count)]
        for head in range(heads)
    ]
    column = lax.axis_index("part") * width
    weights = lax.dynamic_slice_in_dim(conv_weight, column, width, 2)
    gains = lax.dynamic_slice_in_dim(out_gain, column, width, 0)[None]
    map_t = feature_map.T

    inputs = [query_input, key_input, value_heads_input]
    size = BLOCK * (2 if blocks % 2 == 0 else 1)
    narrow = pltpu.VMEM((TAIL + BLOCK, DH), jnp.float32)
    whole_state = pltpu.VMEM((features, DH), jnp.float32)
    chunks = size // rows
    attended = []
    for head in range(heads):
        taps = weights[:, :, head * DH : (head + 1) * DH]
        packed = shaped((count, 3, rows, DH))
        if head == 0:
            (x,) = whole_call(
                functools.partial(pack_kernel, starts[head]),
                inputs,
                [packed],
                [
                    pltpu.VMEM((3, rows, model), jnp.bfloat16),
                    pltpu.VMEM(packed.shape, packed.dtype),
                    pltpu.SemaphoreType.DMA((3, 4)),
                    pltpu.SemaphoreType.DMA((count,)),
                ],
                read=HBM, written=HBM, limit=MOST,
            )
        else:
            (x,) = whole_call(functools.partial(pack_whole_kernel, starts[head]), inputs, [packed])
        x = exchange(x)
        if attended:
            x = after(x, attended[-1])
        halo = jnp.zeros((3, RIM, DH), jnp.bfloat16)
        if spans > 2:
            halo = next_span(x[count - 1, :, rows - RIM :], spans)
        big = chunks * (2 if count % (2 * chunks) == 0 else 1)
        tall = pltpu.VMEM((TAIL + big * rows, DH), jnp.float32)
        (sent,) = whole_call(
            totals_kernel,
            [x, halo, taps, map_t],
            [shaped((features + 3 * RIM, DH))],
            [tall, tall, whole_state],
        )
        if spans == 2:
            both = head == heads - 1
            came = lax.ppermute(sent, "span", [(0, 1), (1, 0)] if both else [(0, 1)])
        else:
            gathered = lax.all_gather(sent[:features], "span").astype(jnp.float32)
            mine = lax.axis_index("span")
            earlier = jnp.where((jnp.arange(spans) < mine)[:, None, None], gathered, 0.0)
            state = jnp.sum(earlier, 0).astype(jnp.bfloat16)
            came = jnp.concatenate([state, halo.reshape(3 * RIM, DH)])
        partial, feats = whole_call(
            span_kernel,
            [x, taps, feature_map, map_t],
            [
                shaped((blocks, BLOCK, DH), jnp.float32),
                shaped((blocks, BLOCK, features)),
            ],
            [tall, tall, tall, whole_state],
        )
        gain = gains[:, head * DH : (head + 1) * DH]
        others = attended if head == heads - 1 else []
        (out,) = whole_call(
            finish_kernel,
            [x, came, taps, feature_map, map_t, partial, feats, gain, *others],
            [shaped((count, len(others) + 1, rows, DH))],
            [narrow, narrow, narrow],
        )
        attended.append(out)
    landed = exchange(attended[-1])
    (result,) = whole_call(
        functools.partial(unpack_kernel, starts), [landed], [shaped((rows, model))]
    )
    return result


def solution(mesh):
    groups, members = mesh.devices.shape
    parts = 1
    while groups % (4 * parts) == 0 and H % (2 * parts * members) == 0:
        parts *= 2
    spans = groups // parts
    split = Mesh(mesh.devices.reshape(spans, parts, members), ("span", "part", "sp"))
    tokens = P(("span", "part", "sp"), None)
    placed = (tokens, tokens, tokens, P(None, None, "sp"), P(), P("sp"))
    return jax.shard_map(
        functools.partial(local, spans),
        mesh=split, in_specs=placed, out_specs=tokens, check_vma=False,
    )
```

```python
import functools

import jax
import jax.numpy as jnp
from jax import lax
from jax.experimental import pallas as pl
from jax.experimental.pallas import tpu as pltpu
from jax.sharding import Mesh
from jax.sharding import PartitionSpec as P

H = 32
DH = 128
BLOCK = 256
TAIL = 8
RIM = 16
GROUP = ("part", "sp")


def dot(a, b):
    return jnp.dot(a, b, preferred_element_type=jnp.float32)


def dot_nt(a, b):
    return lax.dot_general(a, b, (((1,), (1,)), ((), ())), preferred_element_type=jnp.float32)


def conv(pad_ref, weights, begin, count=BLOCK):
    total = jnp.zeros((count, pad_ref.shape[1]), jnp.float32)
    for tap in range(weights.shape[0]):
        row = TAIL + begin - tap
        total = total + weights[tap][None, :] * pad_ref[row : row + count]
    return total.astype(jnp.bfloat16)


def relu16(x):
    return jnp.maximum(x.astype(jnp.bfloat16), 0)


def pack_kernel(layout, starts, *refs):
    *sources, out_ref, held, packed, load_sems, store_sems = refs
    rows, pieces = held.shape[1], load_sems.shape[1]
    width = held.shape[-1] // pieces
    loads = []
    for piece in range(pieces):
        for member, source in enumerate(sources):
            cols = pl.ds(piece * width, width)
            loads.append(
                pltpu.make_async_copy(
                    source.at[:, cols], held.at[member, :, cols], load_sems.at[member, piece]
                )
            )
            loads[-1].start()
    stores = []
    for piece in range(pieces):
        for load in loads[piece * len(sources) : (piece + 1) * len(sources)]:
            load.wait()
        for owner, start in enumerate(starts[0]):
            if start // width != piece:
                continue
            row = 0
            for member, head, first in layout:
                begin = starts[head][owner]
                packed[owner, row : row + rows - first] = held[member, first:, begin : begin + DH]
                row += rows - first
            stores.append(
                pltpu.make_async_copy(packed.at[owner], out_ref.at[owner], store_sems.at[owner])
            )
            stores[-1].start()
    for store in stores:
        store.wait()


def pack_one_kernel(starts, x_ref, out_ref):
    for owner, start in enumerate(starts):
        out_ref[owner] = x_ref[:, start : start + DH]


def unpack_kernel(starts, x_ref, out_ref):
    for head, owners in enumerate(starts):
        for owner, start in enumerate(owners):
            out_ref[:, start : start + DH] = x_ref[owner, head]


def high_low(x):
    high = x.astype(jnp.bfloat16)
    return jnp.concatenate([high, (x - high.astype(jnp.float32)).astype(jnp.bfloat16)], 1)


def folded(x):
    return x[:, :DH] + x[:, DH:]


def fill(pad_ref, held):
    count = pad_ref.shape[0] - TAIL
    pad_ref[TAIL:] = held.reshape(count, DH).astype(jnp.float32)


def totals_kernel(rows, rims, begins, x_ref, halo_ref, w_ref, map_t_ref, sent_ref, k_pad, v_pad, state):
    count = x_ref.shape[0]
    features, size = map_t_ref.shape[0], k_pad.shape[0] - TAIL
    chunks = size // rows
    for member, begin in enumerate(rims):
        held = slice(features + member * RIM, features + (member + 1) * RIM)
        sent_ref[held] = x_ref[count - 1, begin : begin + RIM]
    k_pad[:TAIL] = halo_ref[1, RIM - TAIL :].astype(jnp.float32)
    v_pad[:TAIL] = halo_ref[2, RIM - TAIL :].astype(jnp.float32)
    extent = 2 * BLOCK if size % (2 * BLOCK) == 0 else BLOCK

    def step(i):
        for pad, begin in zip((k_pad, v_pad), begins):
            fill(pad, x_ref[pl.ds(i * chunks, chunks), begin : begin + rows])
        for begin in range(0, size, extent):
            keys = conv(k_pad, w_ref[1], begin, extent)
            values = conv(v_pad, w_ref[2], begin, extent)
            update = dot(relu16(dot_nt(map_t_ref[...], keys)), values)
            if isinstance(i, int) and begin == 0:
                state[...] = update
            else:
                state[...] += update

    step(0)

    def later(i, carry):
        for pad in (k_pad, v_pad):
            pad[:TAIL] = pad[size:]
        step(i)
        return carry

    lax.fori_loop(1, count // chunks, later, 0)
    sent_ref[:features] = state[...].astype(jnp.bfloat16)


def causal_scores(feats, feats_t):
    row = lax.broadcasted_iota(jnp.int32, (BLOCK, BLOCK), 0)
    col = lax.broadcasted_iota(jnp.int32, (BLOCK, BLOCK), 1)
    return jnp.where(col <= row, dot(feats, feats_t), 0.0).astype(jnp.bfloat16)


def span_kernel(
    rows, begins, q_ref, kv_ref, w_ref, map_ref, map_t_ref,
    part_ref, feat_ref, q_pad, k_pad, v_pad, state,
):
    blocks, size = part_ref.shape[0], q_pad.shape[0] - TAIL
    chunks, group = size // rows, size // BLOCK
    pads = (q_pad, k_pad, v_pad)

    def step(i, members):
        for pad, ref, begin in zip(pads, (q_ref, kv_ref, kv_ref), begins):
            fill(pad, ref[pl.ds(i * chunks, chunks), begin : begin + rows])
        for j in members:
            queries, keys, values = (conv(pad, w_ref[m], j * BLOCK) for m, pad in enumerate(pads))
            feats_t = relu16(dot_nt(map_t_ref[...], keys))
            feats = relu16(dot(queries, map_ref[...]))
            block = i * group + j
            feat_ref[block] = feats
            carried = folded(dot(feats, high_low(state[...])))
            part_ref[block] = dot(causal_scores(feats, feats_t), values) + carried
            state[...] += dot(feats_t, values)

    state[...] = jnp.zeros_like(state)
    for pad in pads:
        pad[:TAIL] = jnp.zeros((TAIL, DH), jnp.float32)
    step(0, range(1, group))

    def later(i, carry):
        for pad in pads:
            pad[:TAIL] = pad[size:]
        step(i, range(group))
        return carry

    lax.fori_loop(1, blocks // group, later, 0)


def finish_kernel(
    rows, begins, q_ref, kv_ref, came_ref, w_ref, map_ref, map_t_ref, part_ref, feat_ref, gain_ref,
    *refs,
):
    *others, out_ref, q_pad, k_pad, v_pad = refs
    blocks, _, features = feat_ref.shape
    per_block = BLOCK // out_ref.shape[2]
    gain = gain_ref[...]
    for place, other in enumerate(others):
        out_ref[:, place] = other[:, 0]

    def put(begin, end, numerator):
        scale = lax.rsqrt(jnp.mean(numerator * numerator, -1, keepdims=True) + 1e-06)
        normed = (numerator * scale * gain).astype(jnp.bfloat16)
        held = slice(begin * per_block, end * per_block)
        extent = (end - begin) * per_block
        out_ref[held, len(others)] = normed.reshape(extent, BLOCK // per_block, DH)

    follows = lax.axis_index("span") > 0
    state = jnp.where(follows, came_ref[:features], jnp.zeros((features, DH), jnp.bfloat16))
    pads = (q_pad, k_pad, v_pad)
    for member, (pad, ref, begin) in enumerate(zip(pads, (q_ref, kv_ref, kv_ref), begins)):
        end = features + (member + 1) * RIM
        pad[:TAIL] = jnp.where(follows, came_ref[end - TAIL : end].astype(jnp.float32), 0.0)
        fill(pad, ref[: (pad.shape[0] - TAIL) // rows, begin : begin + rows])
    queries, keys, values = (conv(pad, w_ref[member], 0) for member, pad in enumerate(pads))
    feats_t = relu16(dot_nt(map_t_ref[...], keys))
    feats = relu16(dot(queries, map_ref[...]))
    later = high_low(state.astype(jnp.float32) + dot(feats_t, values))
    put(0, 1, dot(causal_scores(feats, feats_t), values) + dot(feats, state))
    for begin in range(1, blocks, 2):
        end = min(begin + 2, blocks)
        extent = (end - begin) * BLOCK
        feats = feat_ref[begin:end].reshape(extent, features)
        put(begin, end, part_ref[begin:end].reshape(extent, DH) + folded(dot(feats, later)))


LIMIT = 24 * 1024 * 1024
MOST = 60 * 1024 * 1024
VMEM = pl.BlockSpec(memory_space=pltpu.VMEM)
HBM = pl.BlockSpec(memory_space=pltpu.HBM)


COST = pl.CostEstimate(flops=1000, bytes_accessed=1000, transcendentals=0)


def whole_call(kernel, inputs, outputs, scratch=(), read=VMEM, written=VMEM, limit=LIMIT):
    return pl.pallas_call(
        kernel,
        in_specs=[read] * len(inputs),
        out_specs=[written] * len(outputs),
        out_shape=outputs,
        scratch_shapes=scratch,
        compiler_params=pltpu.CompilerParams(vmem_limit_bytes=limit),
        cost_estimate=COST,
    )(*inputs)


def shaped(shape, dtype=jnp.bfloat16):
    return jax.ShapeDtypeStruct(shape, dtype)


def next_span(block, spans):
    return lax.ppermute(block, "span", [(i, i + 1) for i in range(spans - 1)])


def exchange(block):
    return lax.all_to_all(block, GROUP, split_axis=0, concat_axis=0, tiled=True)


def after(value, other):
    return lax.optimization_barrier((value, other))[0]


def local(spans, query_input, key_input, value_heads_input, conv_weight, feature_map, out_gain):
    rows, model = query_input.shape
    parts, members = lax.axis_size("part"), lax.axis_size("sp")
    count = parts * members
    width = model // count
    heads, tokens, features = width // DH, count * rows, feature_map.shape[1]
    blocks = tokens // BLOCK
    starts = [
        [((d % members) * parts + d // members) * width + head * DH for d in range(count)]
        for head in range(heads)
    ]
    column = lax.axis_index("part") * width
    weights = lax.dynamic_slice_in_dim(conv_weight, column, width, 2)
    gains = lax.dynamic_slice_in_dim(out_gain, column, width, 0)[None]
    map_t = feature_map.T

    inputs = [query_input, key_input, value_heads_input]
    size = BLOCK * (2 if blocks % 2 == 0 else 1)
    narrow = pltpu.VMEM((TAIL + BLOCK, DH), jnp.float32)
    whole_state = pltpu.VMEM((features, DH), jnp.float32)
    chunks = size // rows
    big = chunks * (2 if count % (2 * chunks) == 0 else 1)
    tall = pltpu.VMEM((TAIL + big * rows, DH), jnp.float32)
    last = heads - 1

    layout = [(member, head, 0) for head in range(heads) for member in range(3)]
    if last:
        layout.remove((0, last, 0))
        layout.append((0, last, rows - RIM))
    tops = {(member, head): i * rows for i, (member, head, _) in enumerate(layout)}
    height = sum(rows - first for _, _, first in layout)
    packed = shaped((count, height, DH))
    (x,) = whole_call(
        functools.partial(pack_kernel, layout, starts),
        inputs,
        [packed],
        [
            pltpu.VMEM((3, rows, model), jnp.bfloat16),
            pltpu.VMEM(packed.shape, packed.dtype),
            pltpu.SemaphoreType.DMA((3, 4)),
            pltpu.SemaphoreType.DMA((count,)),
        ],
        read=HBM, written=HBM, limit=MOST,
    )
    x = exchange(x)

    sents, cames = [], []
    for head in range(heads):
        begins = [tops[member, head] for member in range(3)]
        taps = weights[:, :, head * DH : (head + 1) * DH]
        rims = [begin + rows - RIM for begin in begins]
        if last and head == last:
            rims[0] = begins[0]
        halo = jnp.zeros((3, RIM, DH), jnp.bfloat16)
        if spans > 2:
            tail = [x[count - 1, rim : rim + RIM] for rim in rims]
            halo = next_span(jnp.stack(tail), spans)
        (sent,) = whole_call(
            functools.partial(totals_kernel, rows, rims, begins[1:]),
            [x, halo, taps, map_t],
            [shaped((features + 3 * RIM, DH))],
            [tall, tall, whole_state],
        )
        if spans == 2:
            came = lax.ppermute(sent, "span", [(0, 1), (1, 0)])
        else:
            gathered = lax.all_gather(sent[:features], "span").astype(jnp.float32)
            mine = lax.axis_index("span")
            earlier = jnp.where((jnp.arange(spans) < mine)[:, None, None], gathered, 0.0)
            state = jnp.sum(earlier, 0).astype(jnp.bfloat16)
            came = jnp.concatenate([state, halo.reshape(3 * RIM, DH)])
        sents.append(sent)
        cames.append(came)

    if last:
        (late,) = whole_call(
            functools.partial(pack_one_kernel, starts[last]),
            [query_input],
            [shaped((count, rows, DH))],
        )
        late = exchange(after(late, sents[-1]))

    attended = []
    for head in range(heads):
        begins = [tops[member, head] for member in range(3)]
        taps = weights[:, :, head * DH : (head + 1) * DH]
        queries = x
        if last and head == last:
            begins[0] = 0
            queries = after(late, attended[-1])
        elif last:
            taps = after(taps, attended[-1] if attended else sents[-1])
        partial, feats = whole_call(
            functools.partial(span_kernel, rows, begins),
            [queries, x, taps, feature_map, map_t],
            [
                shaped((blocks, BLOCK, DH), jnp.float32),
                shaped((blocks, BLOCK, features)),
            ],
            [tall, tall, tall, whole_state],
        )
        gain = gains[:, head * DH : (head + 1) * DH]
        others = attended if head == last else []
        (out,) = whole_call(
            functools.partial(finish_kernel, rows, begins),
            [queries, x, cames[head], taps, feature_map, map_t, partial, feats, gain, *others],
            [shaped((count, len(others) + 1, rows, DH))],
            [narrow, narrow, narrow],
        )
        attended.append(out)
    landed = exchange(attended[-1])
    (result,) = whole_call(
        functools.partial(unpack_kernel, starts), [landed], [shaped((rows, model))]
    )
    return result


def solution(mesh):
    groups, members = mesh.devices.shape
    parts = 1
    while groups % (4 * parts) == 0 and H % (2 * parts * members) == 0:
        parts *= 2
    spans = groups // parts
    split = Mesh(mesh.devices.reshape(spans, parts, members), ("span", "part", "sp"))
    tokens = P(("span", "part", "sp"), None)
    placed = (tokens, tokens, tokens, P(None, None, "sp"), P(), P("sp"))
    return jax.shard_map(
        functools.partial(local, spans),
        mesh=split, in_specs=placed, out_specs=tokens, check_vma=False,
    )
```

```python
import functools

import jax
import jax.numpy as jnp
from jax import lax
from jax.experimental import pallas as pl
from jax.experimental.pallas import tpu as pltpu
from jax.sharding import Mesh
from jax.sharding import PartitionSpec as P

H = 32
DH = 128
BLOCK = 256
TAIL = 8
RIM = 16
GROUP = ("part", "sp")


def dot(a, b):
    return jnp.dot(a, b, preferred_element_type=jnp.float32)


def dot_nt(a, b):
    return lax.dot_general(a, b, (((1,), (1,)), ((), ())), preferred_element_type=jnp.float32)


def conv(pad_ref, weights, begin, count=BLOCK):
    total = jnp.zeros((count, pad_ref.shape[1]), jnp.float32)
    for tap in range(weights.shape[0]):
        row = TAIL + begin - tap
        total = total + weights[tap][None, :] * pad_ref[row : row + count]
    return total.astype(jnp.bfloat16)


def relu16(x):
    return jnp.maximum(x.astype(jnp.bfloat16), 0)


def pack_kernel(starts, *refs):
    *sources, out_ref, held, packed, load_sems, store_sems = refs
    pieces = load_sems.shape[1]
    width = held.shape[-1] // pieces
    loads = {}
    for piece in range(pieces):
        for member, source in enumerate(sources):
            cols = pl.ds(piece * width, width)
            loads[piece, member] = pltpu.make_async_copy(
                source.at[:, cols], held.at[member, :, cols], load_sems.at[member, piece]
            )
            loads[piece, member].start()
    stores = []
    for piece in range(pieces):
        owners = [owner for owner, start in enumerate(starts) if start // width == piece]
        for member in range(len(sources)):
            loads[piece, member].wait()
            for owner in owners:
                start = starts[owner]
                packed[owner, member] = held[member, :, start : start + DH]
        for owner in owners:
            stores.append(
                pltpu.make_async_copy(packed.at[owner], out_ref.at[owner], store_sems.at[owner])
            )
            stores[-1].start()
    for store in stores:
        store.wait()


def pack_whole_kernel(starts, *refs):
    *sources, out_ref = refs
    for member, source in enumerate(sources):
        for owner, start in enumerate(starts):
            out_ref[owner, member] = source[:, start : start + DH]


def unpack_kernel(x_ref, out_ref):
    parts, members, heads, _, _ = x_ref.shape
    for member in range(members):
        for part in range(parts):
            for head in range(heads):
                start = ((member * parts + part) * heads + head) * DH
                out_ref[:, start : start + DH] = x_ref[part, member, head]


def high_low(x):
    high = x.astype(jnp.bfloat16)
    return jnp.concatenate([high, (x - high.astype(jnp.float32)).astype(jnp.bfloat16)], 1)


def folded(x):
    return x[:, :DH] + x[:, DH:]


def fill(pad_ref, held):
    count = pad_ref.shape[0] - TAIL
    pad_ref[TAIL:] = held.reshape(count, DH).astype(jnp.float32)


def totals_kernel(x_ref, halo_ref, w_ref, map_t_ref, sent_ref, k_pad, v_pad, state):
    count, _, rows, _ = x_ref.shape
    features, size = map_t_ref.shape[0], k_pad.shape[0] - TAIL
    chunks = size // rows
    for member in range(3):
        held = slice(features + member * RIM, features + (member + 1) * RIM)
        sent_ref[held] = x_ref[count - 1, member, rows - RIM :]
    k_pad[:TAIL] = halo_ref[1, RIM - TAIL :].astype(jnp.float32)
    v_pad[:TAIL] = halo_ref[2, RIM - TAIL :].astype(jnp.float32)
    extent = 2 * BLOCK if size % (2 * BLOCK) == 0 else BLOCK

    def step(i):
        fill(k_pad, x_ref[pl.ds(i * chunks, chunks), 1])
        fill(v_pad, x_ref[pl.ds(i * chunks, chunks), 2])
        for begin in range(0, size, extent):
            keys = conv(k_pad, w_ref[1], begin, extent)
            values = conv(v_pad, w_ref[2], begin, extent)
            update = dot(relu16(dot_nt(map_t_ref[...], keys)), values)
            if isinstance(i, int) and begin == 0:
                state[...] = update
            else:
                state[...] += update

    step(0)

    def later(i, carry):
        for pad in (k_pad, v_pad):
            pad[:TAIL] = pad[size:]
        step(i)
        return carry

    lax.fori_loop(1, count // chunks, later, 0)
    sent_ref[:features] = state[...].astype(jnp.bfloat16)


def causal_scores(feats, feats_t):
    row = lax.broadcasted_iota(jnp.int32, (BLOCK, BLOCK), 0)
    col = lax.broadcasted_iota(jnp.int32, (BLOCK, BLOCK), 1)
    return jnp.where(col <= row, dot(feats, feats_t), 0.0).astype(jnp.bfloat16)


def span_kernel(x_ref, w_ref, map_ref, map_t_ref, part_ref, feat_ref, q_pad, k_pad, v_pad, state):
    blocks, size = part_ref.shape[0], q_pad.shape[0] - TAIL
    chunks, group = size // x_ref.shape[2], size // BLOCK
    pads = (q_pad, k_pad, v_pad)

    def step(i, members):
        for member, pad in enumerate(pads):
            fill(pad, x_ref[pl.ds(i * chunks, chunks), member])
        for j in members:
            queries, keys, values = (conv(pad, w_ref[m], j * BLOCK) for m, pad in enumerate(pads))
            feats_t = relu16(dot_nt(map_t_ref[...], keys))
            feats = relu16(dot(queries, map_ref[...]))
            block = i * group + j
            feat_ref[block] = feats
            carried = folded(dot(feats, high_low(state[...])))
            part_ref[block] = dot(causal_scores(feats, feats_t), values) + carried
            state[...] += dot(feats_t, values)

    state[...] = jnp.zeros_like(state)
    for pad in pads:
        pad[:TAIL] = jnp.zeros((TAIL, DH), jnp.float32)
    step(0, range(1, group))

    def later(i, carry):
        for pad in pads:
            pad[:TAIL] = pad[size:]
        step(i, range(group))
        return carry

    lax.fori_loop(1, blocks // group, later, 0)


def finish_kernel(
    x_ref, came_ref, w_ref, map_ref, map_t_ref, part_ref, feat_ref, gain_ref, *refs
):
    *others, out_ref, q_pad, k_pad, v_pad = refs
    blocks, _, features = feat_ref.shape
    per_block = BLOCK // out_ref.shape[2]
    gain = gain_ref[...]
    for place, other in enumerate(others):
        out_ref[:, place] = other[:, 0]

    def put(begin, end, numerator):
        scale = lax.rsqrt(jnp.mean(numerator * numerator, -1, keepdims=True) + 1e-06)
        normed = (numerator * scale * gain).astype(jnp.bfloat16)
        held = slice(begin * per_block, end * per_block)
        extent = (end - begin) * per_block
        out_ref[held, len(others)] = normed.reshape(extent, BLOCK // per_block, DH)

    follows = lax.axis_index("span") > 0
    state = jnp.where(follows, came_ref[:features], jnp.zeros((features, DH), jnp.bfloat16))
    pads = (q_pad, k_pad, v_pad)
    for member, pad in enumerate(pads):
        end = features + (member + 1) * RIM
        pad[:TAIL] = jnp.where(follows, came_ref[end - TAIL : end].astype(jnp.float32), 0.0)
        fill(pad, x_ref[: (pad.shape[0] - TAIL) // x_ref.shape[2], member])
    queries, keys, values = (conv(pad, w_ref[member], 0) for member, pad in enumerate(pads))
    feats_t = relu16(dot_nt(map_t_ref[...], keys))
    feats = relu16(dot(queries, map_ref[...]))
    later = high_low(state.astype(jnp.float32) + dot(feats_t, values))
    put(0, 1, dot(causal_scores(feats, feats_t), values) + dot(feats, state))
    for begin in range(1, blocks, 2):
        end = min(begin + 2, blocks)
        extent = (end - begin) * BLOCK
        feats = feat_ref[begin:end].reshape(extent, features)
        put(begin, end, part_ref[begin:end].reshape(extent, DH) + folded(dot(feats, later)))


LIMIT = 14 * 1024 * 1024
MOST = 60 * 1024 * 1024
VMEM = pl.BlockSpec(memory_space=pltpu.VMEM)
HBM = pl.BlockSpec(memory_space=pltpu.HBM)


COST = pl.CostEstimate(flops=1000, bytes_accessed=1000, transcendentals=0)


def whole_call(kernel, inputs, outputs, scratch=(), read=VMEM, written=VMEM, limit=LIMIT):
    return pl.pallas_call(
        kernel,
        in_specs=[read] * len(inputs),
        out_specs=[written] * len(outputs),
        out_shape=outputs,
        scratch_shapes=scratch,
        compiler_params=pltpu.CompilerParams(vmem_limit_bytes=limit),
        cost_estimate=COST,
    )(*inputs)


def shaped(shape, dtype=jnp.bfloat16):
    return jax.ShapeDtypeStruct(shape, dtype)


def next_span(block, spans):
    return lax.ppermute(block, "span", [(i, i + 1) for i in range(spans - 1)])


def exchange(block):
    return lax.all_to_all(block, GROUP, split_axis=0, concat_axis=0, tiled=True)


def after(value, other):
    return lax.optimization_barrier((value, other))[0]


def local(spans, query_input, key_input, value_heads_input, conv_weight, feature_map, out_gain):
    rows, model = query_input.shape
    parts, members = lax.axis_size("part"), lax.axis_size("sp")
    count = parts * members
    width = model // count
    heads, tokens, features = width // DH, count * rows, feature_map.shape[1]
    blocks = tokens // BLOCK
    starts = [
        [((d % members) * parts + d // members) * width + head * DH for d in range(count)]
        for head in range(heads)
    ]
    column = lax.axis_index("part") * width
    weights = lax.dynamic_slice_in_dim(conv_weight, column, width, 2)
    gains = lax.dynamic_slice_in_dim(out_gain, column, width, 0)[None]
    map_t = feature_map.T

    inputs = [query_input, key_input, value_heads_input]
    size = BLOCK * (2 if blocks % 2 == 0 else 1)
    narrow = pltpu.VMEM((TAIL + BLOCK, DH), jnp.float32)
    whole_state = pltpu.VMEM((features, DH), jnp.float32)
    chunks = size // rows
    xs, sents, spans_done = [], [], []
    for head in range(heads):
        taps = weights[:, :, head * DH : (head + 1) * DH]
        packed = shaped((count, 3, rows, DH))
        if head == 0:
            (x,) = whole_call(
                functools.partial(pack_kernel, starts[head]),
                inputs,
                [packed],
                [
                    pltpu.VMEM((3, rows, model), jnp.bfloat16),
                    pltpu.VMEM(packed.shape, packed.dtype),
                    pltpu.SemaphoreType.DMA((3, 4)),
                    pltpu.SemaphoreType.DMA((count,)),
                ],
                read=HBM, written=HBM, limit=MOST,
            )
        else:
            (x,) = whole_call(functools.partial(pack_whole_kernel, starts[head]), inputs, [packed])
        x = exchange(x)
        if spans_done:
            x = after(x, spans_done[-1][1])
        halo = jnp.zeros((3, RIM, DH), jnp.bfloat16)
        if spans > 2:
            halo = next_span(x[count - 1, :, rows - RIM :], spans)
        big = chunks * (2 if count % (2 * chunks) == 0 else 1)
        tall = pltpu.VMEM((TAIL + big * rows, DH), jnp.float32)
        (sent,) = whole_call(
            totals_kernel,
            [x, halo, taps, map_t],
            [shaped((features + 3 * RIM, DH))],
            [tall, tall, whole_state],
        )
        if spans == 2:
            both = head == heads - 1
            came = lax.ppermute(sent, "span", [(0, 1), (1, 0)] if both else [(0, 1)])
        else:
            gathered = lax.all_gather(sent[:features], "span").astype(jnp.float32)
            mine = lax.axis_index("span")
            earlier = jnp.where((jnp.arange(spans) < mine)[:, None, None], gathered, 0.0)
            state = jnp.sum(earlier, 0).astype(jnp.bfloat16)
            came = jnp.concatenate([state, halo.reshape(3 * RIM, DH)])
        done = whole_call(
            span_kernel,
            [x, taps, feature_map, map_t],
            [
                shaped((blocks, BLOCK, DH), jnp.float32),
                shaped((blocks, BLOCK, features)),
            ],
            [tall, tall, tall, whole_state],
        )
        xs.append((x, came, taps))
        sents.append(sent)
        spans_done.append(done)

    attended = []
    for head in range(heads):
        x, came, taps = xs[head]
        partial, feats = spans_done[head]
        gain = gains[:, head * DH : (head + 1) * DH]
        if head < heads - 1:
            gain = after(gain, sents[-1])
        others = attended if head == heads - 1 else []
        piece = shaped((count, len(others) + 1, rows, DH))
        (out,) = whole_call(
            finish_kernel,
            [x, came, taps, feature_map, map_t, partial, feats, gain, *others],
            [piece],
            [narrow, narrow, narrow],
        )
        attended.append(out)
    landed = exchange(attended[-1]).reshape(parts, members, heads, rows, DH)
    (result,) = whole_call(unpack_kernel, [landed], [shaped((rows, model))])
    return result


def solution(mesh):
    groups, members = mesh.devices.shape
    parts = 1
    while groups % (4 * parts) == 0 and H % (2 * parts * members) == 0:
        parts *= 2
    spans = groups // parts
    split = Mesh(mesh.devices.reshape(spans, parts, members), ("span", "part", "sp"))
    tokens = P(("span", "part", "sp"), None)
    placed = (tokens, tokens, tokens, P(None, None, "sp"), P(), P("sp"))
    return jax.shard_map(
        functools.partial(local, spans),
        mesh=split, in_specs=placed, out_specs=tokens, check_vma=False,
    )
```

```python
import functools

import jax
import jax.numpy as jnp
from jax import lax
from jax.experimental import pallas as pl
from jax.experimental.pallas import tpu as pltpu
from jax.sharding import Mesh
from jax.sharding import PartitionSpec as P

H = 32
DH = 128
BLOCK = 256
TAIL = 8
RIM = 16
GROUP = ("part", "sp")


def dot(a, b):
    return jnp.dot(a, b, preferred_element_type=jnp.float32)


def dot_nt(a, b):
    return lax.dot_general(a, b, (((1,), (1,)), ((), ())), preferred_element_type=jnp.float32)


def conv(pad_ref, weights, begin, count=BLOCK):
    total = jnp.zeros((count, pad_ref.shape[1]), jnp.float32)
    for tap in range(weights.shape[0]):
        row = TAIL + begin - tap
        total = total + weights[tap][None, :] * pad_ref[row : row + count]
    return total.astype(jnp.bfloat16)


def relu16(x):
    return jnp.maximum(x.astype(jnp.bfloat16), 0)


def pack_kernel(starts, *refs):
    *sources, out_ref, held, packed, load_sems, store_sems = refs
    pieces = load_sems.shape[1]
    width = held.shape[-1] // pieces
    loads = {}
    for piece in range(pieces):
        for member, source in enumerate(sources):
            cols = pl.ds(piece * width, width)
            loads[piece, member] = pltpu.make_async_copy(
                source.at[:, cols], held.at[member, :, cols], load_sems.at[member, piece]
            )
            loads[piece, member].start()
    stores = []
    for piece in range(pieces):
        owners = [owner for owner, start in enumerate(starts) if start // width == piece]
        for member in range(len(sources)):
            loads[piece, member].wait()
            for owner in owners:
                start = starts[owner]
                packed[owner, member] = held[member, :, start : start + DH]
        for owner in owners:
            stores.append(
                pltpu.make_async_copy(packed.at[owner], out_ref.at[owner], store_sems.at[owner])
            )
            stores[-1].start()
    for store in stores:
        store.wait()


def pack_whole_kernel(starts, *refs):
    *sources, out_ref = refs
    for member, source in enumerate(sources):
        for owner, start in enumerate(starts):
            out_ref[owner, member] = source[:, start : start + DH]


def unpack_kernel(x_ref, out_ref):
    parts, members, heads, _, _ = x_ref.shape
    for member in range(members):
        for part in range(parts):
            for head in range(heads):
                start = ((member * parts + part) * heads + head) * DH
                out_ref[:, start : start + DH] = x_ref[part, member, head]


def high_low(x):
    high = x.astype(jnp.bfloat16)
    return jnp.concatenate([high, (x - high.astype(jnp.float32)).astype(jnp.bfloat16)], 1)


def folded(x):
    return x[:, :DH] + x[:, DH:]


def fill(pad_ref, held):
    count = pad_ref.shape[0] - TAIL
    pad_ref[TAIL:] = held.reshape(count, DH).astype(jnp.float32)


def carry_tail(pads, first, halo):
    for member, pad in enumerate(pads):
        count = pad.shape[0] - TAIL

        @pl.when(first)
        def _(pad=pad, member=member):
            pad[:TAIL] = halo(member)

        @pl.when(jnp.logical_not(first))
        def _(pad=pad, count=count):
            pad[:TAIL] = pad[count:]


def totals_kernel(k_ref, v_ref, rim_ref, halo_ref, w_ref, map_t_ref, sent_ref, k_pad, v_pad, state):
    rows, features = k_ref.shape[2], map_t_ref.shape[0]
    size = k_pad.shape[0] - TAIL
    first = pl.program_id(0) == 0
    carry_tail(
        (k_pad, v_pad), first,
        lambda member: halo_ref[member + 1, RIM - TAIL :].astype(jnp.float32),
    )
    fill(k_pad, k_ref[...])
    fill(v_pad, v_ref[...])

    @pl.when(first)
    def _():
        state[...] = jnp.zeros_like(state)

    extent = 2 * BLOCK if size % (2 * BLOCK) == 0 else BLOCK
    for begin in range(0, size, extent):
        keys = conv(k_pad, w_ref[1], begin, extent)
        values = conv(v_pad, w_ref[2], begin, extent)
        state[...] += dot(relu16(dot_nt(map_t_ref[...], keys)), values)

    @pl.when(pl.program_id(0) == pl.num_programs(0) - 1)
    def _():
        sent_ref[:features] = state[...].astype(jnp.bfloat16)
        for member in range(3):
            held = slice(features + member * RIM, features + (member + 1) * RIM)
            sent_ref[held] = rim_ref[0, member, rows - RIM :]


def causal_scores(feats, feats_t):
    row = lax.broadcasted_iota(jnp.int32, (BLOCK, BLOCK), 0)
    col = lax.broadcasted_iota(jnp.int32, (BLOCK, BLOCK), 1)
    return jnp.where(col <= row, dot(feats, feats_t), 0.0).astype(jnp.bfloat16)


def span_kernel(x_ref, w_ref, map_ref, map_t_ref, part_ref, feat_ref, q_pad, k_pad, v_pad, state):
    blocks, size = part_ref.shape[0], q_pad.shape[0] - TAIL
    chunks, group = size // x_ref.shape[2], size // BLOCK
    pads = (q_pad, k_pad, v_pad)

    def step(i, members):
        for member, pad in enumerate(pads):
            fill(pad, x_ref[pl.ds(i * chunks, chunks), member])
        for j in members:
            queries, keys, values = (conv(pad, w_ref[m], j * BLOCK) for m, pad in enumerate(pads))
            feats_t = relu16(dot_nt(map_t_ref[...], keys))
            feats = relu16(dot(queries, map_ref[...]))
            block = i * group + j
            feat_ref[block] = feats
            carried = folded(dot(feats, high_low(state[...])))
            part_ref[block] = dot(causal_scores(feats, feats_t), values) + carried
            state[...] += dot(feats_t, values)

    state[...] = jnp.zeros_like(state)
    for pad in pads:
        pad[:TAIL] = jnp.zeros((TAIL, DH), jnp.float32)
    step(0, range(1, group))

    def later(i, carry):
        for pad in pads:
            pad[:TAIL] = pad[size:]
        step(i, range(group))
        return carry

    lax.fori_loop(1, blocks // group, later, 0)


def finish_kernel(
    x_ref, came_ref, w_ref, map_ref, map_t_ref, part_ref, feat_ref, gain_ref, *refs
):
    *others, out_ref, q_pad, k_pad, v_pad = refs
    blocks, _, features = feat_ref.shape
    per_block = BLOCK // out_ref.shape[2]
    gain = gain_ref[...]
    for place, other in enumerate(others):
        out_ref[:, place] = other[:, 0]

    def put(begin, end, numerator):
        scale = lax.rsqrt(jnp.mean(numerator * numerator, -1, keepdims=True) + 1e-06)
        normed = (numerator * scale * gain).astype(jnp.bfloat16)
        held = slice(begin * per_block, end * per_block)
        extent = (end - begin) * per_block
        out_ref[held, len(others)] = normed.reshape(extent, BLOCK // per_block, DH)

    follows = lax.axis_index("span") > 0
    state = jnp.where(follows, came_ref[:features], jnp.zeros((features, DH), jnp.bfloat16))
    pads = (q_pad, k_pad, v_pad)
    for member, pad in enumerate(pads):
        end = features + (member + 1) * RIM
        pad[:TAIL] = jnp.where(follows, came_ref[end - TAIL : end].astype(jnp.float32), 0.0)
        fill(pad, x_ref[: (pad.shape[0] - TAIL) // x_ref.shape[2], member])
    queries, keys, values = (conv(pad, w_ref[member], 0) for member, pad in enumerate(pads))
    feats_t = relu16(dot_nt(map_t_ref[...], keys))
    feats = relu16(dot(queries, map_ref[...]))
    later = high_low(state.astype(jnp.float32) + dot(feats_t, values))
    put(0, 1, dot(causal_scores(feats, feats_t), values) + dot(feats, state))
    for begin in range(1, blocks, 2):
        end = min(begin + 2, blocks)
        extent = (end - begin) * BLOCK
        feats = feat_ref[begin:end].reshape(extent, features)
        put(begin, end, part_ref[begin:end].reshape(extent, DH) + folded(dot(feats, later)))


LIMIT = 24 * 1024 * 1024
MOST = 60 * 1024 * 1024
VMEM = pl.BlockSpec(memory_space=pltpu.VMEM)
HBM = pl.BlockSpec(memory_space=pltpu.HBM)


COST = pl.CostEstimate(flops=1000, bytes_accessed=1000, transcendentals=0)
GRID = pltpu.CompilerParams(dimension_semantics=("arbitrary",), vmem_limit_bytes=LIMIT)


def whole_call(kernel, inputs, outputs, scratch=(), read=VMEM, written=VMEM, limit=LIMIT):
    return pl.pallas_call(
        kernel,
        in_specs=[read] * len(inputs),
        out_specs=[written] * len(outputs),
        out_shape=outputs,
        scratch_shapes=scratch,
        compiler_params=pltpu.CompilerParams(vmem_limit_bytes=limit),
        cost_estimate=COST,
    )(*inputs)


def stepped(kernel, steps, inputs, specs, out_specs, outputs, scratch):
    return pl.pallas_call(
        kernel,
        grid=(steps,),
        in_specs=specs,
        out_specs=out_specs,
        out_shape=outputs,
        scratch_shapes=scratch,
        compiler_params=GRID,
        cost_estimate=COST,
    )(*inputs)


def whole(array):
    zeros = (0,) * array.ndim
    return pl.BlockSpec(array.shape, lambda i: zeros)


def shaped(shape, dtype=jnp.bfloat16):
    return jax.ShapeDtypeStruct(shape, dtype)


def next_span(block, spans):
    return lax.ppermute(block, "span", [(i, i + 1) for i in range(spans - 1)])


def exchange(block):
    return lax.all_to_all(block, GROUP, split_axis=0, concat_axis=0, tiled=True)


def after(value, other):
    return lax.optimization_barrier((value, other))[0]


def local(spans, query_input, key_input, value_heads_input, conv_weight, feature_map, out_gain):
    rows, model = query_input.shape
    parts, members = lax.axis_size("part"), lax.axis_size("sp")
    count = parts * members
    width = model // count
    heads, tokens, features = width // DH, count * rows, feature_map.shape[1]
    blocks = tokens // BLOCK
    starts = [
        [((d % members) * parts + d // members) * width + head * DH for d in range(count)]
        for head in range(heads)
    ]
    column = lax.axis_index("part") * width
    weights = lax.dynamic_slice_in_dim(conv_weight, column, width, 2)
    gains = lax.dynamic_slice_in_dim(out_gain, column, width, 0)[None]
    map_t = feature_map.T

    inputs = [query_input, key_input, value_heads_input]
    size = BLOCK * (2 if blocks % 2 == 0 else 1)
    narrow = pltpu.VMEM((TAIL + BLOCK, DH), jnp.float32)
    whole_state = pltpu.VMEM((features, DH), jnp.float32)
    chunks = size // rows
    xs, sents, spans_done = [], [], []
    for head in range(heads):
        taps = weights[:, :, head * DH : (head + 1) * DH]
        packed = shaped((count, 3, rows, DH))
        if head == 0:
            (x,) = whole_call(
                functools.partial(pack_kernel, starts[head]),
                inputs,
                [packed],
                [
                    pltpu.VMEM((3, rows, model), jnp.bfloat16),
                    pltpu.VMEM(packed.shape, packed.dtype),
                    pltpu.SemaphoreType.DMA((3, 4)),
                    pltpu.SemaphoreType.DMA((count,)),
                ],
                read=HBM, written=HBM, limit=MOST,
            )
        else:
            (x,) = whole_call(functools.partial(pack_whole_kernel, starts[head]), inputs, [packed])
        x = exchange(x)
        if spans_done:
            x = after(x, spans_done[-1][1])
        halo = jnp.zeros((3, RIM, DH), jnp.bfloat16)
        if spans > 2:
            halo = next_span(x[count - 1, :, rows - RIM :], spans)
        big = chunks * (2 if count % (2 * chunks) == 0 else 1)
        tall = pltpu.VMEM((TAIL + big * rows, DH), jnp.float32)
        sent = stepped(
            totals_kernel,
            count // big,
            [x, x, x, halo, taps, map_t],
            [
                pl.BlockSpec((big, 1, rows, DH), lambda i: (i, 1, 0, 0)),
                pl.BlockSpec((big, 1, rows, DH), lambda i: (i, 2, 0, 0)),
                pl.BlockSpec((1, 3, rows, DH), lambda i: (count - 1, 0, 0, 0)),
                whole(halo), whole(taps), whole(map_t),
            ],
            pl.BlockSpec((features + 3 * RIM, DH), lambda i: (0, 0)),
            shaped((features + 3 * RIM, DH)),
            [tall, tall, whole_state],
        )
        done = whole_call(
            span_kernel,
            [x, taps, feature_map, map_t],
            [
                shaped((blocks, BLOCK, DH), jnp.float32),
                shaped((blocks, BLOCK, features)),
            ],
            [tall, tall, tall, whole_state],
        )
        if head < heads - 1:
            sent = after(sent, done[0])
        if spans == 2:
            both = head == heads - 1
            came = lax.ppermute(sent, "span", [(0, 1), (1, 0)] if both else [(0, 1)])
        else:
            gathered = lax.all_gather(sent[:features], "span").astype(jnp.float32)
            mine = lax.axis_index("span")
            earlier = jnp.where((jnp.arange(spans) < mine)[:, None, None], gathered, 0.0)
            state = jnp.sum(earlier, 0).astype(jnp.bfloat16)
            came = jnp.concatenate([state, halo.reshape(3 * RIM, DH)])
        xs.append((x, came, taps))
        sents.append(sent)
        spans_done.append(done)

    attended = []
    for head in range(heads):
        x, came, taps = xs[head]
        partial, feats = spans_done[head]
        gain = gains[:, head * DH : (head + 1) * DH]
        if head < heads - 1:
            gain = after(gain, sents[-1])
        others = attended if head == heads - 1 else []
        piece = shaped((count, len(others) + 1, rows, DH))
        (out,) = whole_call(
            finish_kernel,
            [x, came, taps, feature_map, map_t, partial, feats, gain, *others],
            [piece],
            [narrow, narrow, narrow],
        )
        attended.append(out)
    landed = exchange(attended[-1]).reshape(parts, members, heads, rows, DH)
    (result,) = whole_call(unpack_kernel, [landed], [shaped((rows, model))])
    return result


def solution(mesh):
    groups, members = mesh.devices.shape
    parts = 1
    while groups % (4 * parts) == 0 and H % (2 * parts * members) == 0:
        parts *= 2
    spans = groups // parts
    split = Mesh(mesh.devices.reshape(spans, parts, members), ("span", "part", "sp"))
    tokens = P(("span", "part", "sp"), None)
    placed = (tokens, tokens, tokens, P(None, None, "sp"), P(), P("sp"))
    return jax.shard_map(
        functools.partial(local, spans),
        mesh=split, in_specs=placed, out_specs=tokens, check_vma=False,
    )
```

```python
import functools

import jax
import jax.numpy as jnp
from jax import lax
from jax.experimental import pallas as pl
from jax.experimental.pallas import tpu as pltpu
from jax.sharding import Mesh
from jax.sharding import PartitionSpec as P

H = 32
DH = 128
BLOCK = 256
TAIL = 8
RIM = 16
GROUP = ("part", "sp")


def dot(a, b):
    return jnp.dot(a, b, preferred_element_type=jnp.float32)


def dot_nt(a, b):
    return lax.dot_general(a, b, (((1,), (1,)), ((), ())), preferred_element_type=jnp.float32)


def conv(pad_ref, weights, begin, count=BLOCK):
    total = jnp.zeros((count, pad_ref.shape[1]), jnp.float32)
    for tap in range(weights.shape[0]):
        row = TAIL + begin - tap
        total = total + weights[tap][None, :] * pad_ref[row : row + count]
    return total.astype(jnp.bfloat16)


def relu16(x):
    return jnp.maximum(x.astype(jnp.bfloat16), 0)


def pack_kernel(starts, *refs):
    *sources, out_ref, held, packed, load_sems, store_sems = refs
    pieces = load_sems.shape[1]
    width = held.shape[-1] // pieces
    loads = {}
    for piece in range(pieces):
        for member, source in enumerate(sources):
            cols = pl.ds(piece * width, width)
            loads[piece, member] = pltpu.make_async_copy(
                source.at[:, cols], held.at[member, :, cols], load_sems.at[member, piece]
            )
            loads[piece, member].start()
    stores = []
    for piece in range(pieces):
        owners = [owner for owner, start in enumerate(starts) if start // width == piece]
        for member in range(len(sources)):
            loads[piece, member].wait()
            for owner in owners:
                start = starts[owner]
                packed[owner, member] = held[member, :, start : start + DH]
        for owner in owners:
            stores.append(
                pltpu.make_async_copy(packed.at[owner], out_ref.at[owner], store_sems.at[owner])
            )
            stores[-1].start()
    for store in stores:
        store.wait()


def pack_whole_kernel(starts, *refs):
    *sources, out_ref = refs
    for member, source in enumerate(sources):
        for owner, start in enumerate(starts):
            out_ref[owner, member] = source[:, start : start + DH]


def unpack_kernel(x_ref, out_ref):
    parts, members, heads, _, _ = x_ref.shape
    for member in range(members):
        for part in range(parts):
            for head in range(heads):
                start = ((member * parts + part) * heads + head) * DH
                out_ref[:, start : start + DH] = x_ref[part, member, head]


def high_low(x):
    high = x.astype(jnp.bfloat16)
    return jnp.concatenate([high, (x - high.astype(jnp.float32)).astype(jnp.bfloat16)], 1)


def folded(x):
    return x[:, :DH] + x[:, DH:]


def fill(pad_ref, held):
    count = pad_ref.shape[0] - TAIL
    pad_ref[TAIL:] = held.reshape(count, DH).astype(jnp.float32)


def carry_tail(pads, first, halo):
    for member, pad in enumerate(pads):
        count = pad.shape[0] - TAIL

        @pl.when(first)
        def _(pad=pad, member=member):
            pad[:TAIL] = halo(member)

        @pl.when(jnp.logical_not(first))
        def _(pad=pad, count=count):
            pad[:TAIL] = pad[count:]


def totals_kernel(k_ref, v_ref, rim_ref, halo_ref, w_ref, map_t_ref, sent_ref, k_pad, v_pad, state):
    rows, features = k_ref.shape[2], map_t_ref.shape[0]
    size = k_pad.shape[0] - TAIL
    first = pl.program_id(0) == 0
    carry_tail(
        (k_pad, v_pad), first,
        lambda member: halo_ref[member + 1, RIM - TAIL :].astype(jnp.float32),
    )
    fill(k_pad, k_ref[...])
    fill(v_pad, v_ref[...])

    @pl.when(first)
    def _():
        state[...] = jnp.zeros_like(state)

    extent = 2 * BLOCK if size % (2 * BLOCK) == 0 else BLOCK
    for begin in range(0, size, extent):
        keys = conv(k_pad, w_ref[1], begin, extent)
        values = conv(v_pad, w_ref[2], begin, extent)
        state[...] += dot(relu16(dot_nt(map_t_ref[...], keys)), values)

    @pl.when(pl.program_id(0) == pl.num_programs(0) - 1)
    def _():
        sent_ref[:features] = state[...].astype(jnp.bfloat16)
        for member in range(3):
            held = slice(features + member * RIM, features + (member + 1) * RIM)
            sent_ref[held] = rim_ref[0, member, rows - RIM :]


def causal_scores(feats, feats_t):
    row = lax.broadcasted_iota(jnp.int32, (BLOCK, BLOCK), 0)
    col = lax.broadcasted_iota(jnp.int32, (BLOCK, BLOCK), 1)
    return jnp.where(col <= row, dot(feats, feats_t), 0.0).astype(jnp.bfloat16)


def span_kernel(x_ref, w_ref, map_ref, map_t_ref, part_ref, feat_ref, q_pad, k_pad, v_pad, state):
    blocks, size = part_ref.shape[0], q_pad.shape[0] - TAIL
    chunks, group = size // x_ref.shape[2], size // BLOCK
    pads = (q_pad, k_pad, v_pad)

    def step(i, members):
        for member, pad in enumerate(pads):
            fill(pad, x_ref[pl.ds(i * chunks, chunks), member])
        for j in members:
            queries, keys, values = (conv(pad, w_ref[m], j * BLOCK) for m, pad in enumerate(pads))
            feats_t = relu16(dot_nt(map_t_ref[...], keys))
            feats = relu16(dot(queries, map_ref[...]))
            block = i * group + j
            feat_ref[block] = feats
            carried = folded(dot(feats, high_low(state[...])))
            part_ref[block] = dot(causal_scores(feats, feats_t), values) + carried
            state[...] += dot(feats_t, values)

    state[...] = jnp.zeros_like(state)
    for pad in pads:
        pad[:TAIL] = jnp.zeros((TAIL, DH), jnp.float32)
    step(0, range(1, group))

    def later(i, carry):
        for pad in pads:
            pad[:TAIL] = pad[size:]
        step(i, range(group))
        return carry

    lax.fori_loop(1, blocks // group, later, 0)


def finish_kernel(
    x_ref, came_ref, w_ref, map_ref, map_t_ref, part_ref, feat_ref, gain_ref, *refs
):
    *others, out_ref, q_pad, k_pad, v_pad = refs
    blocks, _, features = feat_ref.shape
    per_block = BLOCK // out_ref.shape[2]
    gain = gain_ref[...]
    for place, other in enumerate(others):
        out_ref[:, place] = other[:, 0]

    def put(begin, end, numerator):
        scale = lax.rsqrt(jnp.mean(numerator * numerator, -1, keepdims=True) + 1e-06)
        normed = (numerator * scale * gain).astype(jnp.bfloat16)
        held = slice(begin * per_block, end * per_block)
        extent = (end - begin) * per_block
        out_ref[held, len(others)] = normed.reshape(extent, BLOCK // per_block, DH)

    follows = lax.axis_index("span") > 0
    state = jnp.where(follows, came_ref[:features], jnp.zeros((features, DH), jnp.bfloat16))
    pads = (q_pad, k_pad, v_pad)
    for member, pad in enumerate(pads):
        end = features + (member + 1) * RIM
        pad[:TAIL] = jnp.where(follows, came_ref[end - TAIL : end].astype(jnp.float32), 0.0)
        fill(pad, x_ref[: (pad.shape[0] - TAIL) // x_ref.shape[2], member])
    queries, keys, values = (conv(pad, w_ref[member], 0) for member, pad in enumerate(pads))
    feats_t = relu16(dot_nt(map_t_ref[...], keys))
    feats = relu16(dot(queries, map_ref[...]))
    later = high_low(state.astype(jnp.float32) + dot(feats_t, values))
    put(0, 1, dot(causal_scores(feats, feats_t), values) + dot(feats, state))
    for begin in range(1, blocks, 2):
        end = min(begin + 2, blocks)
        extent = (end - begin) * BLOCK
        feats = feat_ref[begin:end].reshape(extent, features)
        put(begin, end, part_ref[begin:end].reshape(extent, DH) + folded(dot(feats, later)))


LIMIT = 24 * 1024 * 1024
MOST = 60 * 1024 * 1024
VMEM = pl.BlockSpec(memory_space=pltpu.VMEM)
HBM = pl.BlockSpec(memory_space=pltpu.HBM)


COST = pl.CostEstimate(flops=1000, bytes_accessed=1000, transcendentals=0)
GRID = pltpu.CompilerParams(dimension_semantics=("arbitrary",), vmem_limit_bytes=LIMIT)


def whole_call(kernel, inputs, outputs, scratch=(), read=VMEM, written=VMEM, limit=LIMIT):
    return pl.pallas_call(
        kernel,
        in_specs=[read] * len(inputs),
        out_specs=[written] * len(outputs),
        out_shape=outputs,
        scratch_shapes=scratch,
        compiler_params=pltpu.CompilerParams(vmem_limit_bytes=limit),
        cost_estimate=COST,
    )(*inputs)


def stepped(kernel, steps, inputs, specs, out_specs, outputs, scratch):
    return pl.pallas_call(
        kernel,
        grid=(steps,),
        in_specs=specs,
        out_specs=out_specs,
        out_shape=outputs,
        scratch_shapes=scratch,
        compiler_params=GRID,
        cost_estimate=COST,
    )(*inputs)


def whole(array):
    zeros = (0,) * array.ndim
    return pl.BlockSpec(array.shape, lambda i: zeros)


def shaped(shape, dtype=jnp.bfloat16):
    return jax.ShapeDtypeStruct(shape, dtype)


def next_span(block, spans):
    return lax.ppermute(block, "span", [(i, i + 1) for i in range(spans - 1)])


def exchange(block):
    return lax.all_to_all(block, GROUP, split_axis=0, concat_axis=0, tiled=True)


def after(value, other):
    return lax.optimization_barrier((value, other))[0]


def local(spans, query_input, key_input, value_heads_input, conv_weight, feature_map, out_gain):
    rows, model = query_input.shape
    parts, members = lax.axis_size("part"), lax.axis_size("sp")
    count = parts * members
    width = model // count
    heads, tokens, features = width // DH, count * rows, feature_map.shape[1]
    blocks = tokens // BLOCK
    starts = [
        [((d % members) * parts + d // members) * width + head * DH for d in range(count)]
        for head in range(heads)
    ]
    column = lax.axis_index("part") * width
    weights = lax.dynamic_slice_in_dim(conv_weight, column, width, 2)
    gains = lax.dynamic_slice_in_dim(out_gain, column, width, 0)[None]
    map_t = feature_map.T

    inputs = [query_input, key_input, value_heads_input]
    size = BLOCK * (2 if blocks % 2 == 0 else 1)
    narrow = pltpu.VMEM((TAIL + BLOCK, DH), jnp.float32)
    whole_state = pltpu.VMEM((features, DH), jnp.float32)
    chunks = size // rows
    xs, sents, spans_done = [], [], []
    for head in range(heads):
        taps = weights[:, :, head * DH : (head + 1) * DH]
        packed = shaped((count, 3, rows, DH))
        if head == 0:
            (x,) = whole_call(
                functools.partial(pack_kernel, starts[head]),
                inputs,
                [packed],
                [
                    pltpu.VMEM((3, rows, model), jnp.bfloat16),
                    pltpu.VMEM(packed.shape, packed.dtype),
                    pltpu.SemaphoreType.DMA((3, 4)),
                    pltpu.SemaphoreType.DMA((count,)),
                ],
                read=HBM, written=HBM, limit=MOST,
            )
        else:
            (x,) = whole_call(functools.partial(pack_whole_kernel, starts[head]), inputs, [packed])
        x = exchange(x)
        if spans_done:
            x = after(x, spans_done[-1][1])
        halo = jnp.zeros((3, RIM, DH), jnp.bfloat16)
        if spans > 2:
            halo = next_span(x[count - 1, :, rows - RIM :], spans)
        big = chunks * (2 if count % (2 * chunks) == 0 else 1)
        tall = pltpu.VMEM((TAIL + big * rows, DH), jnp.float32)
        sent = stepped(
            totals_kernel,
            count // big,
            [x, x, x, halo, taps, map_t],
            [
                pl.BlockSpec((big, 1, rows, DH), lambda i: (i, 1, 0, 0)),
                pl.BlockSpec((big, 1, rows, DH), lambda i: (i, 2, 0, 0)),
                pl.BlockSpec((1, 3, rows, DH), lambda i: (count - 1, 0, 0, 0)),
                whole(halo), whole(taps), whole(map_t),
            ],
            pl.BlockSpec((features + 3 * RIM, DH), lambda i: (0, 0)),
            shaped((features + 3 * RIM, DH)),
            [tall, tall, whole_state],
        )
        if spans == 2:
            both = head == heads - 1
            came = lax.ppermute(sent, "span", [(0, 1), (1, 0)] if both else [(0, 1)])
        else:
            gathered = lax.all_gather(sent[:features], "span").astype(jnp.float32)
            mine = lax.axis_index("span")
            earlier = jnp.where((jnp.arange(spans) < mine)[:, None, None], gathered, 0.0)
            state = jnp.sum(earlier, 0).astype(jnp.bfloat16)
            came = jnp.concatenate([state, halo.reshape(3 * RIM, DH)])
        done = whole_call(
            span_kernel,
            [x, taps, feature_map, map_t],
            [
                shaped((blocks, BLOCK, DH), jnp.float32),
                shaped((blocks, BLOCK, features)),
            ],
            [tall, tall, tall, whole_state],
        )
        xs.append((x, came, taps))
        sents.append(sent)
        spans_done.append(done)

    attended = []
    for head in range(heads):
        x, came, taps = xs[head]
        partial, feats = spans_done[head]
        gain = gains[:, head * DH : (head + 1) * DH]
        if head < heads - 1:
            gain = after(gain, sents[-1])
        others = attended if head == heads - 1 else []
        piece = shaped((count, len(others) + 1, rows, DH))
        (out,) = whole_call(
            finish_kernel,
            [x, came, taps, feature_map, map_t, partial, feats, gain, *others],
            [piece],
            [narrow, narrow, narrow],
        )
        attended.append(out)
    landed = exchange(attended[-1]).reshape(parts, members, heads, rows, DH)
    (result,) = whole_call(unpack_kernel, [landed], [shaped((rows, model))])
    return result


def solution(mesh):
    groups, members = mesh.devices.shape
    parts = 1
    while groups % (4 * parts) == 0 and H % (2 * parts * members) == 0:
        parts *= 2
    spans = groups // parts
    split = Mesh(mesh.devices.reshape(spans, parts, members), ("span", "part", "sp"))
    tokens = P(("span", "part", "sp"), None)
    placed = (tokens, tokens, tokens, P(None, None, "sp"), P(), P("sp"))
    return jax.shard_map(
        functools.partial(local, spans),
        mesh=split, in_specs=placed, out_specs=tokens, check_vma=False,
    )
```

```python
import functools

import jax
import jax.numpy as jnp
from jax import lax
from jax.experimental import pallas as pl
from jax.experimental.pallas import tpu as pltpu
from jax.sharding import Mesh
from jax.sharding import PartitionSpec as P

H = 32
DH = 128
BLOCK = 256
TAIL = 8
RIM = 16
GROUP = ("part", "sp")


def dot(a, b):
    return jnp.dot(a, b, preferred_element_type=jnp.float32)


def dot_nt(a, b):
    return lax.dot_general(a, b, (((1,), (1,)), ((), ())), preferred_element_type=jnp.float32)


def conv(pad_ref, weights, begin, count=BLOCK):
    total = jnp.zeros((count, pad_ref.shape[1]), jnp.float32)
    for tap in range(weights.shape[0]):
        row = TAIL + begin - tap
        total = total + weights[tap][None, :] * pad_ref[row : row + count]
    return total.astype(jnp.bfloat16)


def relu16(x):
    return jnp.maximum(x.astype(jnp.bfloat16), 0)


def pack_kernel(starts, *refs):
    *sources, out_ref, held, packed, load_sems, store_sems = refs
    pieces = load_sems.shape[1]
    extent = held.shape[1] // pieces
    loads = {}
    for piece in range(pieces):
        rows = pl.ds(piece * extent, extent)
        for member, source in enumerate(sources):
            loads[piece, member] = pltpu.make_async_copy(
                source.at[rows], held.at[member, rows], load_sems.at[member, piece]
            )
            loads[piece, member].start()
    stores = []
    for piece in range(pieces):
        rows = pl.ds(piece * extent, extent)
        for member in range(len(sources)):
            loads[piece, member].wait()
            for owner, start in enumerate(starts):
                packed[owner, member, rows] = held[member, rows, start : start + DH]
        stores.append(
            pltpu.make_async_copy(
                packed.at[:, :, rows], out_ref.at[:, :, rows], store_sems.at[piece]
            )
        )
        stores[-1].start()
    for store in stores:
        store.wait()


def pack_whole_kernel(starts, *refs):
    *sources, out_ref = refs
    for member, source in enumerate(sources):
        for owner, start in enumerate(starts):
            out_ref[owner, member] = source[:, start : start + DH]


def unpack_kernel(x_ref, out_ref):
    parts, members, heads, _, _ = x_ref.shape
    for member in range(members):
        for part in range(parts):
            for head in range(heads):
                start = ((member * parts + part) * heads + head) * DH
                out_ref[:, start : start + DH] = x_ref[part, member, head]


def high_low(x):
    high = x.astype(jnp.bfloat16)
    return jnp.concatenate([high, (x - high.astype(jnp.float32)).astype(jnp.bfloat16)], 1)


def folded(x):
    return x[:, :DH] + x[:, DH:]


def fill(pad_ref, held):
    count = pad_ref.shape[0] - TAIL
    pad_ref[TAIL:] = held.reshape(count, DH).astype(jnp.float32)


def carry_tail(pads, first, halo):
    for member, pad in enumerate(pads):
        count = pad.shape[0] - TAIL

        @pl.when(first)
        def _(pad=pad, member=member):
            pad[:TAIL] = halo(member)

        @pl.when(jnp.logical_not(first))
        def _(pad=pad, count=count):
            pad[:TAIL] = pad[count:]


def totals_kernel(k_ref, v_ref, rim_ref, halo_ref, w_ref, map_t_ref, sent_ref, k_pad, v_pad, state):
    rows, features = k_ref.shape[2], map_t_ref.shape[0]
    size = k_pad.shape[0] - TAIL
    first = pl.program_id(0) == 0
    carry_tail(
        (k_pad, v_pad), first,
        lambda member: halo_ref[member + 1, RIM - TAIL :].astype(jnp.float32),
    )
    fill(k_pad, k_ref[...])
    fill(v_pad, v_ref[...])

    @pl.when(first)
    def _():
        state[...] = jnp.zeros_like(state)

    extent = 2 * BLOCK if size % (2 * BLOCK) == 0 else BLOCK
    for begin in range(0, size, extent):
        keys = conv(k_pad, w_ref[1], begin, extent)
        values = conv(v_pad, w_ref[2], begin, extent)
        state[...] += dot(relu16(dot_nt(map_t_ref[...], keys)), values)

    @pl.when(pl.program_id(0) == pl.num_programs(0) - 1)
    def _():
        sent_ref[:features] = state[...].astype(jnp.bfloat16)
        for member in range(3):
            held = slice(features + member * RIM, features + (member + 1) * RIM)
            sent_ref[held] = rim_ref[0, member, rows - RIM :]


def causal_scores(feats, feats_t):
    row = lax.broadcasted_iota(jnp.int32, (BLOCK, BLOCK), 0)
    col = lax.broadcasted_iota(jnp.int32, (BLOCK, BLOCK), 1)
    return jnp.where(col <= row, dot(feats, feats_t), 0.0).astype(jnp.bfloat16)


def span_kernel(x_ref, w_ref, map_ref, map_t_ref, part_ref, feat_ref, q_pad, k_pad, v_pad, state):
    blocks, size = part_ref.shape[0], q_pad.shape[0] - TAIL
    chunks, group = size // x_ref.shape[2], size // BLOCK
    pads = (q_pad, k_pad, v_pad)

    def step(i, members):
        for member, pad in enumerate(pads):
            fill(pad, x_ref[pl.ds(i * chunks, chunks), member])
        for j in members:
            queries, keys, values = (conv(pad, w_ref[m], j * BLOCK) for m, pad in enumerate(pads))
            feats_t = relu16(dot_nt(map_t_ref[...], keys))
            feats = relu16(dot(queries, map_ref[...]))
            block = i * group + j
            feat_ref[block] = feats
            carried = folded(dot(feats, high_low(state[...])))
            part_ref[block] = dot(causal_scores(feats, feats_t), values) + carried
            state[...] += dot(feats_t, values)

    state[...] = jnp.zeros_like(state)
    for pad in pads:
        pad[:TAIL] = jnp.zeros((TAIL, DH), jnp.float32)
    step(0, range(1, group))

    def later(i, carry):
        for pad in pads:
            pad[:TAIL] = pad[size:]
        step(i, range(group))
        return carry

    lax.fori_loop(1, blocks // group, later, 0)


def finish_kernel(
    x_ref, came_ref, w_ref, map_ref, map_t_ref, part_ref, feat_ref, gain_ref, *refs
):
    *others, out_ref, q_pad, k_pad, v_pad = refs
    blocks, _, features = feat_ref.shape
    per_block = BLOCK // out_ref.shape[2]
    gain = gain_ref[...]
    for place, other in enumerate(others):
        out_ref[:, place] = other[:, 0]

    def put(begin, end, numerator):
        scale = lax.rsqrt(jnp.mean(numerator * numerator, -1, keepdims=True) + 1e-06)
        normed = (numerator * scale * gain).astype(jnp.bfloat16)
        held = slice(begin * per_block, end * per_block)
        extent = (end - begin) * per_block
        out_ref[held, len(others)] = normed.reshape(extent, BLOCK // per_block, DH)

    follows = lax.axis_index("span") > 0
    state = jnp.where(follows, came_ref[:features], jnp.zeros((features, DH), jnp.bfloat16))
    pads = (q_pad, k_pad, v_pad)
    for member, pad in enumerate(pads):
        end = features + (member + 1) * RIM
        pad[:TAIL] = jnp.where(follows, came_ref[end - TAIL : end].astype(jnp.float32), 0.0)
        fill(pad, x_ref[: (pad.shape[0] - TAIL) // x_ref.shape[2], member])
    queries, keys, values = (conv(pad, w_ref[member], 0) for member, pad in enumerate(pads))
    feats_t = relu16(dot_nt(map_t_ref[...], keys))
    feats = relu16(dot(queries, map_ref[...]))
    later = high_low(state.astype(jnp.float32) + dot(feats_t, values))
    put(0, 1, dot(causal_scores(feats, feats_t), values) + dot(feats, state))
    for begin in range(1, blocks, 2):
        end = min(begin + 2, blocks)
        extent = (end - begin) * BLOCK
        feats = feat_ref[begin:end].reshape(extent, features)
        put(begin, end, part_ref[begin:end].reshape(extent, DH) + folded(dot(feats, later)))


LIMIT = 24 * 1024 * 1024
MOST = 60 * 1024 * 1024
VMEM = pl.BlockSpec(memory_space=pltpu.VMEM)
HBM = pl.BlockSpec(memory_space=pltpu.HBM)


COST = pl.CostEstimate(flops=1000, bytes_accessed=1000, transcendentals=0)
GRID = pltpu.CompilerParams(dimension_semantics=("arbitrary",), vmem_limit_bytes=LIMIT)


def whole_call(kernel, inputs, outputs, scratch=(), read=VMEM, written=VMEM, limit=LIMIT):
    return pl.pallas_call(
        kernel,
        in_specs=[read] * len(inputs),
        out_specs=[written] * len(outputs),
        out_shape=outputs,
        scratch_shapes=scratch,
        compiler_params=pltpu.CompilerParams(vmem_limit_bytes=limit),
        cost_estimate=COST,
    )(*inputs)


def stepped(kernel, steps, inputs, specs, out_specs, outputs, scratch):
    return pl.pallas_call(
        kernel,
        grid=(steps,),
        in_specs=specs,
        out_specs=out_specs,
        out_shape=outputs,
        scratch_shapes=scratch,
        compiler_params=GRID,
        cost_estimate=COST,
    )(*inputs)


def whole(array):
    zeros = (0,) * array.ndim
    return pl.BlockSpec(array.shape, lambda i: zeros)


def shaped(shape, dtype=jnp.bfloat16):
    return jax.ShapeDtypeStruct(shape, dtype)


def next_span(block, spans):
    return lax.ppermute(block, "span", [(i, i + 1) for i in range(spans - 1)])


def exchange(block):
    return lax.all_to_all(block, GROUP, split_axis=0, concat_axis=0, tiled=True)


def after(value, other):
    return lax.optimization_barrier((value, other))[0]


def local(spans, query_input, key_input, value_heads_input, conv_weight, feature_map, out_gain):
    rows, model = query_input.shape
    parts, members = lax.axis_size("part"), lax.axis_size("sp")
    count = parts * members
    width = model // count
    heads, tokens, features = width // DH, count * rows, feature_map.shape[1]
    blocks = tokens // BLOCK
    starts = [
        [((d % members) * parts + d // members) * width + head * DH for d in range(count)]
        for head in range(heads)
    ]
    column = lax.axis_index("part") * width
    weights = lax.dynamic_slice_in_dim(conv_weight, column, width, 2)
    gains = lax.dynamic_slice_in_dim(out_gain, column, width, 0)[None]
    map_t = feature_map.T

    inputs = [query_input, key_input, value_heads_input]
    size = BLOCK * (2 if blocks % 2 == 0 else 1)
    narrow = pltpu.VMEM((TAIL + BLOCK, DH), jnp.float32)
    whole_state = pltpu.VMEM((features, DH), jnp.float32)
    chunks = size // rows
    xs, sents, spans_done = [], [], []
    for head in range(heads):
        taps = weights[:, :, head * DH : (head + 1) * DH]
        packed = shaped((count, 3, rows, DH))
        if head == 0:
            (x,) = whole_call(
                functools.partial(pack_kernel, starts[head]),
                inputs,
                [packed],
                [
                    pltpu.VMEM((3, rows, model), jnp.bfloat16),
                    pltpu.VMEM(packed.shape, packed.dtype),
                    pltpu.SemaphoreType.DMA((3, 4)),
                    pltpu.SemaphoreType.DMA((4,)),
                ],
                read=HBM, written=HBM, limit=MOST,
            )
        else:
            (x,) = whole_call(functools.partial(pack_whole_kernel, starts[head]), inputs, [packed])
        x = exchange(x)
        if spans_done:
            x = after(x, spans_done[-1][1])
        halo = jnp.zeros((3, RIM, DH), jnp.bfloat16)
        if spans > 2:
            halo = next_span(x[count - 1, :, rows - RIM :], spans)
        big = chunks * (2 if count % (2 * chunks) == 0 else 1)
        tall = pltpu.VMEM((TAIL + big * rows, DH), jnp.float32)
        sent = stepped(
            totals_kernel,
            count // big,
            [x, x, x, halo, taps, map_t],
            [
                pl.BlockSpec((big, 1, rows, DH), lambda i: (i, 1, 0, 0)),
                pl.BlockSpec((big, 1, rows, DH), lambda i: (i, 2, 0, 0)),
                pl.BlockSpec((1, 3, rows, DH), lambda i: (count - 1, 0, 0, 0)),
                whole(halo), whole(taps), whole(map_t),
            ],
            pl.BlockSpec((features + 3 * RIM, DH), lambda i: (0, 0)),
            shaped((features + 3 * RIM, DH)),
            [tall, tall, whole_state],
        )
        if spans == 2:
            both = head == heads - 1
            came = lax.ppermute(sent, "span", [(0, 1), (1, 0)] if both else [(0, 1)])
        else:
            gathered = lax.all_gather(sent[:features], "span").astype(jnp.float32)
            mine = lax.axis_index("span")
            earlier = jnp.where((jnp.arange(spans) < mine)[:, None, None], gathered, 0.0)
            state = jnp.sum(earlier, 0).astype(jnp.bfloat16)
            came = jnp.concatenate([state, halo.reshape(3 * RIM, DH)])
        done = whole_call(
            span_kernel,
            [x, taps, feature_map, map_t],
            [
                shaped((blocks, BLOCK, DH), jnp.float32),
                shaped((blocks, BLOCK, features)),
            ],
            [tall, tall, tall, whole_state],
        )
        xs.append((x, came, taps))
        sents.append(sent)
        spans_done.append(done)

    attended = []
    for head in range(heads):
        x, came, taps = xs[head]
        partial, feats = spans_done[head]
        gain = gains[:, head * DH : (head + 1) * DH]
        if head < heads - 1:
            gain = after(gain, sents[-1])
        others = attended if head == heads - 1 else []
        piece = shaped((count, len(others) + 1, rows, DH))
        (out,) = whole_call(
            finish_kernel,
            [x, came, taps, feature_map, map_t, partial, feats, gain, *others],
            [piece],
            [narrow, narrow, narrow],
        )
        attended.append(out)
    landed = exchange(attended[-1]).reshape(parts, members, heads, rows, DH)
    (result,) = whole_call(unpack_kernel, [landed], [shaped((rows, model))])
    return result


def solution(mesh):
    groups, members = mesh.devices.shape
    parts = 1
    while groups % (4 * parts) == 0 and H % (2 * parts * members) == 0:
        parts *= 2
    spans = groups // parts
    split = Mesh(mesh.devices.reshape(spans, parts, members), ("span", "part", "sp"))
    tokens = P(("span", "part", "sp"), None)
    placed = (tokens, tokens, tokens, P(None, None, "sp"), P(), P("sp"))
    return jax.shard_map(
        functools.partial(local, spans),
        mesh=split, in_specs=placed, out_specs=tokens, check_vma=False,
    )
```

```python
import functools

import jax
import jax.numpy as jnp
from jax import lax
from jax.experimental import pallas as pl
from jax.experimental.pallas import tpu as pltpu
from jax.sharding import Mesh
from jax.sharding import PartitionSpec as P

H = 32
DH = 128
BLOCK = 256
TAIL = 8
RIM = 16
GROUP = ("part", "sp")


def dot(a, b):
    return jnp.dot(a, b, preferred_element_type=jnp.float32)


def dot_nt(a, b):
    return lax.dot_general(a, b, (((1,), (1,)), ((), ())), preferred_element_type=jnp.float32)


def conv(pad_ref, weights, begin, count=BLOCK):
    total = jnp.zeros((count, pad_ref.shape[1]), jnp.float32)
    for tap in range(weights.shape[0]):
        row = TAIL + begin - tap
        total = total + weights[tap][None, :] * pad_ref[row : row + count]
    return total.astype(jnp.bfloat16)


def relu16(x):
    return jnp.maximum(x.astype(jnp.bfloat16), 0)


def pack_kernel(starts, *refs):
    *sources, out_ref, held, packed, load_sems, store_sems = refs
    pieces = load_sems.shape[1]
    extent = held.shape[1] // pieces
    loads = {}
    for piece in range(pieces):
        rows = pl.ds(piece * extent, extent)
        for member, source in enumerate(sources):
            loads[piece, member] = pltpu.make_async_copy(
                source.at[rows], held.at[member, rows], load_sems.at[member, piece]
            )
            loads[piece, member].start()
    stores = []
    for piece in range(pieces):
        rows = pl.ds(piece * extent, extent)
        for member in range(len(sources)):
            loads[piece, member].wait()
            for owner, start in enumerate(starts):
                packed[owner, member, rows] = held[member, rows, start : start + DH]
        stores.append(
            pltpu.make_async_copy(
                packed.at[:, :, rows], out_ref.at[:, :, rows], store_sems.at[piece]
            )
        )
        stores[-1].start()
    for store in stores:
        store.wait()


def pack_whole_kernel(starts, *refs):
    *sources, out_ref = refs
    for member, source in enumerate(sources):
        for owner, start in enumerate(starts):
            out_ref[owner, member] = source[:, start : start + DH]


def unpack_kernel(x_ref, out_ref):
    parts, members, heads, _, _ = x_ref.shape
    for member in range(members):
        for part in range(parts):
            for head in range(heads):
                start = ((member * parts + part) * heads + head) * DH
                out_ref[:, start : start + DH] = x_ref[part, member, head]


def high_low(x):
    high = x.astype(jnp.bfloat16)
    return jnp.concatenate([high, (x - high.astype(jnp.float32)).astype(jnp.bfloat16)], 1)


def folded(x):
    return x[:, :DH] + x[:, DH:]


def fill(pad_ref, held):
    count = pad_ref.shape[0] - TAIL
    pad_ref[TAIL:] = held.reshape(count, DH).astype(jnp.float32)


def carry_tail(pads, first, halo):
    for member, pad in enumerate(pads):
        count = pad.shape[0] - TAIL

        @pl.when(first)
        def _(pad=pad, member=member):
            pad[:TAIL] = halo(member)

        @pl.when(jnp.logical_not(first))
        def _(pad=pad, count=count):
            pad[:TAIL] = pad[count:]


def totals_kernel(k_ref, v_ref, rim_ref, halo_ref, w_ref, map_t_ref, sent_ref, k_pad, v_pad, state):
    rows, features = k_ref.shape[2], map_t_ref.shape[0]
    size = k_pad.shape[0] - TAIL
    first = pl.program_id(0) == 0
    carry_tail(
        (k_pad, v_pad), first,
        lambda member: halo_ref[member + 1, RIM - TAIL :].astype(jnp.float32),
    )
    fill(k_pad, k_ref[...])
    fill(v_pad, v_ref[...])

    @pl.when(first)
    def _():
        state[...] = jnp.zeros_like(state)

    extent = 2 * BLOCK if size % (2 * BLOCK) == 0 else BLOCK
    for begin in range(0, size, extent):
        keys = conv(k_pad, w_ref[1], begin, extent)
        values = conv(v_pad, w_ref[2], begin, extent)
        state[...] += dot(relu16(dot_nt(map_t_ref[...], keys)), values)

    @pl.when(pl.program_id(0) == pl.num_programs(0) - 1)
    def _():
        sent_ref[:features] = state[...].astype(jnp.bfloat16)
        for member in range(3):
            held = slice(features + member * RIM, features + (member + 1) * RIM)
            sent_ref[held] = rim_ref[0, member, rows - RIM :]


def whole_totals_kernel(x_ref, halo_ref, w_ref, map_t_ref, sent_ref, k_pad, v_pad, state):
    count, _, rows, _ = x_ref.shape
    features, size = map_t_ref.shape[0], k_pad.shape[0] - TAIL
    chunks = size // rows
    for member in range(3):
        held = slice(features + member * RIM, features + (member + 1) * RIM)
        sent_ref[held] = x_ref[count - 1, member, rows - RIM :]
    k_pad[:TAIL] = halo_ref[1, RIM - TAIL :].astype(jnp.float32)
    v_pad[:TAIL] = halo_ref[2, RIM - TAIL :].astype(jnp.float32)
    extent = 2 * BLOCK if size % (2 * BLOCK) == 0 else BLOCK

    def step(i):
        fill(k_pad, x_ref[pl.ds(i * chunks, chunks), 1])
        fill(v_pad, x_ref[pl.ds(i * chunks, chunks), 2])
        for begin in range(0, size, extent):
            keys = conv(k_pad, w_ref[1], begin, extent)
            values = conv(v_pad, w_ref[2], begin, extent)
            update = dot(relu16(dot_nt(map_t_ref[...], keys)), values)
            if isinstance(i, int) and begin == 0:
                state[...] = update
            else:
                state[...] += update

    step(0)

    def later(i, carry):
        for pad in (k_pad, v_pad):
            pad[:TAIL] = pad[size:]
        step(i)
        return carry

    lax.fori_loop(1, count // chunks, later, 0)
    sent_ref[:features] = state[...].astype(jnp.bfloat16)


def causal_scores(feats, feats_t):
    row = lax.broadcasted_iota(jnp.int32, (BLOCK, BLOCK), 0)
    col = lax.broadcasted_iota(jnp.int32, (BLOCK, BLOCK), 1)
    return jnp.where(col <= row, dot(feats, feats_t), 0.0).astype(jnp.bfloat16)


def span_kernel(x_ref, w_ref, map_ref, map_t_ref, part_ref, feat_ref, q_pad, k_pad, v_pad, state):
    blocks, size = part_ref.shape[0], q_pad.shape[0] - TAIL
    chunks, group = size // x_ref.shape[2], size // BLOCK
    pads = (q_pad, k_pad, v_pad)

    def step(i, members):
        for member, pad in enumerate(pads):
            fill(pad, x_ref[pl.ds(i * chunks, chunks), member])
        for j in members:
            queries, keys, values = (conv(pad, w_ref[m], j * BLOCK) for m, pad in enumerate(pads))
            feats_t = relu16(dot_nt(map_t_ref[...], keys))
            feats = relu16(dot(queries, map_ref[...]))
            block = i * group + j
            feat_ref[block] = feats
            carried = folded(dot(feats, high_low(state[...])))
            part_ref[block] = dot(causal_scores(feats, feats_t), values) + carried
            state[...] += dot(feats_t, values)

    state[...] = jnp.zeros_like(state)
    for pad in pads:
        pad[:TAIL] = jnp.zeros((TAIL, DH), jnp.float32)
    step(0, range(1, group))

    def later(i, carry):
        for pad in pads:
            pad[:TAIL] = pad[size:]
        step(i, range(group))
        return carry

    lax.fori_loop(1, blocks // group, later, 0)


def finish_kernel(
    x_ref, came_ref, w_ref, map_ref, map_t_ref, part_ref, feat_ref, gain_ref, *refs
):
    *others, out_ref, q_pad, k_pad, v_pad = refs
    blocks, _, features = feat_ref.shape
    per_block = BLOCK // out_ref.shape[2]
    gain = gain_ref[...]
    for place, other in enumerate(others):
        out_ref[:, place] = other[:, 0]

    def put(begin, end, numerator):
        scale = lax.rsqrt(jnp.mean(numerator * numerator, -1, keepdims=True) + 1e-06)
        normed = (numerator * scale * gain).astype(jnp.bfloat16)
        held = slice(begin * per_block, end * per_block)
        extent = (end - begin) * per_block
        out_ref[held, len(others)] = normed.reshape(extent, BLOCK // per_block, DH)

    follows = lax.axis_index("span") > 0
    state = jnp.where(follows, came_ref[:features], jnp.zeros((features, DH), jnp.bfloat16))
    pads = (q_pad, k_pad, v_pad)
    for member, pad in enumerate(pads):
        end = features + (member + 1) * RIM
        pad[:TAIL] = jnp.where(follows, came_ref[end - TAIL : end].astype(jnp.float32), 0.0)
        fill(pad, x_ref[: (pad.shape[0] - TAIL) // x_ref.shape[2], member])
    queries, keys, values = (conv(pad, w_ref[member], 0) for member, pad in enumerate(pads))
    feats_t = relu16(dot_nt(map_t_ref[...], keys))
    feats = relu16(dot(queries, map_ref[...]))
    later = high_low(state.astype(jnp.float32) + dot(feats_t, values))
    put(0, 1, dot(causal_scores(feats, feats_t), values) + dot(feats, state))
    for begin in range(1, blocks, 2):
        end = min(begin + 2, blocks)
        extent = (end - begin) * BLOCK
        feats = feat_ref[begin:end].reshape(extent, features)
        put(begin, end, part_ref[begin:end].reshape(extent, DH) + folded(dot(feats, later)))


LIMIT = 24 * 1024 * 1024
MOST = 60 * 1024 * 1024
VMEM = pl.BlockSpec(memory_space=pltpu.VMEM)
HBM = pl.BlockSpec(memory_space=pltpu.HBM)


COST = pl.CostEstimate(flops=1000, bytes_accessed=1000, transcendentals=0)
GRID = pltpu.CompilerParams(dimension_semantics=("arbitrary",), vmem_limit_bytes=LIMIT)


def whole_call(kernel, inputs, outputs, scratch=(), read=VMEM, written=VMEM, limit=LIMIT):
    return pl.pallas_call(
        kernel,
        in_specs=[read] * len(inputs),
        out_specs=[written] * len(outputs),
        out_shape=outputs,
        scratch_shapes=scratch,
        compiler_params=pltpu.CompilerParams(vmem_limit_bytes=limit),
        cost_estimate=COST,
    )(*inputs)


def stepped(kernel, steps, inputs, specs, out_specs, outputs, scratch):
    return pl.pallas_call(
        kernel,
        grid=(steps,),
        in_specs=specs,
        out_specs=out_specs,
        out_shape=outputs,
        scratch_shapes=scratch,
        compiler_params=GRID,
        cost_estimate=COST,
    )(*inputs)


def whole(array):
    zeros = (0,) * array.ndim
    return pl.BlockSpec(array.shape, lambda i: zeros)


def shaped(shape, dtype=jnp.bfloat16):
    return jax.ShapeDtypeStruct(shape, dtype)


def next_span(block, spans):
    return lax.ppermute(block, "span", [(i, i + 1) for i in range(spans - 1)])


def exchange(block):
    return lax.all_to_all(block, GROUP, split_axis=0, concat_axis=0, tiled=True)


def after(value, other):
    return lax.optimization_barrier((value, other))[0]


def local(spans, query_input, key_input, value_heads_input, conv_weight, feature_map, out_gain):
    rows, model = query_input.shape
    parts, members = lax.axis_size("part"), lax.axis_size("sp")
    count = parts * members
    width = model // count
    heads, tokens, features = width // DH, count * rows, feature_map.shape[1]
    blocks = tokens // BLOCK
    starts = [
        [((d % members) * parts + d // members) * width + head * DH for d in range(count)]
        for head in range(heads)
    ]
    column = lax.axis_index("part") * width
    weights = lax.dynamic_slice_in_dim(conv_weight, column, width, 2)
    gains = lax.dynamic_slice_in_dim(out_gain, column, width, 0)[None]
    map_t = feature_map.T

    inputs = [query_input, key_input, value_heads_input]
    size = BLOCK * (2 if blocks % 2 == 0 else 1)
    narrow = pltpu.VMEM((TAIL + BLOCK, DH), jnp.float32)
    whole_state = pltpu.VMEM((features, DH), jnp.float32)
    chunks = size // rows
    xs, sents, spans_done = [], [], []
    for head in range(heads):
        taps = weights[:, :, head * DH : (head + 1) * DH]
        packed = shaped((count, 3, rows, DH))
        if head == 0:
            (x,) = whole_call(
                functools.partial(pack_kernel, starts[head]),
                inputs,
                [packed],
                [
                    pltpu.VMEM((3, rows, model), jnp.bfloat16),
                    pltpu.VMEM(packed.shape, packed.dtype),
                    pltpu.SemaphoreType.DMA((3, 4)),
                    pltpu.SemaphoreType.DMA((4,)),
                ],
                read=HBM, written=HBM, limit=MOST,
            )
        else:
            (x,) = whole_call(functools.partial(pack_whole_kernel, starts[head]), inputs, [packed])
        x = exchange(x)
        if spans_done:
            x = after(x, spans_done[-1][1])
        halo = jnp.zeros((3, RIM, DH), jnp.bfloat16)
        if spans > 2:
            halo = next_span(x[count - 1, :, rows - RIM :], spans)
        big = chunks * (2 if count % (2 * chunks) == 0 else 1)
        tall = pltpu.VMEM((TAIL + big * rows, DH), jnp.float32)
        if head < heads - 1:
            sent = stepped(
                totals_kernel,
                count // big,
                [x, x, x, halo, taps, map_t],
                [
                    pl.BlockSpec((big, 1, rows, DH), lambda i: (i, 1, 0, 0)),
                    pl.BlockSpec((big, 1, rows, DH), lambda i: (i, 2, 0, 0)),
                    pl.BlockSpec((1, 3, rows, DH), lambda i: (count - 1, 0, 0, 0)),
                    whole(halo), whole(taps), whole(map_t),
                ],
                pl.BlockSpec((features + 3 * RIM, DH), lambda i: (0, 0)),
                shaped((features + 3 * RIM, DH)),
                [tall, tall, whole_state],
            )
        else:
            (sent,) = whole_call(
                whole_totals_kernel,
                [x, halo, taps, map_t],
                [shaped((features + 3 * RIM, DH))],
                [tall, tall, whole_state],
            )
        if spans == 2:
            both = head == heads - 1
            came = lax.ppermute(sent, "span", [(0, 1), (1, 0)] if both else [(0, 1)])
        else:
            gathered = lax.all_gather(sent[:features], "span").astype(jnp.float32)
            mine = lax.axis_index("span")
            earlier = jnp.where((jnp.arange(spans) < mine)[:, None, None], gathered, 0.0)
            state = jnp.sum(earlier, 0).astype(jnp.bfloat16)
            came = jnp.concatenate([state, halo.reshape(3 * RIM, DH)])
        done = whole_call(
            span_kernel,
            [x, taps, feature_map, map_t],
            [
                shaped((blocks, BLOCK, DH), jnp.float32),
                shaped((blocks, BLOCK, features)),
            ],
            [tall, tall, tall, whole_state],
        )
        xs.append((x, came, taps))
        sents.append(sent)
        spans_done.append(done)

    attended = []
    for head in range(heads):
        x, came, taps = xs[head]
        partial, feats = spans_done[head]
        gain = gains[:, head * DH : (head + 1) * DH]
        if head < heads - 1:
            gain = after(gain, sents[-1])
        others = attended if head == heads - 1 else []
        piece = shaped((count, len(others) + 1, rows, DH))
        (out,) = whole_call(
            finish_kernel,
            [x, came, taps, feature_map, map_t, partial, feats, gain, *others],
            [piece],
            [narrow, narrow, narrow],
        )
        attended.append(out)
    landed = exchange(attended[-1]).reshape(parts, members, heads, rows, DH)
    (result,) = whole_call(unpack_kernel, [landed], [shaped((rows, model))])
    return result


def solution(mesh):
    groups, members = mesh.devices.shape
    parts = 1
    while groups % (4 * parts) == 0 and H % (2 * parts * members) == 0:
        parts *= 2
    spans = groups // parts
    split = Mesh(mesh.devices.reshape(spans, parts, members), ("span", "part", "sp"))
    tokens = P(("span", "part", "sp"), None)
    placed = (tokens, tokens, tokens, P(None, None, "sp"), P(), P("sp"))
    return jax.shard_map(
        functools.partial(local, spans),
        mesh=split, in_specs=placed, out_specs=tokens, check_vma=False,
    )
```
